32 devices in a mesh: ctx: 4 (over x, core), dp: 4 (over z), fsdp: 2 (over y).
Axes of the slice: x: 2, y: 2, z: 4, core: 2. Of those that a mesh axis runs over, the one named last changes fastest.
Arguments:
- tokens: bfloat16 [8, 2048, 768], P(('dp', 'fsdp'), 'ctx'), may hold values from -6 to 6
- cotangent: bfloat16 [8, 2048, 768], P(('dp', 'fsdp'), 'ctx'), may hold values from -6 to 6
- block_order: int32 [8], replicated, may hold values from 0 to 7, each once
- first_gain: bfloat16 [768], P('fsdp'), may hold values from 0.099609375 to 1.8984375
- first_shift: bfloat16 [768], P('fsdp'), may hold values from -1.5 to 1.5
- second_gain: bfloat16 [768], P('fsdp'), may hold values from 0.099609375 to 1.8984375
- second_shift: bfloat16 [768], P('fsdp'), may hold values from -1.5 to 1.5
- triple_weight: bfloat16 [768, 2304], P('fsdp'), may hold values from -0.21875 to 0.21875
- triple_bias: bfloat16 [2304], P('fsdp'), may hold values from -1.5 to 1.5
- merge_weight: bfloat16 [768, 768], P('fsdp'), may hold values from -3 to 3
- merge_bias: bfloat16 [768], P('fsdp'), may hold values from -1.5 to 1.5
- expand_weight: bfloat16 [768, 3072], P('fsdp'), may hold values from -0.21875 to 0.21875
- expand_bias: bfloat16 [3072], P('fsdp'), may hold values from -1.5 to 1.5
- reduce_weight: bfloat16 [3072, 768], P('fsdp'), may hold values from -0.109375 to 0.109375
- reduce_bias: bfloat16 [768], P('fsdp'), may hold values from -1.5 to 1.5
Outputs:
- mixed: bfloat16 [8, 2048, 768], P(('dp', 'fsdp'), 'ctx')
- input_grad: float32 [8, 2048, 768], P(('dp', 'fsdp'), 'ctx')
- grad_first_gain: float32 [768], P('fsdp')
- grad_first_shift: float32 [768], P('fsdp')
- grad_second_gain: float32 [768], P('fsdp')
- grad_second_shift: float32 [768], P('fsdp')
- grad_triple_weight: float32 [768, 2304], P('fsdp')
- grad_triple_bias: float32 [2304], P('fsdp')
- grad_merge_weight: float32 [768, 768], P('fsdp')
- grad_merge_bias: float32 [768], P('fsdp')
- grad_expand_weight: float32 [768, 3072], P('fsdp')
- grad_expand_bias: float32 [3072], P('fsdp')
- grad_reduce_weight: float32 [3072, 768], P('fsdp')
- grad_reduce_bias: float32 [768], P('fsdp')
The draws below stay inside these ranges and needn't reach their ends.
Inputs may be any that keep to these rules, and one draw needn't show every extreme that they name: `block_order`: each block number appears once.
All inputs are finite; a program needn't handle non-finite values.
Results may differ from the reference program's by a relative error of at most 0.018.
Values may be sent and summed in bfloat16 or wider, within the bound.
No kernel may reach another device: no remote copies, remote signals or barrier semaphores. Data moves between devices by JAX's collectives and lax.ppermute only.
A program may use at most 128 MiB of HBM per device.

```python
import math
import jax
import jax.numpy as jnp
from jax import lax

D = 768
HEADS = 12
HEAD = 64
ROT = 16
FF = 3072
SEQ_LEN = 2048
BLOCKS = 8
BLOCK = 256
SEQS = 8


def level_of(stream_key, extent, pieces, low, top_value):
    level = 1.0
    for position, blocks in pieces:
        draws = jax.random.uniform(jax.random.fold_in(jax.random.fold_in(stream_key, 6), position), (blocks,), jnp.float32, low / len(pieces), top_value / len(pieces))
        level = level * jnp.repeat(jnp.exp(draws), extent[position] // blocks).reshape((-1,) + (1,) * (len(extent) - 1 - position))
    return level


def gaussian(key, extent, scale, bound, pieces=(), kind=jnp.bfloat16):
    factor_of = level_of(key, extent, pieces, -0.22, 0.18) if pieces else 1.0
    values = jax.random.normal(key, extent, jnp.float32) * scale * factor_of
    return jnp.minimum(jnp.maximum(values, -bound), bound).astype(kind)


def setup_inputs(seed: int = 0) -> dict:
    key_list = jax.random.split(jax.random.key(seed), 16)
    tokens = gaussian(key_list[0], (SEQS, SEQ_LEN, D), 1.0, 6.0, ((0, 8), (1, 4)))
    cotangent = gaussian(key_list[1], (SEQS, SEQ_LEN, D), 1.0, 6.0, ((0, 8), (1, 4)))
    block_order = jax.random.permutation(key_list[2], BLOCKS).astype(jnp.int32)
    first_gain = jnp.clip(1.0 + 0.18 * jax.random.normal(key_list[3], (D,), jnp.float32), 0.099609375, 1.8984375).astype(jnp.bfloat16)
    first_shift = gaussian(key_list[4], (D,), 0.3, 1.5, ((0, 2),))
    second_gain = jnp.clip(1.0 + 0.18 * jax.random.normal(key_list[5], (D,), jnp.float32), 0.099609375, 1.8984375).astype(jnp.bfloat16)
    second_shift = gaussian(key_list[6], (D,), 0.3, 1.5, ((0, 2),))
    triple_weight = gaussian(key_list[7], (D, 3 * D), D ** -0.5, 0.21875, ((0, 2),))
    triple_bias = gaussian(key_list[8], (3 * D,), 0.3, 1.5, ((0, 2),))
    merge_weight = gaussian(key_list[9], (D, D), 4 ** -0.5, 3.0, ((0, 2),))
    merge_bias = gaussian(key_list[10], (D,), 0.3, 1.5, ((0, 2),))
    expand_weight = gaussian(key_list[11], (D, FF), D ** -0.5, 0.21875, ((0, 2),))
    expand_bias = gaussian(key_list[12], (FF,), 0.3, 1.5, ((0, 2),))
    reduce_weight = gaussian(key_list[13], (FF, D), FF ** -0.5, 0.109375, ((0, 2),))
    reduce_bias = gaussian(key_list[14], (D,), 0.3, 1.5, ((0, 2),))
    return {"tokens": tokens, "cotangent": cotangent, "block_order": block_order, "first_gain": first_gain, "first_shift": first_shift, "second_gain": second_gain, "second_shift": second_shift, "triple_weight": triple_weight, "triple_bias": triple_bias, "merge_weight": merge_weight, "merge_bias": merge_bias, "expand_weight": expand_weight, "expand_bias": expand_bias, "reduce_weight": reduce_weight, "reduce_bias": reduce_bias}


HIGH = lax.Precision.HIGHEST
epsilon = 1e-05
masked_value = -1e+30

@jax.custom_vjp
def low(v):
    return lax.optimization_barrier(v.astype(jnp.bfloat16)).astype(jnp.float32)

@jax.custom_vjp
def low_back(v):
    return v

def low_keep(v):
    return (low(v), None)

def low_pass(kept, grad):
    return (grad,)

def back_keep(v):
    return (v, None)

def back_low(kept, grad):
    return (low(grad),)
low.defvjp(low_keep, low_pass)
low_back.defvjp(back_keep, back_low)

def norm_rows(inputs, gain, shift):
    average = lax.optimization_barrier(jnp.mean(inputs, axis=-1, keepdims=True))
    centred = inputs - average
    spread = lax.optimization_barrier(jnp.mean(centred * centred, axis=-1, keepdims=True))
    return centred * lax.rsqrt(spread + epsilon) * gain + shift

def rotate(values, cosine, sine):
    half_rot = ROT // 2
    turned = jnp.concatenate([-values[..., half_rot:ROT], values[..., :half_rot]], axis=-1)
    return jnp.concatenate([values[..., :ROT] * cosine + turned * sine, values[..., ROT:]], axis=-1)

def rotary_tables(positions):
    indices = jnp.arange(ROT // 2, dtype=jnp.float32)
    inverse = 10000.0 ** (-2.0 * indices / ROT)
    angles = positions.astype(jnp.float32)[:, None] * inverse[None, :]
    angles = jnp.concatenate([angles, angles], axis=-1)[:, None, :]
    return (jnp.cos(angles), jnp.sin(angles))

def attention(queries, keys, values, positions):
    query_rows = min(512, SEQ_LEN)
    block_count = SEQ_LEN // query_rows
    scale_factor = 1.0 / math.sqrt(HEAD)

    def one_block(index):
        start = index * query_rows
        block_q = lax.dynamic_slice_in_dim(queries, start, query_rows, 1)
        query_pos = lax.dynamic_slice_in_dim(positions, start, query_rows, 0)
        scores = jnp.einsum('gqhd,gkhd->ghqk', block_q, keys, precision=HIGH) * scale_factor
        scores = low_back(scores)
        allowed = positions[None, :] <= query_pos[:, None]
        scores = jnp.where(allowed, scores, masked_value)
        probs = jax.nn.softmax(scores, axis=-1)
        return jnp.einsum('ghqk,gkhd->gqhd', low(probs), values, precision=HIGH)
    blocks = lax.map(jax.checkpoint(one_block), jnp.arange(block_count, dtype=jnp.int32))
    blocks = jnp.moveaxis(blocks, 0, 1)
    return blocks.reshape(queries.shape)

def layer_forward(params, inputs, positions, cosine, sine):
    gain_one, shift_one, gain_two, shift_two, triple_w, triple_b, merge_w, merge_b, expand_w, expand_b, reduce_w, reduce_b = params
    group = inputs.shape[0]
    first_in = low(norm_rows(inputs, gain_one, shift_one))
    second_in = low(norm_rows(inputs, gain_two, shift_two))
    joined = jnp.einsum('gtd,de->gte', first_in, triple_w, precision=HIGH) + triple_b
    joined = low_back(joined).reshape(group, SEQ_LEN, HEADS, 3, HEAD)
    queries = low(rotate(joined[:, :, :, 0, :], cosine, sine))
    keys = low(rotate(joined[:, :, :, 1, :], cosine, sine))
    values = low(joined[:, :, :, 2, :])
    attended = attention(queries, keys, values, positions)
    attended = low(low_back(attended)).reshape(group, SEQ_LEN, D)
    merged = jnp.einsum('gtd,de->gte', attended, merge_w, precision=HIGH) + merge_b
    hidden = low_back(jnp.einsum('gtd,df->gtf', second_in, expand_w, precision=HIGH) + expand_b)
    active = low(jax.nn.gelu(hidden, approximate=False))
    lowered = jnp.einsum('gtf,fd->gtd', active, reduce_w, precision=HIGH) + reduce_b
    return inputs + merged + lowered

def reference(tokens, cotangent, block_order, first_gain, first_shift, second_gain, second_shift, triple_weight, triple_bias, merge_weight, merge_bias, expand_weight, expand_bias, reduce_weight, reduce_bias):
    params = tuple((p.astype(jnp.float32) for p in (first_gain, first_shift, second_gain, second_shift, triple_weight, triple_bias, merge_weight, merge_bias, expand_weight, expand_bias, reduce_weight, reduce_bias)))
    within = jnp.arange(SEQ_LEN, dtype=jnp.int32)
    positions = (block_order[within // BLOCK] * BLOCK + within % BLOCK).astype(jnp.int32)
    cosine, sine = rotary_tables(positions)
    group = math.gcd(SEQS, max(1, 4096 // SEQ_LEN))
    group_count = SEQS // group
    inputs = tokens.astype(jnp.float32).reshape(group_count, group, SEQ_LEN, D)
    backs = cotangent.astype(jnp.float32).reshape(group_count, group, SEQ_LEN, D)

    def per_group(totals, pair):
        block_in, block_back = pair
        result, pullback = jax.vjp(lambda weights, inside: layer_forward(weights, inside, positions, cosine, sine), params, block_in)
        grads_params, grad_inputs = pullback(block_back)
        return (jax.tree.map(jnp.add, totals, grads_params), (result, grad_inputs))
    zeros = tuple((jnp.zeros_like(p) for p in params))
    totals, (outputs, input_grads) = lax.scan(per_group, zeros, (inputs, backs))
    mixed = outputs.reshape(SEQS, SEQ_LEN, D).astype(jnp.bfloat16)
    input_grad = input_grads.reshape(SEQS, SEQ_LEN, D)
    return (mixed, input_grad, totals[0], totals[1], totals[2], totals[3], totals[4], totals[5], totals[6], totals[7], totals[8], totals[9], totals[10], totals[11])
```

```python
import functools
import math

import jax
import jax.numpy as jnp
from jax import lax
from jax.experimental import pallas as pl
from jax.experimental.pallas import tpu as pltpu
from jax.sharding import PartitionSpec as P

HEADS = 12
HEAD = 64
ROT = 16
TILE = 256
CTX = 4
epsilon = 1e-05
masked_value = -1e30
F32 = jnp.float32
BF16 = jnp.bfloat16
VMEM_LIMIT = 58 * 1024 * 1024

NN = (((1,), (0,)), ((), ()))
NT = (((1,), (1,)), ((), ()))
TN = (((0,), (0,)), ((), ()))


def mm(a, b, dims=NN):
    return lax.dot_general(a, b, dims, preferred_element_type=F32)


def swap(value, axis, bit):
    count = lax.axis_size(axis)
    return lax.ppermute(value, axis, [(i, i ^ bit) for i in range(count)])


def pick(stacked, index):
    return lax.dynamic_index_in_dim(stacked, index, 0, keepdims=False)


def gather_rows(value, f):
    count = lax.axis_size("fsdp")
    if count != 2:
        return lax.all_gather(value, "fsdp", axis=0, tiled=False)
    other = swap(value, "fsdp", 1)
    return jnp.where(f == 0, jnp.stack([value, other]), jnp.stack([other, value]))


def add_low(a, b):
    return (a.astype(F32) + b.astype(F32)).astype(BF16)


def scatter_rows(value, f):
    count = lax.axis_size("fsdp")
    if count != 2:
        return lax.psum_scatter(value, "fsdp", scatter_dimension=0, tiled=False)
    return add_low(pick(value, f), swap(pick(value, 1 - f), "fsdp", 1))


def sum_dp(value, d):
    count = lax.axis_size("dp")
    bits = [1 << i for i in range(count.bit_length() - 1)]
    for bit in bits:
        side = (d // bit) % 2
        halves = value.reshape(2, value.shape[0] // 2, value.shape[1])
        value = add_low(pick(halves, side), swap(pick(halves, 1 - side), "dp", bit))
    for bit in reversed(bits):
        side = (d // bit) % 2
        other = swap(value, "dp", bit)
        value = jnp.where(
            side == 0, jnp.concatenate([value, other]), jnp.concatenate([other, value])
        )
    return value


def slot_of(relative):
    return (relative % 2) * 2 + relative // 2


def gather_ctx(value, c):
    chip = jnp.stack([value, swap(value, "ctx", 2)])
    both = jnp.concatenate([chip, swap(chip, "ctx", 1)])
    return [pick(both, slot_of(c ^ b)) for b in range(CTX)]


def gather_tokens(value):
    far = swap(value, "ctx", 2)
    near = swap(value, "ctx", 1)
    return jnp.concatenate([value, far, near, swap(far, "ctx", 1)])


def scatter_tokens(value):
    chip = add_low(value[:2], swap(value[2:], "ctx", 1))
    return chip[0].astype(F32) + swap(chip[1], "ctx", 2).astype(F32)


def normal(x):
    average = jnp.mean(x, axis=-1, keepdims=True)
    centred = x - average
    spread = jnp.mean(centred * centred, axis=-1, keepdims=True)
    return centred * lax.rsqrt(spread + epsilon)


def colsum(v):
    return jnp.sum(v, axis=0, keepdims=True)


def feed_kernel(
    x_ref, c_ref, vec_ref, we_ref, wr_ref, low_ref, u_ref, ge_ref, gr_ref, sums_ref, ge_acc, gr_acc
):
    step = pl.program_id(0)

    @pl.when(step == 0)
    def _():
        ge_acc[...] = jnp.zeros_like(ge_acc)
        gr_acc[...] = jnp.zeros_like(gr_acc)
        sums_ref[...] = jnp.zeros_like(sums_ref)
        sums_ref[3:4, :] = colsum(c_ref[...].astype(F32))

    gain, shift, bias = vec_ref[2:3, :], vec_ref[3:4, :], vec_ref[4:5, :]
    n = normal(x_ref[...].astype(F32))
    second = (n * gain + shift).astype(BF16)
    back = c_ref[...]
    hidden = mm(second, we_ref[...]) + bias
    cdf = 0.5 * (1.0 + lax.erf(hidden * (1.0 / math.sqrt(2.0))))
    active = (hidden * cdf).astype(BF16)
    low_ref[...] = mm(active, wr_ref[...]).astype(BF16)
    slope = cdf + hidden * (jnp.exp(-0.5 * hidden * hidden) * (1.0 / math.sqrt(2.0 * math.pi)))
    grad_hidden = (mm(back, wr_ref[...], NT) * slope).astype(BF16)
    gr_acc[...] += mm(active, back, TN)
    ge_acc[...] += mm(second, grad_hidden, TN)
    grad_second = mm(grad_hidden, we_ref[...], NT)
    u_ref[...] = (grad_second * gain).astype(BF16)
    sums_ref[0:1, :] += colsum(grad_second * n)
    sums_ref[1:2, :] += colsum(grad_second)
    sums_ref[2:3, :] += colsum(grad_hidden.astype(F32))

    @pl.when(step == pl.num_programs(0) - 1)
    def _():
        ge_ref[...] = ge_acc[...].astype(BF16)
        gr_ref[...] = gr_acc[...].astype(BF16)


def whole(shape):
    return pl.BlockSpec(shape, lambda *_: (0,) * len(shape))


def params(**more):
    return pltpu.CompilerParams(
        dimension_semantics=("arbitrary",), vmem_limit_bytes=VMEM_LIMIT, **more
    )


def feed(x, back, vec, we, wr):
    rows, width = x.shape
    inner = we.shape[1]
    tile = 2 * TILE
    row = pl.BlockSpec((tile, width), lambda i: (i, 0))
    return pl.pallas_call(
        feed_kernel,
        grid=(rows // tile,),
        in_specs=[row, row, whole(vec.shape), whole(we.shape), whole(wr.shape)],
        out_specs=[row, row, whole(we.shape), whole(wr.shape), whole((8, width))],
        out_shape=[
            jax.ShapeDtypeStruct((rows, width), BF16),
            jax.ShapeDtypeStruct((rows, width), BF16),
            jax.ShapeDtypeStruct(we.shape, BF16),
            jax.ShapeDtypeStruct(wr.shape, BF16),
            jax.ShapeDtypeStruct((8, width), F32),
        ],
        scratch_shapes=[pltpu.VMEM(we.shape, F32), pltpu.VMEM(wr.shape, F32)],
        compiler_params=params(),
        cost_estimate=pl.CostEstimate(
            flops=12 * rows * width * inner, bytes_accessed=16 * rows * width, transcendentals=rows * inner
        ),
        name="feed_forward",
    )(x, back, vec, we, wr)


def turn(u, cos, sin_a, sin_b):
    return u * cos + pltpu.roll(u, 120, 1) * sin_a + pltpu.roll(u, 8, 1) * sin_b


def project_kernel(
    pos_ref, x_ref, c_ref, vec_ref, tb_ref, wt_ref, wm_ref, cos_ref, sa_ref, sb_ref, qk_ref, vd_ref
):
    first = (normal(x_ref[...].astype(F32)) * vec_ref[0:1, :] + vec_ref[1:2, :]).astype(BF16)
    grad_out = mm(c_ref[...], wm_ref[...], NT)
    heads = wt_ref.shape[0]
    lane = lax.broadcasted_iota(jnp.int32, (TILE, 2 * HEAD), 1)
    scale = jnp.where(lane < HEAD, 1.0 / math.sqrt(HEAD), 1.0)
    for h in range(heads):
        joined = mm(first, wt_ref[h]) + tb_ref[h]
        turned = turn(joined[:, : 2 * HEAD], cos_ref[...], sa_ref[...], sb_ref[...])
        qk_ref[h] = (turned * scale).astype(BF16)
        vd_ref[h, :, :HEAD] = joined[:, 2 * HEAD :].astype(BF16)
        vd_ref[h, :, HEAD:] = grad_out[:, HEAD * h : HEAD * (h + 1)].astype(BF16)


def project(pos, x, back, vec, tb, wt, wm, tables):
    rows, width = x.shape
    heads = wt.shape[0]
    row = pl.BlockSpec((TILE, width), lambda i, p: (i, 0))
    table = pl.BlockSpec((TILE, 2 * HEAD), lambda i, p: (p[i], 0))
    out = pl.BlockSpec((heads, TILE, 2 * HEAD), lambda i, p: (0, p[i], 0))
    return pl.pallas_call(
        project_kernel,
        grid_spec=pltpu.PrefetchScalarGridSpec(
            num_scalar_prefetch=1,
            grid=(rows // TILE,),
            in_specs=[row, row, whole(vec.shape), whole(tb.shape), whole(wt.shape), whole(wm.shape)]
            + [table] * 3,
            out_specs=[out, out],
        ),
        out_shape=[jax.ShapeDtypeStruct((heads, rows, 2 * HEAD), BF16)] * 2,
        compiler_params=params(),
        cost_estimate=pl.CostEstimate(
            flops=2 * rows * width * heads * 4 * HEAD,
            bytes_accessed=6 * rows * width,
            transcendentals=0,
        ),
        name="project",
    )(pos, x, back, vec, tb, wt, wm, *tables)


def attend_kernel(
    qk_ref, vd_ref, cos_ref, sa_ref, sb_ref, att_ref, gj_ref, qt, vt, ks, vs, ds_, s_ref, gq, gk, gv
):
    rows = qk_ref.shape[1]
    blocks = rows // TILE
    for b in range(blocks):
        r = slice(TILE * b, TILE * (b + 1))
        qt[:, r] = qk_ref[0, r, :].T
        vt[:, r] = vd_ref[0, r, :].T
        ks[r, :] = qk_ref[0, r, HEAD:]
        vs[r, :] = vd_ref[0, r, :HEAD]
        ds_[r, :] = vd_ref[0, r, HEAD:]
    key_id = lax.broadcasted_iota(jnp.int32, (TILE, TILE), 0)
    query_id = lax.broadcasted_iota(jnp.int32, (TILE, TILE), 1)
    keep = key_id <= query_id
    for i in range(blocks):
        qr = slice(TILE * i, TILE * (i + 1))
        q_t = qt[:HEAD, qr]
        peak = None
        for j in range(i + 1):
            kr = slice(TILE * j, TILE * (j + 1))
            s = mm(ks[kr, :], q_t)
            if j == i:
                s = jnp.where(keep, s, masked_value)
            s_ref[kr, :] = s
            top = jnp.max(s, axis=0, keepdims=True)
            peak = top if peak is None else jnp.maximum(peak, top)
        total = jnp.zeros((1, TILE), F32)
        out = jnp.zeros((HEAD, TILE), F32)
        for j in range(i + 1):
            kr = slice(TILE * j, TILE * (j + 1))
            e = jnp.exp(s_ref[kr, :] - peak)
            s_ref[kr, :] = e
            total = total + jnp.sum(e, axis=0, keepdims=True)
            out = out + mm(vt[:HEAD, kr], e.astype(BF16))
        inv = 1.0 / total
        out = out * inv
        att_ref[0, :, qr] = out.astype(BF16)
        d_t = vt[HEAD:, qr]
        delta = jnp.sum(d_t.astype(F32) * out, axis=0, keepdims=True)
        q = qk_ref[0, qr, :HEAD]
        d = ds_[qr, :]
        grad_q = jnp.zeros((HEAD, TILE), F32)
        for j in range(i + 1):
            kr = slice(TILE * j, TILE * (j + 1))
            p = s_ref[kr, :] * inv
            grad_v = mm(p.astype(BF16), d)
            g = (p * (mm(vs[kr, :], d_t) - delta)).astype(BF16)
            grad_k = mm(g, q)
            grad_q = grad_q + mm(qt[HEAD:, kr], g)
            if j == i:
                gv[kr, :] = grad_v
                gk[kr, :] = grad_k
            else:
                gv[kr, :] += grad_v
                gk[kr, :] += grad_k
        gq[:, qr] = grad_q * (1.0 / math.sqrt(HEAD))
    for b in range(blocks):
        r = slice(TILE * b, TILE * (b + 1))
        both = jnp.concatenate([gq[:, r].T, gk[r, :]], axis=1)
        gj_ref[0, r, : 2 * HEAD] = turn(both, cos_ref[r, :], -sa_ref[r, :], -sb_ref[r, :]).astype(BF16)
        gj_ref[0, r, 2 * HEAD :] = gv[r, :].astype(BF16)


def attend(qk, vd, tables):
    heads, rows, _ = qk.shape
    packed = pl.BlockSpec((1, rows, 2 * HEAD), lambda h: (h, 0, 0))
    return pl.pallas_call(
        attend_kernel,
        grid=(heads,),
        in_specs=[packed, packed] + [whole((rows, 2 * HEAD))] * 3,
        out_specs=[
            pl.BlockSpec((1, HEAD, rows), lambda h: (h, 0, 0)),
            pl.BlockSpec((1, rows, 3 * HEAD), lambda h: (h, 0, 0)),
        ],
        out_shape=[
            jax.ShapeDtypeStruct((heads, HEAD, rows), BF16),
            jax.ShapeDtypeStruct((heads, rows, 3 * HEAD), BF16),
        ],
        scratch_shapes=[
            pltpu.VMEM((2 * HEAD, rows), BF16),
            pltpu.VMEM((2 * HEAD, rows), BF16),
            pltpu.VMEM((rows, HEAD), BF16),
            pltpu.VMEM((rows, HEAD), BF16),
            pltpu.VMEM((rows, HEAD), BF16),
            pltpu.VMEM((rows, TILE), F32),
            pltpu.VMEM((HEAD, rows), F32),
            pltpu.VMEM((rows, HEAD), F32),
            pltpu.VMEM((rows, HEAD), F32),
        ],
        compiler_params=params(),
        cost_estimate=pl.CostEstimate(
            flops=7 * heads * rows * rows * HEAD,
            bytes_accessed=heads * rows * 16 * HEAD,
            transcendentals=heads * rows * rows // 2,
        ),
        name="attend",
    )(qk, vd, *tables)


def collect_kernel(
    pos_ref, x_ref, c_ref, att_ref, gj_ref, low_ref, u2_ref, vec_ref, wt_ref, wm_ref,
    pair_ref, gt_ref, gm_ref, sums_ref, tb_ref, gt_acc, gm_acc,
):
    step = pl.program_id(0)
    heads = wt_ref.shape[0]

    @pl.when(step == 0)
    def _():
        gt_acc[...] = jnp.zeros_like(gt_acc)
        gm_acc[...] = jnp.zeros_like(gm_acc)
        sums_ref[...] = jnp.zeros_like(sums_ref)
        tb_ref[...] = jnp.zeros_like(tb_ref)

    gain = vec_ref[0:1, :]
    n = normal(x_ref[...].astype(F32))
    first = (n * gain + vec_ref[1:2, :]).astype(BF16)
    att = att_ref[...].reshape(heads * HEAD, TILE)
    pair_ref[0, 0] = (low_ref[...].astype(F32) + mm(att, wm_ref[...], TN)).astype(BF16)
    gm_acc[...] += mm(att, c_ref[...])
    grad_first = jnp.zeros(n.shape, F32)
    for h in range(heads):
        gj = gj_ref[h]
        tb_ref[h] += colsum(gj.astype(F32))
        gt_acc[h] += mm(first, gj, TN)
        grad_first = grad_first + mm(gj, wt_ref[h], NT)
    pair_ref[0, 1] = (u2_ref[...].astype(F32) + grad_first * gain).astype(BF16)
    sums_ref[0:1, :] += colsum(grad_first * n)
    sums_ref[1:2, :] += colsum(grad_first)

    @pl.when(step == pl.num_programs(0) - 1)
    def _():
        gt_ref[...] = gt_acc[...].astype(BF16)
        gm_ref[...] = gm_acc[...].astype(BF16)


def collect(pos, x, back, att, gj, low, u2, vec, wt, wm):
    rows, width = x.shape
    heads = wt.shape[0]
    row = pl.BlockSpec((TILE, width), lambda i, p: (i, 0))
    per_slot = rows // CTX // TILE
    return pl.pallas_call(
        collect_kernel,
        grid_spec=pltpu.PrefetchScalarGridSpec(
            num_scalar_prefetch=1,
            grid=(rows // TILE,),
            in_specs=[
                row,
                row,
                pl.BlockSpec((heads, HEAD, TILE), lambda i, p: (0, 0, p[i])),
                pl.BlockSpec((heads, TILE, 3 * HEAD), lambda i, p: (0, p[i], 0)),
                row,
                row,
                whole(vec.shape),
                whole(wt.shape),
                whole(wm.shape),
            ],
            out_specs=[
                pl.BlockSpec(
                    (1, 2, TILE, width), lambda i, p: (i // per_slot, 0, i % per_slot, 0)
                ),
                whole(wt.shape),
                whole(wm.shape),
                whole((8, width)),
                whole((heads, 1, 3 * HEAD)),
            ],
            scratch_shapes=[pltpu.VMEM(wt.shape, F32), pltpu.VMEM(wm.shape, F32)],
        ),
        out_shape=[
            jax.ShapeDtypeStruct((CTX, 2, rows // CTX, width), BF16),
            jax.ShapeDtypeStruct(wt.shape, BF16),
            jax.ShapeDtypeStruct(wm.shape, BF16),
            jax.ShapeDtypeStruct((8, width), F32),
            jax.ShapeDtypeStruct((heads, 1, 3 * HEAD), F32),
        ],
        compiler_params=params(),
        cost_estimate=pl.CostEstimate(
            flops=16 * rows * width * heads * HEAD, bytes_accessed=14 * rows * width, transcendentals=0
        ),
        name="collect",
    )(pos, x, back, att, gj, low, u2, vec, wt, wm)


def rotary(rows):
    lane = jnp.arange(2 * HEAD, dtype=jnp.int32)[None, :] % HEAD
    half = ROT // 2
    inverse = 10000.0 ** (-2.0 * (lane % half).astype(F32) / ROT)
    angles = jnp.arange(rows, dtype=jnp.int32).astype(F32)[:, None] * inverse
    cos = jnp.where(lane < ROT, jnp.cos(angles), 1.0)
    sine = jnp.sin(angles)
    low = jnp.where(lane < half, -sine, 0.0)
    high = jnp.where((lane >= half) & (lane < ROT), sine, 0.0)
    return cos, low, high


def local(
    tokens, cotangent, block_order, first_gain, first_shift, second_gain, second_shift,
    triple_weight, triple_bias, merge_weight, merge_bias, expand_weight, expand_bias,
    reduce_weight, reduce_bias,
):
    c, d, f = lax.axis_index("ctx"), lax.axis_index("dp"), lax.axis_index("fsdp")
    shards = lax.axis_size("fsdp")
    own_len, width = tokens.shape[1:]
    inner = expand_weight.shape[1]
    own_inner = inner // shards // CTX
    own_heads = HEADS // CTX
    own_cols = own_heads * 3 * HEAD
    own_merge = own_heads * HEAD

    own_x = tokens.reshape(own_len, width)
    own_back = cotangent.reshape(own_len, width)

    own_expand = jnp.concatenate(
        [
            lax.dynamic_slice_in_dim(expand_weight, g * CTX * own_inner + c * own_inner, own_inner, 1)
            for g in range(shards)
        ],
        axis=1,
    )
    we = gather_rows(own_expand, f).reshape(width, shards * own_inner)
    own_reduce = lax.dynamic_slice_in_dim(reduce_weight, c * own_inner, own_inner, 0)
    wr = gather_rows(own_reduce, f).reshape(shards * own_inner, width)

    smalls = (
        first_gain, first_shift, second_gain, second_shift,
        merge_bias, reduce_bias, expand_bias, triple_bias,
    )
    packed = gather_rows(jnp.concatenate(smalls), f)
    full, at = [], 0
    for v in smalls:
        full.append(packed[:, at : at + v.shape[0]].reshape(-1).astype(F32))
        at += v.shape[0]
    g1, s1, g2, s2, merge_b, reduce_b, expand_b, triple_b = full
    be = pick(expand_b.reshape(shards, CTX, own_inner).transpose(1, 0, 2), c).reshape(-1)
    vec = jnp.stack([g1, s1, g2, s2, be, jnp.zeros_like(be), jnp.zeros_like(be), jnp.zeros_like(be)])
    tb = pick(triple_b.reshape(CTX, own_heads, 1, 3 * HEAD), c)

    own_triple = lax.dynamic_slice_in_dim(triple_weight, c * own_cols, own_cols, 1)
    own_triple = jnp.stack(jnp.split(own_triple, own_heads, axis=1))
    wt = gather_rows(own_triple, f)
    wt = wt.transpose(1, 0, 2, 3).reshape(own_heads, width, 3 * HEAD)
    if shards == 2:
        half = CTX // shards
        mine = lax.dynamic_slice_in_dim(merge_weight, (c % half) * own_merge, own_merge, 0)
        pairs = [
            (i * shards + i // half, i * shards + 1 - i // half) for i in range(CTX)
        ]
        theirs = lax.ppermute(mine, ("ctx", "fsdp"), pairs)
        wm = jnp.where(f == c // half, mine, theirs)
    else:
        wm = gather_rows(merge_weight, f).reshape(width, width)
        wm = lax.dynamic_slice_in_dim(wm, c * own_merge, own_merge, 0)

    x = gather_tokens(own_x)
    back = gather_tokens(own_back)
    pos = jnp.concatenate(
        [lax.dynamic_slice_in_dim(block_order, 2 * (c ^ r), 2) for r in (0, 2, 1, 3)]
    )
    tables = rotary(x.shape[0])

    low, u2, ge, gr, sums2 = feed(x, back, vec, we, wr)
    qk, vd = project(pos, x, back, vec, tb, wt, wm, tables)
    att, gj = attend(qk, vd, tables)
    pair, gt, gm, sums1, gtb = collect(pos, x, back, att, gj, low, u2, vec, wt, wm)

    both = scatter_tokens(pair)
    x_f = own_x.astype(F32)
    mixed = (x_f + both[0] + (merge_b + reduce_b)[None, :]).astype(BF16)
    average = jnp.mean(x_f, axis=-1, keepdims=True)
    centred = x_f - average
    r = lax.rsqrt(jnp.mean(centred * centred, axis=-1, keepdims=True) + epsilon)
    n = centred * r
    u = both[1]
    input_grad = own_back.astype(F32) + r * (
        u - jnp.mean(u, axis=-1, keepdims=True) - n * jnp.mean(u * n, axis=-1, keepdims=True)
    )

    rows = width // shards
    ge = sum_dp(scatter_rows(ge.reshape(shards, rows, -1), f), d)
    gr = sum_dp(scatter_rows(gr.reshape(shards, own_inner, width), f), d)
    gt = gt.reshape(own_heads, shards, rows, 3 * HEAD).transpose(1, 0, 2, 3)
    gt = sum_dp(scatter_rows(gt.reshape(shards, own_heads * rows, 3 * HEAD), f), d)
    ge = gather_ctx(ge, c)
    grad_expand = jnp.concatenate(
        [ge[b][:, g * own_inner : (g + 1) * own_inner] for g in range(shards) for b in range(CTX)],
        axis=1,
    ).astype(F32)
    grad_reduce = jnp.concatenate(gather_ctx(gr, c)).astype(F32)
    gt = gather_ctx(gt, c)
    grad_triple = jnp.concatenate(
        [gt[b].reshape(own_heads, rows, 3 * HEAD)[h] for b in range(CTX) for h in range(own_heads)],
        axis=1,
    ).astype(F32)
    if shards == 2:
        half = CTX // shards
        back_pairs = [(b, a) for a, b in pairs]
        gm = sum_dp(add_low(gm, lax.ppermute(gm, ("ctx", "fsdp"), back_pairs)), d)
        far = swap(gm, "ctx", 2)
        own = jnp.where(f == c // half, gm, far)
        near = swap(own, "ctx", 1)
        grad_merge = jnp.where(
            c % 2 == 0, jnp.concatenate([own, near]), jnp.concatenate([near, own])
        ).astype(F32)
    else:
        spread = jnp.zeros((width, width), BF16)
        spread = lax.dynamic_update_slice_in_dim(spread, gm, c * own_merge, 0)
        spread = lax.psum_scatter(spread, "fsdp", scatter_dimension=0, tiled=True)
        grad_merge = lax.psum(spread, ("ctx", "dp")).astype(F32)

    wide_tb = jnp.zeros((CTX, own_cols), F32)
    wide_tb = lax.dynamic_update_slice_in_dim(wide_tb, gtb.reshape(1, own_cols), c, 0)
    wide_eb = jnp.zeros((shards, CTX, own_inner), F32)
    wide_eb = lax.dynamic_update_slice_in_dim(
        wide_eb, sums2[2].reshape(shards, 1, own_inner), c, 1
    )
    vector = jnp.concatenate(
        [sums1[0], sums1[1], sums2[0], sums2[1], sums2[3], wide_tb.reshape(-1), wide_eb.reshape(-1)]
    )
    vector = lax.psum(vector, ("ctx", "dp", "fsdp"))
    pieces, at = [], 0
    for size in (width, width, width, width, width, 3 * width, inner):
        part = size // shards
        pieces.append(lax.dynamic_slice_in_dim(vector, at + f * part, part, 0))
        at += size
    d_g1, d_s1, d_g2, d_s2, d_cot, d_tb, d_eb = pieces
    return (
        mixed[None],
        input_grad[None],
        d_g1,
        d_s1,
        d_g2,
        d_s2,
        grad_triple,
        d_tb,
        grad_merge,
        d_cot,
        grad_expand,
        d_eb,
        grad_reduce,
        d_cot,
    )


def solution(mesh):
    tokens = P(("dp", "fsdp"), "ctx", None)
    row, vector = P("fsdp", None), P("fsdp")
    weights = (row, vector, row, vector, row, vector, row, vector)
    in_specs = (tokens, tokens, P()) + (vector,) * 4 + weights
    out_specs = (tokens, tokens) + (vector,) * 4 + weights
    return jax.shard_map(local, mesh=mesh, in_specs=in_specs, out_specs=out_specs, check_vma=False)
```

```python
import functools
import math

import jax
import jax.numpy as jnp
from jax import lax
from jax.experimental import pallas as pl
from jax.experimental.pallas import tpu as pltpu
from jax.sharding import PartitionSpec as P

HEADS = 12
HEAD = 64
ROT = 16
TILE = 256
CTX = 4
epsilon = 1e-05
masked_value = -1e30
F32 = jnp.float32
BF16 = jnp.bfloat16
VMEM_LIMIT = 58 * 1024 * 1024

NN = (((1,), (0,)), ((), ()))
NT = (((1,), (1,)), ((), ()))
TN = (((0,), (0,)), ((), ()))


def mm(a, b, dims=NN):
    return lax.dot_general(a, b, dims, preferred_element_type=F32)


def swap(value, axis, bit):
    count = lax.axis_size(axis)
    return lax.ppermute(value, axis, [(i, i ^ bit) for i in range(count)])


def pick(stacked, index):
    return lax.dynamic_index_in_dim(stacked, index, 0, keepdims=False)


def add_low(a, b):
    return (a.astype(F32) + b.astype(F32)).astype(BF16)


def after(value, *others):
    return lax.optimization_barrier((value,) + others)[0]


def slot_of(relative):
    return (relative % 2) * 2 + relative // 2


def in_order(both, c):
    both = jnp.stack(both)
    return [pick(both, slot_of(c ^ b)) for b in range(CTX)]


class Summed:
    def __init__(self, value, f, d):
        self.value, self.f, self.d = value, f, d
        self.steps = ["fsdp", "dp_down", "dp_up", "far", "near"]
        self.moving = None

    def send(self):
        kind, value = self.steps[0], self.value
        count = lax.axis_size("dp")
        if kind == "fsdp":
            self.moving = [value[1]] if isinstance(value, tuple) else []
        elif kind == "dp_down":
            self.value = value.reshape(count, value.shape[0] // count, value.shape[1])
            self.moving = [pick(self.value, (self.d + k) % count) for k in range(1, count)]
        elif kind == "near":
            self.moving = [value[1]]
        else:
            self.moving = [value]
        return self.moving

    def take(self):
        kind = self.steps.pop(0)
        count = lax.axis_size("dp")
        turns = [[(i, (i + k) % count) for i in range(count)] for k in range(1, count)]
        if kind == "fsdp":
            if self.moving:
                self.value = add_low(self.value[0], swap(self.moving[0], "fsdp", 1))
            else:
                self.value = lax.psum_scatter(self.value, "fsdp", scatter_dimension=0, tiled=False)
        elif kind == "dp_down":
            total = pick(self.value, self.d).astype(F32)
            for moving, turn_ in zip(self.moving, turns):
                total = total + lax.ppermute(moving, "dp", turn_).astype(F32)
            self.value = total.astype(BF16)
        elif kind == "dp_up":
            here = self.moving[0]
            self.value = jnp.stack([here] + [lax.ppermute(here, "dp", turn_) for turn_ in turns])
        elif kind == "far":
            here = self.moving[0]
            self.value = [here, swap(here, "ctx", 2), swap(here, "ctx", 1)]
        else:
            self.value = self.value + [swap(self.moving[0], "ctx", 1)]

    def finish(self):
        while self.steps:
            if self.moving is None:
                self.send()
            self.take()
            self.moving = None
        return self.value


def boundary(ways, *values):
    for way in ways:
        if way.moving is not None:
            way.take()
        way.moving = way.send() if way.steps else None
    sent = [tuple(way.moving or ()) for way in ways]
    sent, values = lax.optimization_barrier((sent, values))
    for way, moving in zip(ways, sent):
        if way.moving is not None:
            way.moving = list(moving)
    return values


def normal(x):
    average = jnp.mean(x, axis=-1, keepdims=True)
    centred = x - average
    spread = jnp.mean(centred * centred, axis=-1, keepdims=True)
    return centred * lax.rsqrt(spread + epsilon)


def colsum(v):
    return jnp.sum(v, axis=0, keepdims=True)


def whole(shape):
    return pl.BlockSpec(shape, lambda *_: (0,) * len(shape))


def params(**more):
    return pltpu.CompilerParams(
        dimension_semantics=("arbitrary",), vmem_limit_bytes=VMEM_LIMIT, **more
    )


def cost(flops, moved, exps=0):
    return pl.CostEstimate(flops=flops, bytes_accessed=moved, transcendentals=exps)


def beside(moved):
    return cost(0, 100 * moved)


def short():
    return cost(0, 0)


def place(f, own, other, out):
    rows = own.shape[0]
    out[pl.ds(pl.multiple_of(f * rows, rows), rows), :] = own
    out[pl.ds(pl.multiple_of((1 - f) * rows, rows), rows), :] = other


def feed_kernel(
    f_ref, a_ref, b_ref, c_ref, d_ref, vec_ref, own_ref, other_ref,
    keep_ref, send_ref, g_keep_ref, g_send_ref, sums_ref, we_ref, wr_ref, ge_acc, gr_acc,
):
    step = pl.program_id(0)
    half = we_ref.shape[0] // 2

    @pl.when(step == 0)
    def _():
        f = f_ref[0]
        place(f, own_ref[:half], other_ref[:half], we_ref)
        place(f, own_ref[half : 2 * half], other_ref[half : 2 * half], wr_ref)
        ge_acc[...] = jnp.zeros_like(ge_acc)
        gr_acc[...] = jnp.zeros_like(gr_acc)
        sums_ref[...] = jnp.zeros_like(sums_ref)
        sums_ref[3:4, :] = colsum(a_ref[1].astype(F32))

    def piece(k):
        first = jnp.where(step == 0, a_ref[k], b_ref[k])
        return jnp.where(step < 2, first, jnp.where(step == 2, c_ref[k], d_ref[k]))

    gain, shift, bias = vec_ref[2:3, :], vec_ref[3:4, :], vec_ref[4:5, :]
    n = normal(piece(0).astype(F32))
    second = (n * gain + shift).astype(BF16)
    back = piece(1)
    hidden = mm(second, we_ref[...]) + bias
    cdf = 0.5 * (1.0 + lax.erf(hidden * (1.0 / math.sqrt(2.0))))
    active = (hidden * cdf).astype(BF16)
    low = mm(active, wr_ref[...]).astype(BF16)
    slope = cdf + hidden * (jnp.exp(-0.5 * hidden * hidden) * (1.0 / math.sqrt(2.0 * math.pi)))
    grad_hidden = (mm(back, wr_ref[...], NT) * slope).astype(BF16)
    gr_acc[...] += mm(active, back, TN)
    ge_acc[...] += mm(second, grad_hidden, TN)
    grad_second = mm(grad_hidden, we_ref[...], NT)
    u = (grad_second * gain).astype(BF16)
    sums_ref[0:1, :] += colsum(grad_second * n)
    sums_ref[1:2, :] += colsum(grad_second)
    sums_ref[2:3, :] += colsum(grad_hidden.astype(F32))

    @pl.when(step < 2)
    def _():
        keep_ref[0, 0], keep_ref[0, 1] = low, u

    @pl.when(step >= 2)
    def _():
        send_ref[0, 0], send_ref[0, 1] = low, u

    @pl.when(step == pl.num_programs(0) - 1)
    def _():
        for s, g_ref in ((f_ref[0], g_keep_ref), (1 - f_ref[0], g_send_ref)):
            rows = pl.ds(pl.multiple_of(s * half, half), half)
            g_ref[:half] = ge_acc[rows, :].astype(BF16)
            g_ref[half:] = gr_acc[rows, :].astype(BF16)


def feed(f, own_x, far, near, both, vec, own, other, width, inner):
    rows = own_x.shape[1]
    shape_e, shape_r = (width, inner), (inner, width)
    outs = [
        jax.ShapeDtypeStruct((2, 2, rows, width), BF16),
        jax.ShapeDtypeStruct((2, 2, rows, width), BF16),
        jax.ShapeDtypeStruct(((width + inner) // 2, width), BF16),
        jax.ShapeDtypeStruct(((width + inner) // 2, width), BF16),
        jax.ShapeDtypeStruct((8, width), F32),
    ]
    args = (own_x, far, near, both, vec, own, other)
    block = (1, 2, rows, width)
    return pl.pallas_call(
        feed_kernel,
        grid_spec=pltpu.PrefetchScalarGridSpec(
            num_scalar_prefetch=1,
            grid=(CTX,),
            in_specs=[whole(v.shape) for v in args],
            out_specs=[
                pl.BlockSpec(block, lambda i, *_: (jnp.minimum(i, 1), 0, 0, 0)),
                pl.BlockSpec(block, lambda i, *_: (jnp.maximum(i - 2, 0), 0, 0, 0)),
            ]
            + [whole(v.shape) for v in outs[2:]],
            scratch_shapes=[
                pltpu.VMEM(shape_e, BF16), pltpu.VMEM(shape_r, BF16),
                pltpu.VMEM(shape_e, F32), pltpu.VMEM(shape_r, F32),
            ],
        ),
        out_shape=outs,
        compiler_params=params(),
        cost_estimate=beside(16 * rows * width),
        name="feed",
    )(f, *args)


def turn(u, cos, sin_a, sin_b):
    return u * cos + pltpu.roll(u, 120, 1) * sin_a + pltpu.roll(u, 8, 1) * sin_b


def place_heads(f, own, other, out):
    rows = own.shape[0]
    wide = out.shape[2]
    for h in range(out.shape[0]):
        part = slice(wide * h, wide * (h + 1))
        out[h, pl.ds(pl.multiple_of(f * rows, rows), rows), :] = own[:, part]
        out[h, pl.ds(pl.multiple_of((1 - f) * rows, rows), rows), :] = other[:, part]


def choose(step, refs, index):
    value = refs[-1][index]
    for k in range(len(refs) - 2, -1, -1):
        value = jnp.where(step < 2 * k + 2, refs[k][index], value)
    return value


def piece_specs(count, lead, width, first=0):
    return [
        pl.BlockSpec(
            (lead, TILE, width), lambda i, *_, k=k: (first, jnp.clip(i - 2 * k, 0, 1), 0)
        )
        for k in range(count)
    ]


def project_kernel(pos_ref, f_ref, a_ref, b_ref, vec_ref, tb_ref, own_ref, other_ref, wm_ref,
    cos_ref, sa_ref, sb_ref, *refs):
    qk_ref, vd_ref, first_ref, back_ref, wt_ref = refs[-5:]
    step = pl.program_id(0)

    @pl.when(step == 0)
    def _():
        place_heads(f_ref[0], own_ref[...], other_ref[...], wt_ref)

    pieces = (a_ref, b_ref)
    x = choose(step, pieces, 0)
    back = choose(step, pieces, 1)
    first = (normal(x.astype(F32)) * vec_ref[0:1, :] + vec_ref[1:2, :]).astype(BF16)
    first_ref[...] = first
    back_ref[...] = back
    grad_out = mm(back, wm_ref[...], NT)
    heads = wt_ref.shape[0]
    lane = lax.broadcasted_iota(jnp.int32, (TILE, 2 * HEAD), 1)
    scale = jnp.where(lane < HEAD, 1.0 / math.sqrt(HEAD), 1.0)
    for h in range(heads):
        joined = mm(first, wt_ref[h]) + tb_ref[h]
        turned = turn(joined[:, : 2 * HEAD], cos_ref[...], sa_ref[...], sb_ref[...])
        qk_ref[h] = (turned * scale).astype(BF16)
        vd_ref[h, :, :HEAD] = joined[:, 2 * HEAD :].astype(BF16)
        vd_ref[h, :, HEAD:] = grad_out[:, HEAD * h : HEAD * (h + 1)].astype(BF16)


def project(pos, f, pieces, vec, tb, own, other, wm, tables, so_far=()):
    width = pieces[0].shape[2]
    rows = CTX * pieces[0].shape[1]
    heads = tb.shape[0]
    table = pl.BlockSpec((TILE, 2 * HEAD), lambda i, p, f: (p[i], 0))
    out = pl.BlockSpec((heads, TILE, 2 * HEAD), lambda i, p, f: (0, p[i], 0))
    row = pl.BlockSpec((TILE, width), lambda i, p, f: (p[i], 0))
    args = (pos, f, *pieces, vec, tb, own, other, wm, *tables)
    return pl.pallas_call(
        project_kernel,
        grid_spec=pltpu.PrefetchScalarGridSpec(
            num_scalar_prefetch=2,
            grid=(rows // TILE // 2,),
            in_specs=piece_specs(2, 2, width)
            + [whole(v.shape) for v in (vec, tb, own, other, wm)]
            + [table] * 3
            + [pl.BlockSpec(memory_space=pl.ANY)] * len(so_far),
            out_specs=[out, out, row, row],
            scratch_shapes=[pltpu.VMEM((heads, width, 3 * HEAD), BF16)],
        ),
        out_shape=[jax.ShapeDtypeStruct((heads, rows, 2 * HEAD), BF16)] * 2
        + [jax.ShapeDtypeStruct((rows, width), BF16)] * 2,
        input_output_aliases={len(args) + k: k for k in range(len(so_far))},
        compiler_params=params(),
        cost_estimate=beside(10 * rows * width),
        name="project",
    )(*args, *so_far)


def attend_kernel(
    slot_ref, f_ref, qk_ref, vd_ref, cos_ref, sa_ref, sb_ref, first_ref, back_ref, keep_ref, send_ref, g_keep_ref, g_send_ref,
    qt, vt, ks, vs, ds_, s_ref, gq, gk, gv, att_ref, gj_ref, grad_t,
):
    rows = qk_ref.shape[1]
    blocks = rows // TILE

    for b in range(blocks):
        r = slice(TILE * b, TILE * (b + 1))
        qt[:, r] = qk_ref[0, r, :].T
        vt[:, r] = vd_ref[0, r, :].T
        ks[r, :] = qk_ref[0, r, HEAD:]
        vs[r, :] = vd_ref[0, r, :HEAD]
        ds_[r, :] = vd_ref[0, r, HEAD:]
    key_id = lax.broadcasted_iota(jnp.int32, (TILE, TILE), 0)
    query_id = lax.broadcasted_iota(jnp.int32, (TILE, TILE), 1)
    keep = key_id <= query_id
    for i in range(blocks):
        qr = slice(TILE * i, TILE * (i + 1))
        q_t = qt[:HEAD, qr]
        peak = None
        for j in range(i + 1):
            kr = slice(TILE * j, TILE * (j + 1))
            s = mm(ks[kr, :], q_t)
            if j == i:
                s = jnp.where(keep, s, masked_value)
            s_ref[kr, :] = s
            top = jnp.max(s, axis=0, keepdims=True)
            peak = top if peak is None else jnp.maximum(peak, top)
        total = jnp.zeros((1, TILE), F32)
        out = jnp.zeros((HEAD, TILE), F32)
        for j in range(i + 1):
            kr = slice(TILE * j, TILE * (j + 1))
            e = jnp.exp(s_ref[kr, :] - peak)
            s_ref[kr, :] = e
            total = total + jnp.sum(e, axis=0, keepdims=True)
            out = out + mm(vt[:HEAD, kr], e.astype(BF16))
        inv = 1.0 / total
        out = out * inv
        att_ref[:, qr] = out.astype(BF16)
        gj_ref[qr, 3 * HEAD :] = out.T.astype(BF16)
        d_t = vt[HEAD:, qr]
        delta = jnp.sum(d_t.astype(F32) * out, axis=0, keepdims=True)
        q = qk_ref[0, qr, :HEAD]
        d = ds_[qr, :]
        grad_q = jnp.zeros((HEAD, TILE), F32)
        for j in range(i + 1):
            kr = slice(TILE * j, TILE * (j + 1))
            p = s_ref[kr, :] * inv
            grad_v = mm(p.astype(BF16), d)
            g = (p * (mm(vs[kr, :], d_t) - delta)).astype(BF16)
            grad_k = mm(g, q)
            grad_q = grad_q + mm(qt[HEAD:, kr], g)
            if j == i:
                gv[kr, :] = grad_v
                gk[kr, :] = grad_k
            else:
                gv[kr, :] += grad_v
                gk[kr, :] += grad_k
        gq[:, qr] = grad_q * (1.0 / math.sqrt(HEAD))
    for b in range(blocks):
        r = slice(TILE * b, TILE * (b + 1))
        both = jnp.concatenate([gq[:, r].T, gk[r, :]], axis=1)
        gj_ref[r, : 2 * HEAD] = turn(both, cos_ref[r, :], -sa_ref[r, :], -sb_ref[r, :]).astype(BF16)
        gj_ref[r, 2 * HEAD : 3 * HEAD] = gv[r, :].astype(BF16)
    grad_t[...] = mm(first_ref[...], gj_ref[:, : 3 * HEAD], TN).astype(BF16)
    grad_m = mm(att_ref[...], back_ref[...]).astype(BF16)
    wide = 3 * HEAD
    half = grad_t.shape[0] // 2
    for s, g_ref in ((f_ref[0], g_keep_ref), (1 - f_ref[0], g_send_ref)):
        g_ref[:half, :] = grad_t[pl.ds(pl.multiple_of(s * half, half), half), :]
        for k in range(grad_m.shape[1] // wide):
            g_ref[half + HEAD * k : half + HEAD * (k + 1), :] = grad_m[:, wide * k : wide * (k + 1)]
    for b in range(blocks):
        slot = slot_ref[b]
        r = slice(TILE * b, TILE * (b + 1))

        @pl.when(slot < blocks // 2)
        def _(r=r, slot=slot):
            keep_ref[slot] = gj_ref[r, :]

        @pl.when(slot >= blocks // 2)
        def _(r=r, slot=slot):
            send_ref[slot - blocks // 2] = gj_ref[r, :]


def attend(slot, f, qk, vd, tables, first, back, h):
    rows = qk.shape[1]
    width = first.shape[1]
    packed = pl.BlockSpec((1, rows, 2 * HEAD), lambda *_: (h, 0, 0))
    g_rows = width // 2 + width // (3 * HEAD) * HEAD
    outs = [
        jax.ShapeDtypeStruct((rows // TILE // 2, TILE, 4 * HEAD), BF16),
        jax.ShapeDtypeStruct((rows // TILE // 2, TILE, 4 * HEAD), BF16),
        jax.ShapeDtypeStruct((g_rows, 3 * HEAD), BF16),
        jax.ShapeDtypeStruct((g_rows, 3 * HEAD), BF16),
    ]
    return pl.pallas_call(
        attend_kernel,
        grid_spec=pltpu.PrefetchScalarGridSpec(
            num_scalar_prefetch=2,
            grid=(1,),
            in_specs=[packed, packed]
            + [whole((rows, 2 * HEAD))] * 3
            + [whole(first.shape), whole(back.shape)],
            out_specs=[whole(v.shape) for v in outs],
            scratch_shapes=[
                pltpu.VMEM((2 * HEAD, rows), BF16),
                pltpu.VMEM((2 * HEAD, rows), BF16),
                pltpu.VMEM((rows, HEAD), BF16),
                pltpu.VMEM((rows, HEAD), BF16),
                pltpu.VMEM((rows, HEAD), BF16),
                pltpu.VMEM((rows, TILE), F32),
                pltpu.VMEM((HEAD, rows), F32),
                pltpu.VMEM((rows, HEAD), F32),
                pltpu.VMEM((rows, HEAD), F32),
                pltpu.VMEM((HEAD, rows), BF16),
                pltpu.VMEM((rows, 4 * HEAD), BF16),
                pltpu.VMEM((width, 3 * HEAD), BF16),
            ],
        ),
        out_shape=outs,
        compiler_params=params(),
        cost_estimate=beside(20 * rows * width),
        name="attend",
    )(slot, f, qk, vd, *tables, first, back)


def collect_kernel(f_ref, a_ref, b_ref, *refs, heads):
    (so_far_ref, sums0_ref, vec_ref, own_ref, other_ref, wm_ref, wm_far_ref), refs = refs[:7], refs[7:]
    packs, refs = refs[: 2 * len(heads)], refs[2 * len(heads) :]
    out_ref, sums_ref, wt_ref = refs
    step = pl.program_id(0)
    first = heads[0] == 0
    wide = 3 * HEAD
    count = len(heads)
    all_heads = own_ref.shape[1] // wide // 2

    @pl.when(step == 0)
    def _():
        f, rows = f_ref[0], own_ref.shape[0]
        for k in range(2):
            for i, h in enumerate(heads):
                part = slice(wide * (all_heads * k + h), wide * (all_heads * k + h + 1))
                to = count * k + i
                wt_ref[to, pl.ds(pl.multiple_of(f * rows, rows), rows), :] = own_ref[:, part]
                wt_ref[to, pl.ds(pl.multiple_of((1 - f) * rows, rows), rows), :] = other_ref[:, part]
        sums_ref[...] = jnp.zeros_like(sums_ref) if first else sums0_ref[...]

    gain = vec_ref[0:1, :]
    n = normal(choose(step, (a_ref, b_ref), 0).astype(F32))
    merged = jnp.zeros(n.shape, F32)
    grad_first = jnp.zeros(n.shape, F32)
    for k, weights in enumerate((wm_ref, wm_far_ref)):
        for i, h in enumerate(heads):
            pack = packs[count * k + i]
            merged = merged + mm(pack[0, :, wide:], weights[HEAD * h : HEAD * (h + 1), :])
            gj = pack[0, :, :wide]
            row = 2 + all_heads * k + h
            sums_ref[row : row + 1, :wide] += colsum(gj.astype(F32))
            grad_first = grad_first + mm(gj, wt_ref[count * k + i], NT)
    u = grad_first * gain
    if not first:
        merged = merged + so_far_ref[0, 0].astype(F32)
        u = u + so_far_ref[0, 1].astype(F32)
    out_ref[0, 0] = merged.astype(BF16)
    out_ref[0, 1] = u.astype(BF16)
    sums_ref[0:1, :] += colsum(grad_first * n)
    sums_ref[1:2, :] += colsum(grad_first)


def collect(f, own_x, near_x, heads, packs, packs_far, vec, own, other, wm, wm_far, so_far=None):
    _, rows, width = own_x.shape
    pack = pl.BlockSpec((1, TILE, 4 * HEAD), lambda i, *_: (i, 0, 0))
    block = pl.BlockSpec((1, 2, TILE, width), lambda i, *_: (i // 2, 0, i % 2, 0))
    if so_far is None:
        so_far = (jnp.zeros((8, 128), F32),) * 2
        so_far_spec = whole((8, 128))
    else:
        so_far_spec = block
    return pl.pallas_call(
        functools.partial(collect_kernel, heads=heads),
        grid_spec=pltpu.PrefetchScalarGridSpec(
            num_scalar_prefetch=1,
            grid=(2 * rows // TILE,),
            in_specs=piece_specs(2, 1, width)
            + [so_far_spec]
            + [whole(v.shape) for v in (so_far[1], vec, own, other, wm, wm_far)]
            + [pack] * (2 * len(heads)),
            out_specs=[block, whole((8, width))],
            scratch_shapes=[pltpu.VMEM((2 * len(heads), width, 3 * HEAD), BF16)],
        ),
        out_shape=[
            jax.ShapeDtypeStruct((2, 2, rows, width), BF16),
            jax.ShapeDtypeStruct((8, width), F32),
        ],
        compiler_params=params(),
        cost_estimate=beside(10 * rows * width),
        name="collect",
    )(f, own_x, near_x, *so_far, vec, own, other, wm, wm_far, *packs, *packs_far)


def slot_part(refs, slot, index):
    value = refs[0][index]
    for k in range(1, len(refs)):
        value = jnp.where(slot == k, refs[k][index], value)
    return value


def put_expand_kernel(c_ref, d_ref, *refs, shards):
    *ins, out = refs
    count, rows, columns = ins[0].shape
    cut = columns // shards
    k = (d_ref[0] - pl.program_id(0) + count) % count
    for b in range(CTX):
        slot = slot_of(c_ref[0] ^ b)
        value = slot_part(ins, slot, k).astype(F32)
        for g in range(shards):
            out[:, (g * CTX + b) * cut : (g * CTX + b + 1) * cut] = value[:, g * cut : (g + 1) * cut]


def put_expand(c, d, parts, shards):
    count, rows, columns = parts[0].shape
    return pl.pallas_call(
        functools.partial(put_expand_kernel, shards=shards),
        grid_spec=pltpu.PrefetchScalarGridSpec(
            num_scalar_prefetch=2,
            grid=(count // 2,),
            in_specs=[whole(parts[0].shape)] * CTX,
            out_specs=pl.BlockSpec((rows, CTX * columns), lambda a, *_: (a, 0)),
        ),
        out_shape=jax.ShapeDtypeStruct((count // 2 * rows, CTX * columns), F32),
        compiler_params=params(),
        cost_estimate=beside(50 * rows * columns),
        name="put_expand",
    )(c, d, *parts)


def put_reduce_kernel(c_ref, d_ref, *refs):
    *ins, out = refs
    count, rows, columns = ins[0].shape
    slot = slot_of(c_ref[0] ^ pl.program_id(0))
    for a in range(count // 2):
        k = (d_ref[0] - a - count // 2 + count) % count
        out[rows * a : rows * (a + 1), :] = slot_part(ins, slot, k).astype(F32)


def put_reduce(c, d, parts):
    count, rows, columns = parts[0].shape
    own = count // 2 * rows
    return pl.pallas_call(
        put_reduce_kernel,
        grid_spec=pltpu.PrefetchScalarGridSpec(
            num_scalar_prefetch=2,
            grid=(CTX,),
            in_specs=[whole(parts[0].shape)] * CTX,
            out_specs=pl.BlockSpec((own, columns), lambda b, *_: (b, 0)),
        ),
        out_shape=jax.ShapeDtypeStruct((CTX * own, columns), F32),
        compiler_params=params(),
        cost_estimate=beside(50 * rows * columns),
        name="put_reduce",
    )(c, d, *parts)


def put_heads_kernel(c_ref, d_ref, f_ref, *refs, top, with_merge):
    two, one = refs[:CTX], refs[CTX : 2 * CTX]
    outs = refs[2 * CTX : 2 * CTX + 1 + with_merge]
    s2, s1 = refs[2 * CTX + 1 + with_merge :]
    count, rows, wide = one[0].shape
    for b in range(CTX):
        slot = slot_of(c_ref[0] ^ b)
        for a in range(count):
            k = (d_ref[0] - a + count) % count
            s2[rows * a : rows * (a + 1), :] = slot_part(two, slot, k)
            s1[rows * a : rows * (a + 1), :] = slot_part(one, slot, k)
        at = 3 * wide * b
        outs[0][:, at : at + 2 * wide] = s2[:top, :].astype(F32)
        outs[0][:, at + 2 * wide : at + 3 * wide] = s1[:top, :].astype(F32)
        if with_merge:
            per = (count * rows - top) // HEAD

            @pl.when(b // (CTX // 2) == f_ref[0])
            def _(b=b):
                for h in range(3):
                    row = 3 * HEAD * (b % (CTX // 2)) + HEAD * h
                    for k in range(per):
                        src = slice(top + HEAD * k, top + HEAD * (k + 1))
                        part = s1[src, :] if h == 2 else s2[src, wide * h : wide * (h + 1)]
                        outs[1][row : row + HEAD, wide * k : wide * (k + 1)] = part.astype(F32)


def put_heads(c, d, f, two, one, top, width, with_merge):
    count, rows, wide = one[0].shape
    shapes = [jax.ShapeDtypeStruct((top, 3 * CTX * wide), F32)]
    if with_merge:
        shapes.append(jax.ShapeDtypeStruct((width // 2, width), F32))
    return pl.pallas_call(
        functools.partial(put_heads_kernel, top=top, with_merge=with_merge),
        grid_spec=pltpu.PrefetchScalarGridSpec(
            num_scalar_prefetch=3,
            grid=(1,),
            in_specs=[whole(v.shape) for v in (*two, *one)],
            out_specs=[whole(v.shape) for v in shapes],
            scratch_shapes=[
                pltpu.VMEM((count * rows, 2 * wide), BF16), pltpu.VMEM((count * rows, wide), BF16)
            ],
        ),
        out_shape=shapes,
        compiler_params=params(),
        cost_estimate=short(),
        name="put_heads",
    )(c, d, f, *two, *one)


def rotary(rows):
    lane = jnp.arange(2 * HEAD, dtype=jnp.int32)[None, :] % HEAD
    half = ROT // 2
    inverse = 10000.0 ** (-2.0 * (lane % half).astype(F32) / ROT)
    angles = jnp.arange(rows, dtype=jnp.int32).astype(F32)[:, None] * inverse
    cos = jnp.where(lane < ROT, jnp.cos(angles), 1.0)
    sine = jnp.sin(angles)
    low = jnp.where(lane < half, -sine, 0.0)
    high = jnp.where((lane >= half) & (lane < ROT), sine, 0.0)
    return cos, low, high


def local(
    tokens, cotangent, block_order, first_gain, first_shift, second_gain, second_shift,
    triple_weight, triple_bias, merge_weight, merge_bias, expand_weight, expand_bias,
    reduce_weight, reduce_bias,
):
    c, d, f = lax.axis_index("ctx"), lax.axis_index("dp"), lax.axis_index("fsdp")
    shards = lax.axis_size("fsdp")
    own_len, width = tokens.shape[1:]
    inner = expand_weight.shape[1]
    own_inner = inner // shards // CTX
    ctx_inner = inner // CTX
    own_heads = HEADS // CTX
    own_cols = own_heads * 3 * HEAD
    own_merge = own_heads * HEAD
    half = CTX // 2

    own_expand = jnp.concatenate(
        [
            lax.dynamic_slice_in_dim(expand_weight, g * CTX * own_inner + c * own_inner, own_inner, 1)
            for g in range(shards)
        ],
        axis=1,
    )
    own_reduce = lax.dynamic_slice_in_dim(reduce_weight, c * own_inner, own_inner, 0)
    own_bias = lax.dynamic_slice_in_dim(expand_bias, c * own_inner, own_inner, 0)
    own_triple = jnp.concatenate(
        [lax.dynamic_slice_in_dim(triple_weight, k * own_cols, own_cols, 1) for k in (c, c ^ 2)], axis=1
    )
    smalls = jnp.stack(
        [first_gain, first_shift, second_gain, second_shift, own_bias, merge_bias, reduce_bias]
    )
    if shards == 2:
        own_tb = lax.dynamic_slice_in_dim(triple_bias, (c % half) * own_cols, own_cols, 0)
        rows = jnp.concatenate(
            [
                jnp.pad(smalls, ((0, 1), (0, width - smalls.shape[1]))),
                jnp.pad(own_tb[None], ((0, 7), (0, width - own_cols))),
            ]
        )
        w_own = jnp.concatenate([own_expand, own_reduce, rows])
        w_other = swap(w_own, "fsdp", 1)
        last = width // 2 + ctx_inner // 2
        own_s, other_s = w_own[last:], w_other[last:]
        cut = smalls.shape[1]
        vec = jnp.where(
            f == 0,
            jnp.concatenate([own_s[:8, :cut], other_s[:8, :cut]], axis=1),
            jnp.concatenate([other_s[:8, :cut], own_s[:8, :cut]], axis=1),
        ).astype(F32)
        tb = jnp.where(f == c // half, own_s[8, :own_cols], other_s[8, :own_cols]).astype(F32)
        t_own = own_triple
        m_own = lax.dynamic_slice_in_dim(merge_weight, (c % half) * own_merge, own_merge, 0)
        side = f
    else:
        def full(v):
            return lax.all_gather(v, "fsdp", axis=0, tiled=True)

        we, wr, wt = full(own_expand), full(own_reduce), full(own_triple)
        w_own = jnp.concatenate([we[: width // 2], wr[: ctx_inner // 2]])
        w_other = jnp.concatenate([we[width // 2 :], wr[ctx_inner // 2 :]])
        t_own, t_other = wt[: width // 2], wt[width // 2 :]
        vec = lax.all_gather(smalls, "fsdp", axis=1, tiled=True).astype(F32)
        vec = jnp.pad(vec, ((0, 1), (0, 0)))
        tb = lax.dynamic_slice_in_dim(full(triple_bias), c * own_cols, own_cols, 0).astype(F32)
        m_own = full(merge_weight)
        side = jnp.int32(0)
    tb = tb.reshape(own_heads, 1, 3 * HEAD)
    flag = side.astype(jnp.int32).reshape(1)

    own = jnp.stack([tokens.reshape(own_len, width), cotangent.reshape(own_len, width)])
    far = swap(own, "ctx", 2)
    near = swap(own, "ctx", 1)
    pos = jnp.concatenate(
        [lax.dynamic_slice_in_dim(block_order, 2 * (c ^ r), 2) for r in range(CTX)]
    )
    blocks = jnp.arange(pos.shape[0], dtype=jnp.int32)
    slot = jnp.sum(jnp.where(pos[None, :] == blocks[:, None], blocks[None, :], 0), axis=1)
    slot = slot.astype(jnp.int32)
    tables = rotary(CTX * own_len)
    far, t_own, m_own, w_other, *tables = lax.optimization_barrier(
        (far, t_own, m_own, w_other, *tables)
    )
    both = swap(far, "ctx", 1)
    if shards == 2:
        t_other, m_other = swap(t_own, "fsdp", 1), swap(m_own, "fsdp", 1)
    else:
        m_own, m_other = (
            lax.dynamic_slice_in_dim(m_own, k * own_merge, own_merge, 0) for k in (c, c ^ 2)
        )

    lu_keep, lu_send, *g_feed, sums2 = feed(
        flag, own, far, near, both, vec, w_own, w_other, width, ctx_inner
    )
    way_f = Summed(split_feed(g_feed, shards, width), f, d)
    lu_send, pos, t_other, m_other = boundary([way_f], lu_send, pos, t_other, m_other)
    if shards == 2:
        wm = jnp.where(f == c // half, m_own, m_other)
        wm_far = jnp.where(f == c // half, m_other, m_own)
    else:
        wm, wm_far = m_own, m_other
    lu_in = swap(lu_send, "ctx", 1)
    last = pos.shape[0] // 2
    qk, vd, first, back = project(
        pos[:last], flag, (own, near), vec, tb, t_own, t_other, wm, tables
    )
    lu_far = add_low(lu_keep[1], lu_in[1])
    qk, lu_far = boundary([way_f], qk, lu_far)
    lu_far = swap(lu_far, "ctx", 2)
    qk, vd, first, back = project(
        pos[last:], flag, (far, both), vec, tb, t_own, t_other, wm, tables, (qk, vd, first, back)
    )
    packs, packs_far, gs = [], [], []

    def next_head(qk, h):
        pack, sent, *g = attend(slot, flag, qk, vd, tables, first, back, h)
        packs.append(pack)
        gs.append(g)
        return sent

    sent = next_head(qk, 0)
    qk, sent, lu_far = boundary([way_f], qk, sent, lu_far)
    packs_far.append(swap(sent, "ctx", 2))
    sent = next_head(qk, 1)
    g_two = [jnp.concatenate(g, axis=1) for g in zip(*gs)]
    way_two = Summed(split_rows(g_two, shards, width), f, d)
    qk, sent_two, packs_far[0] = boundary([way_two, way_f], qk, sent, packs_far[0])
    sent_one = next_head(qk, 2)
    way_one = Summed(split_rows(gs[-1], shards, width), f, d)
    ways = [way_one, way_two]
    c1, d1, f1 = (v.astype(jnp.int32).reshape(1) for v in (c, d, f))
    c1, sent_two, sent_one = boundary(ways + [way_f], c1, sent_two, sent_one)
    packs_far.append(swap(sent_two, "ctx", 2))
    feed_parts = way_f.finish()
    c1, feed_parts = boundary([way_one], c1, feed_parts)
    grad_expand = put_expand(c1, d1, feed_parts, shards)
    grad_reduce = put_reduce(c1, d1, feed_parts)
    flag1, grad_expand, grad_reduce, sent_one, packs_far[1] = boundary(
        ways, flag, grad_expand, grad_reduce, sent_one, packs_far[1]
    )
    packs_far.append(swap(sent_one, "ctx", 2))
    so_far = collect(
        flag1, own, near, (0, 1), packs[:2], packs_far[:2], vec, t_own, t_other, wm, wm_far
    )
    flag1, packs_far[2], so_far = boundary(ways, flag, packs_far[2], so_far)
    mu, sums1 = collect(
        flag1, own, near, (2,), packs[2:], packs_far[2:], vec, t_own, t_other, wm, wm_far, so_far
    )

    tb_rows = sums1[2 : 2 + 2 * own_heads, : 3 * HEAD].reshape(2, own_cols)
    tb_rows = jnp.pad(tb_rows, ((0, 0), (0, width - own_cols)))
    eb_row = jnp.pad(sums2[2:3], ((0, 0), (0, width - ctx_inner)))
    mine = (jnp.arange(CTX) == c)[:, None]
    across = (jnp.arange(CTX) == (c ^ 2))[:, None]
    tb_block = jnp.where(mine, tb_rows[:1], jnp.where(across, tb_rows[1:], 0.0))
    vector = jnp.concatenate(
        [sums1[:2], sums2[:2], sums2[3:4], tb_block, jnp.where(mine, eb_row, 0.0)]
    )
    vector = jnp.pad(vector, ((0, 3), (0, 0)))

    c1, mu, vector = boundary(ways, c1, mu, vector)
    mu_in = swap(mu[1], "ctx", 1)
    vector = vector + swap(vector, "ctx", 2)
    mu_in, vector = boundary(ways, mu_in, vector)
    if shards == 2:
        vector_in = swap(vector, "fsdp", 1)
    else:
        vector, vector_in = lax.psum(vector, "fsdp"), 0.0
    lu = lu_keep[0].astype(F32) + lu_in[0].astype(F32) + lu_far.astype(F32)
    mixed, u = lu + mu[0].astype(F32) + mu_in.astype(F32)

    x_f = own[0].astype(F32)
    mixed = (x_f + mixed + (vec[5] + vec[6])[None, :]).astype(BF16)
    average = jnp.mean(x_f, axis=-1, keepdims=True)
    centred = x_f - average
    r = lax.rsqrt(jnp.mean(centred * centred, axis=-1, keepdims=True) + epsilon)
    n = centred * r
    input_grad = own[1].astype(F32) + r * (
        u - jnp.mean(u, axis=-1, keepdims=True) - n * jnp.mean(u * n, axis=-1, keepdims=True)
    )

    vector = vector + vector_in
    vector = vector + swap(vector, "dp", 1)
    vector = vector + swap(vector, "dp", 2)
    vector = vector + swap(vector, "ctx", 1)
    part = width // shards
    five = lax.dynamic_slice_in_dim(vector[:5], f * part, part, 1)
    d_g1, d_s1, d_g2, d_s2, d_cot = [five[i] for i in range(5)]
    d_tb = vector[5 : 5 + CTX, :own_cols].reshape(-1)
    d_tb = lax.dynamic_slice_in_dim(d_tb, f * (3 * part), 3 * part, 0)
    d_eb = lax.dynamic_slice_in_dim(vector[5 + CTX : 5 + 2 * CTX], f * own_inner, own_inner, 1)
    d_eb = d_eb.reshape(-1)

    two, one = way_two.finish(), way_one.finish()
    placed = put_heads(c1, d1, f1, two, one, part, width, shards == 2)
    grad_triple = placed[0]
    if shards == 2:
        grad_merge = placed[1]
    else:
        count = lax.axis_size("dp")
        g_all = [
            jnp.concatenate([pick(g, (d - a) % count) for a in range(count)])
            for g in in_order([jnp.concatenate([a, b], axis=2) for a, b in zip(two, one)], c)
        ]
        wide = 3 * HEAD
        grad_merge = jnp.concatenate(
            [
                g[part:].reshape(width // wide, HEAD, own_heads, wide).transpose(2, 1, 0, 3)
                .reshape(own_merge, width) for g in g_all
            ]
        )
        grad_merge = lax.dynamic_slice_in_dim(grad_merge, f * part, part, 0).astype(F32)
    return (
        mixed[None],
        input_grad[None],
        d_g1,
        d_s1,
        d_g2,
        d_s2,
        grad_triple,
        d_tb,
        grad_merge,
        d_cot,
        grad_expand,
        d_eb,
        grad_reduce,
        d_cot,
    )


def split_feed(g, shards, width):
    if shards == 2:
        return tuple(g)
    g = jnp.stack(g)
    half = width // 2
    ge, gr = g[:, :half].reshape(width, -1), g[:, half:].reshape(-1, width)
    parts = [v.reshape(shards, v.shape[0] // shards, v.shape[1]) for v in (ge, gr)]
    return jnp.concatenate(parts, axis=1)


def split_rows(g, shards, width):
    if shards == 2:
        return tuple(g)
    g = jnp.stack(g)
    rows = g[:, : width // 2].reshape(shards, width // shards, g.shape[2])
    tail = jnp.broadcast_to(g[:1, width // 2 :], (shards,) + g[0, width // 2 :].shape)
    return jnp.concatenate([rows, tail], axis=1)


def solution(mesh):
    tokens = P(("dp", "fsdp"), "ctx", None)
    row, vector = P("fsdp", None), P("fsdp")
    weights = (row, vector, row, vector, row, vector, row, vector)
    in_specs = (tokens, tokens, P()) + (vector,) * 4 + weights
    out_specs = (tokens, tokens) + (vector,) * 4 + weights
    return jax.shard_map(local, mesh=mesh, in_specs=in_specs, out_specs=out_specs, check_vma=False)
```

```python
import functools
import math

import jax
import jax.numpy as jnp
from jax import lax
from jax.experimental import pallas as pl
from jax.experimental.pallas import tpu as pltpu
from jax.sharding import PartitionSpec as P

HEADS = 12
HEAD = 64
ROT = 16
TILE = 256
CTX = 4
epsilon = 1e-05
masked_value = -1e30
F32 = jnp.float32
BF16 = jnp.bfloat16
VMEM_LIMIT = 58 * 1024 * 1024

NN = (((1,), (0,)), ((), ()))
NT = (((1,), (1,)), ((), ()))
TN = (((0,), (0,)), ((), ()))


def mm(a, b, dims=NN):
    return lax.dot_general(a, b, dims, preferred_element_type=F32)


def swap(value, axis, bit):
    count = lax.axis_size(axis)
    return lax.ppermute(value, axis, [(i, i ^ bit) for i in range(count)])


def pick(stacked, index):
    return lax.dynamic_index_in_dim(stacked, index, 0, keepdims=False)


def add_low(a, b):
    return (a.astype(F32) + b.astype(F32)).astype(BF16)


def after(value, *others):
    return lax.optimization_barrier((value,) + others)[0]


def slot_of(relative):
    return (relative % 2) * 2 + relative // 2


def in_order(both, c):
    both = jnp.stack(both)
    return [pick(both, slot_of(c ^ b)) for b in range(CTX)]


class Summed:
    def __init__(self, value, f, d):
        self.value, self.f, self.d = value, f, d
        self.steps = ["fsdp", "dp_down", "dp_up", "far", "near"]
        self.moving = None

    def send(self):
        kind, value = self.steps[0], self.value
        count = lax.axis_size("dp")
        if kind == "fsdp":
            self.moving = [value[1]] if isinstance(value, tuple) else []
        elif kind == "dp_down":
            self.value = value.reshape(count, value.shape[0] // count, value.shape[1])
            self.moving = [pick(self.value, (self.d + k) % count) for k in range(1, count)]
        elif kind == "near":
            self.moving = [value[1]]
        else:
            self.moving = [value]
        return self.moving

    def receive(self):
        kind, moving = self.steps[0], self.moving
        count = lax.axis_size("dp")
        turns = [[(i, (i + k) % count) for i in range(count)] for k in range(1, count)]
        if kind == "fsdp":
            return [swap(v, "fsdp", 1) for v in moving]
        if kind == "dp_down":
            return [lax.ppermute(v, "dp", t) for v, t in zip(moving, turns)]
        if kind == "dp_up":
            return [lax.ppermute(moving[0], "dp", t) for t in turns]
        if kind == "far":
            return [swap(moving[0], "ctx", 2), swap(moving[0], "ctx", 1)]
        return [swap(moving[0], "ctx", 1)]

    def take(self, came):
        kind = self.steps.pop(0)
        if kind == "fsdp":
            if came:
                self.value = add_low(self.value[0], came[0])
            else:
                self.value = lax.psum_scatter(self.value, "fsdp", scatter_dimension=0, tiled=False)
        elif kind == "dp_down":
            total = pick(self.value, self.d).astype(F32)
            for v in came:
                total = total + v.astype(F32)
            self.value = total.astype(BF16)
        elif kind == "dp_up":
            self.value = jnp.stack([self.moving[0]] + came)
        elif kind == "far":
            self.value = [self.moving[0]] + came
        else:
            self.value = self.value + came
        self.moving = None

    def beside(self, other):
        self.value = jnp.concatenate([self.value, other.value], axis=1)
        return self

    def finish(self):
        while self.steps:
            if self.moving is None:
                self.send()
            self.take(self.receive())
        return self.value


def boundary(ways, *values, hold=()):
    moved = [way for way in (*ways, *hold) if way.moving is not None]
    came, values = lax.optimization_barrier(([way.receive() for way in moved], values))
    for way, v in zip(moved, came):
        way.take(v)
    for way in ways:
        way.moving = way.send() if way.steps else None
    for way in hold:
        way.value, values = lax.optimization_barrier((way.value, values))
    sent = [tuple(way.moving or ()) for way in ways]
    sent, values = lax.optimization_barrier((sent, values))
    for way, moving in zip(ways, sent):
        if way.moving is not None:
            way.moving = list(moving)
    return values


def normal(x):
    average = jnp.mean(x, axis=-1, keepdims=True)
    centred = x - average
    spread = jnp.mean(centred * centred, axis=-1, keepdims=True)
    return centred * lax.rsqrt(spread + epsilon)


def colsum(v):
    return jnp.sum(v, axis=0, keepdims=True)


def whole(shape):
    return pl.BlockSpec(shape, lambda *_: (0,) * len(shape))


def params(**more):
    return pltpu.CompilerParams(
        dimension_semantics=("arbitrary",), vmem_limit_bytes=VMEM_LIMIT, **more
    )


def cost(flops, moved, exps=0):
    return pl.CostEstimate(flops=flops, bytes_accessed=moved, transcendentals=exps)


def beside(moved):
    return cost(0, 100 * moved)


def short():
    return cost(0, 0)


def place(f, own, other, out):
    rows = own.shape[0]
    out[pl.ds(pl.multiple_of(f * rows, rows), rows), :] = own
    out[pl.ds(pl.multiple_of((1 - f) * rows, rows), rows), :] = other


def feed_kernel(
    f_ref, a_ref, b_ref, c_ref, d_ref, vec_ref, own_ref, other_ref,
    keep_ref, send_ref, g_keep_ref, g_send_ref, sums_ref, we_ref, wr_ref, ge_acc, gr_acc,
):
    step = pl.program_id(0)
    half = we_ref.shape[0] // 2

    @pl.when(step == 0)
    def _():
        f = f_ref[0]
        place(f, own_ref[:half], other_ref[:half], we_ref)
        place(f, own_ref[half : 2 * half], other_ref[half : 2 * half], wr_ref)
        ge_acc[...] = jnp.zeros_like(ge_acc)
        gr_acc[...] = jnp.zeros_like(gr_acc)
        sums_ref[...] = jnp.zeros_like(sums_ref)
        sums_ref[3:4, :] = colsum(a_ref[1].astype(F32))

    def piece(k):
        first = jnp.where(step == 0, a_ref[k], b_ref[k])
        return jnp.where(step < 2, first, jnp.where(step == 2, c_ref[k], d_ref[k]))

    gain, shift, bias = vec_ref[2:3, :], vec_ref[3:4, :], vec_ref[4:5, :]
    n = normal(piece(0).astype(F32))
    second = (n * gain + shift).astype(BF16)
    back = piece(1)
    hidden = mm(second, we_ref[...]) + bias
    cdf = 0.5 * (1.0 + lax.erf(hidden * (1.0 / math.sqrt(2.0))))
    active = (hidden * cdf).astype(BF16)
    low = mm(active, wr_ref[...]).astype(BF16)
    slope = cdf + hidden * (jnp.exp(-0.5 * hidden * hidden) * (1.0 / math.sqrt(2.0 * math.pi)))
    grad_hidden = (mm(back, wr_ref[...], NT) * slope).astype(BF16)
    gr_acc[...] += mm(active, back, TN)
    ge_acc[...] += mm(second, grad_hidden, TN)
    grad_second = mm(grad_hidden, we_ref[...], NT)
    u = (grad_second * gain).astype(BF16)
    sums_ref[0:1, :] += colsum(grad_second * n)
    sums_ref[1:2, :] += colsum(grad_second)
    sums_ref[2:3, :] += colsum(grad_hidden.astype(F32))

    @pl.when(step < 2)
    def _():
        keep_ref[0, 0], keep_ref[0, 1] = low, u

    @pl.when(step >= 2)
    def _():
        send_ref[0, 0], send_ref[0, 1] = low, u

    @pl.when(step == pl.num_programs(0) - 1)
    def _():
        for s, g_ref in ((f_ref[0], g_keep_ref), (1 - f_ref[0], g_send_ref)):
            rows = pl.ds(pl.multiple_of(s * half, half), half)
            g_ref[:half] = ge_acc[rows, :].astype(BF16)
            g_ref[half:] = gr_acc[rows, :].astype(BF16)


def feed(f, own_x, far, near, both, vec, own, other, width, inner):
    rows = own_x.shape[1]
    shape_e, shape_r = (width, inner), (inner, width)
    outs = [
        jax.ShapeDtypeStruct((2, 2, rows, width), BF16),
        jax.ShapeDtypeStruct((2, 2, rows, width), BF16),
        jax.ShapeDtypeStruct(((width + inner) // 2, width), BF16),
        jax.ShapeDtypeStruct(((width + inner) // 2, width), BF16),
        jax.ShapeDtypeStruct((8, width), F32),
    ]
    args = (own_x, far, near, both, vec, own, other)
    block = (1, 2, rows, width)
    return pl.pallas_call(
        feed_kernel,
        grid_spec=pltpu.PrefetchScalarGridSpec(
            num_scalar_prefetch=1,
            grid=(CTX,),
            in_specs=[whole(v.shape) for v in args],
            out_specs=[
                pl.BlockSpec(block, lambda i, *_: (jnp.minimum(i, 1), 0, 0, 0)),
                pl.BlockSpec(block, lambda i, *_: (jnp.maximum(i - 2, 0), 0, 0, 0)),
            ]
            + [whole(v.shape) for v in outs[2:]],
            scratch_shapes=[
                pltpu.VMEM(shape_e, BF16), pltpu.VMEM(shape_r, BF16),
                pltpu.VMEM(shape_e, F32), pltpu.VMEM(shape_r, F32),
            ],
        ),
        out_shape=outs,
        compiler_params=params(),
        cost_estimate=beside(16 * rows * width),
        name="feed",
    )(f, *args)


def turn(u, cos, sin_a, sin_b):
    return u * cos + pltpu.roll(u, 120, 1) * sin_a + pltpu.roll(u, 8, 1) * sin_b


def place_heads(f, own, other, out):
    rows = own.shape[0]
    wide = out.shape[2]
    for h in range(out.shape[0]):
        part = slice(wide * h, wide * (h + 1))
        out[h, pl.ds(pl.multiple_of(f * rows, rows), rows), :] = own[:, part]
        out[h, pl.ds(pl.multiple_of((1 - f) * rows, rows), rows), :] = other[:, part]


def choose(step, refs, index):
    value = refs[-1][index]
    for k in range(len(refs) - 2, -1, -1):
        value = jnp.where(step < 2 * k + 2, refs[k][index], value)
    return value


def piece_specs(count, lead, width, first=0):
    return [
        pl.BlockSpec(
            (lead, TILE, width), lambda i, *_, k=k: (first, jnp.clip(i - 2 * k, 0, 1), 0)
        )
        for k in range(count)
    ]


def project_kernel(pos_ref, f_ref, a_ref, b_ref, vec_ref, tb_ref, own_ref, other_ref, wm_ref,
    cos_ref, sa_ref, sb_ref, *refs):
    qk_ref, vd_ref, first_ref, back_ref, wt_ref = refs[-5:]
    step = pl.program_id(0)

    @pl.when(step == 0)
    def _():
        place_heads(f_ref[0], own_ref[...], other_ref[...], wt_ref)

    pieces = (a_ref, b_ref)
    x = choose(step, pieces, 0)
    back = choose(step, pieces, 1)
    first = (normal(x.astype(F32)) * vec_ref[0:1, :] + vec_ref[1:2, :]).astype(BF16)
    first_ref[...] = first
    back_ref[...] = back
    grad_out = mm(back, wm_ref[...], NT)
    heads = wt_ref.shape[0]
    lane = lax.broadcasted_iota(jnp.int32, (TILE, 2 * HEAD), 1)
    scale = jnp.where(lane < HEAD, 1.0 / math.sqrt(HEAD), 1.0)
    for h in range(heads):
        joined = mm(first, wt_ref[h]) + tb_ref[h]
        turned = turn(joined[:, : 2 * HEAD], cos_ref[...], sa_ref[...], sb_ref[...])
        qk_ref[h] = (turned * scale).astype(BF16)
        vd_ref[h, :, :HEAD] = joined[:, 2 * HEAD :].astype(BF16)
        vd_ref[h, :, HEAD:] = grad_out[:, HEAD * h : HEAD * (h + 1)].astype(BF16)


def project(pos, f, pieces, vec, tb, own, other, wm, tables, so_far=()):
    width = pieces[0].shape[2]
    rows = CTX * pieces[0].shape[1]
    heads = tb.shape[0]
    table = pl.BlockSpec((TILE, 2 * HEAD), lambda i, p, f: (p[i], 0))
    out = pl.BlockSpec((heads, TILE, 2 * HEAD), lambda i, p, f: (0, p[i], 0))
    row = pl.BlockSpec((TILE, width), lambda i, p, f: (p[i], 0))
    args = (pos, f, *pieces, vec, tb, own, other, wm, *tables)
    return pl.pallas_call(
        project_kernel,
        grid_spec=pltpu.PrefetchScalarGridSpec(
            num_scalar_prefetch=2,
            grid=(rows // TILE // 2,),
            in_specs=piece_specs(2, 2, width)
            + [whole(v.shape) for v in (vec, tb, own, other, wm)]
            + [table] * 3
            + [pl.BlockSpec(memory_space=pl.ANY)] * len(so_far),
            out_specs=[out, out, row, row],
            scratch_shapes=[pltpu.VMEM((heads, width, 3 * HEAD), BF16)],
        ),
        out_shape=[jax.ShapeDtypeStruct((heads, rows, 2 * HEAD), BF16)] * 2
        + [jax.ShapeDtypeStruct((rows, width), BF16)] * 2,
        input_output_aliases={len(args) + k: k for k in range(len(so_far))},
        compiler_params=params(),
        cost_estimate=beside(10 * rows * width),
        name="project",
    )(*args, *so_far)


def attend_kernel(
    slot_ref, f_ref, qk_ref, vd_ref, cos_ref, sa_ref, sb_ref, first_ref, back_ref, keep_ref, send_ref, g_keep_ref, g_send_ref,
    qt, vt, ks, vs, ds_, s_ref, gq, gk, gv, att_ref, gj_ref, grad_t,
):
    rows = qk_ref.shape[1]
    blocks = rows // TILE

    for b in range(blocks):
        r = slice(TILE * b, TILE * (b + 1))
        qt[:, r] = qk_ref[0, r, :].T
        vt[:, r] = vd_ref[0, r, :].T
        ks[r, :] = qk_ref[0, r, HEAD:]
        vs[r, :] = vd_ref[0, r, :HEAD]
        ds_[r, :] = vd_ref[0, r, HEAD:]
    key_id = lax.broadcasted_iota(jnp.int32, (TILE, TILE), 0)
    query_id = lax.broadcasted_iota(jnp.int32, (TILE, TILE), 1)
    keep = key_id <= query_id
    for i in range(blocks):
        qr = slice(TILE * i, TILE * (i + 1))
        q_t = qt[:HEAD, qr]
        peak = None
        for j in range(i + 1):
            kr = slice(TILE * j, TILE * (j + 1))
            s = mm(ks[kr, :], q_t)
            if j == i:
                s = jnp.where(keep, s, masked_value)
            s_ref[kr, :] = s
            top = jnp.max(s, axis=0, keepdims=True)
            peak = top if peak is None else jnp.maximum(peak, top)
        total = jnp.zeros((1, TILE), F32)
        out = jnp.zeros((HEAD, TILE), F32)
        for j in range(i + 1):
            kr = slice(TILE * j, TILE * (j + 1))
            e = jnp.exp(s_ref[kr, :] - peak)
            s_ref[kr, :] = e
            total = total + jnp.sum(e, axis=0, keepdims=True)
            out = out + mm(vt[:HEAD, kr], e.astype(BF16))
        inv = 1.0 / total
        out = out * inv
        att_ref[:, qr] = out.astype(BF16)
        gj_ref[qr, 3 * HEAD :] = out.T.astype(BF16)
        d_t = vt[HEAD:, qr]
        delta = jnp.sum(d_t.astype(F32) * out, axis=0, keepdims=True)
        q = qk_ref[0, qr, :HEAD]
        d = ds_[qr, :]
        grad_q = jnp.zeros((HEAD, TILE), F32)
        for j in range(i + 1):
            kr = slice(TILE * j, TILE * (j + 1))
            p = s_ref[kr, :] * inv
            grad_v = mm(p.astype(BF16), d)
            g = (p * (mm(vs[kr, :], d_t) - delta)).astype(BF16)
            grad_k = mm(g, q)
            grad_q = grad_q + mm(qt[HEAD:, kr], g)
            if j == i:
                gv[kr, :] = grad_v
                gk[kr, :] = grad_k
            else:
                gv[kr, :] += grad_v
                gk[kr, :] += grad_k
        gq[:, qr] = grad_q * (1.0 / math.sqrt(HEAD))
    for b in range(blocks):
        r = slice(TILE * b, TILE * (b + 1))
        both = jnp.concatenate([gq[:, r].T, gk[r, :]], axis=1)
        gj_ref[r, : 2 * HEAD] = turn(both, cos_ref[r, :], -sa_ref[r, :], -sb_ref[r, :]).astype(BF16)
        gj_ref[r, 2 * HEAD : 3 * HEAD] = gv[r, :].astype(BF16)
    grad_t[...] = mm(first_ref[...], gj_ref[:, : 3 * HEAD], TN).astype(BF16)
    grad_m = mm(att_ref[...], back_ref[...]).astype(BF16)
    wide = 3 * HEAD
    half = grad_t.shape[0] // 2
    for s, g_ref in ((f_ref[0], g_keep_ref), (1 - f_ref[0], g_send_ref)):
        g_ref[:half, :] = grad_t[pl.ds(pl.multiple_of(s * half, half), half), :]
        for k in range(grad_m.shape[1] // wide):
            g_ref[half + HEAD * k : half + HEAD * (k + 1), :] = grad_m[:, wide * k : wide * (k + 1)]
    for b in range(blocks):
        slot = slot_ref[b]
        r = slice(TILE * b, TILE * (b + 1))

        @pl.when(slot < blocks // 2)
        def _(r=r, slot=slot):
            keep_ref[slot] = gj_ref[r, :]

        @pl.when(slot >= blocks // 2)
        def _(r=r, slot=slot):
            send_ref[slot - blocks // 2] = gj_ref[r, :]


def attend(slot, f, qk, vd, tables, first, back, h):
    rows = qk.shape[1]
    width = first.shape[1]
    packed = pl.BlockSpec((1, rows, 2 * HEAD), lambda *_: (h, 0, 0))
    g_rows = width // 2 + width // (3 * HEAD) * HEAD
    outs = [
        jax.ShapeDtypeStruct((rows // TILE // 2, TILE, 4 * HEAD), BF16),
        jax.ShapeDtypeStruct((rows // TILE // 2, TILE, 4 * HEAD), BF16),
        jax.ShapeDtypeStruct((g_rows, 3 * HEAD), BF16),
        jax.ShapeDtypeStruct((g_rows, 3 * HEAD), BF16),
    ]
    return pl.pallas_call(
        attend_kernel,
        grid_spec=pltpu.PrefetchScalarGridSpec(
            num_scalar_prefetch=2,
            grid=(1,),
            in_specs=[packed, packed]
            + [whole((rows, 2 * HEAD))] * 3
            + [whole(first.shape), whole(back.shape)],
            out_specs=[whole(v.shape) for v in outs],
            scratch_shapes=[
                pltpu.VMEM((2 * HEAD, rows), BF16),
                pltpu.VMEM((2 * HEAD, rows), BF16),
                pltpu.VMEM((rows, HEAD), BF16),
                pltpu.VMEM((rows, HEAD), BF16),
                pltpu.VMEM((rows, HEAD), BF16),
                pltpu.VMEM((rows, TILE), F32),
                pltpu.VMEM((HEAD, rows), F32),
                pltpu.VMEM((rows, HEAD), F32),
                pltpu.VMEM((rows, HEAD), F32),
                pltpu.VMEM((HEAD, rows), BF16),
                pltpu.VMEM((rows, 4 * HEAD), BF16),
                pltpu.VMEM((width, 3 * HEAD), BF16),
            ],
        ),
        out_shape=outs,
        compiler_params=params(),
        cost_estimate=beside(20 * rows * width),
        name="attend",
    )(slot, f, qk, vd, *tables, first, back)


def collect_kernel(f_ref, a_ref, b_ref, *refs, heads):
    (so0_ref, so1_ref, sums0_ref, vec_ref, own_ref, other_ref, wm_ref, wm_far_ref) = refs[:8]
    refs = refs[8:]
    packs, refs = refs[: 2 * len(heads)], refs[2 * len(heads) :]
    own_out, near_out, sums_ref, wt_ref = refs
    step = pl.program_id(0)
    first = heads[0] == 0
    wide = 3 * HEAD
    count = len(heads)
    all_heads = own_ref.shape[1] // wide // 2

    @pl.when(step == 0)
    def _():
        f, rows = f_ref[0], own_ref.shape[0]
        for k in range(2):
            for i, h in enumerate(heads):
                part = slice(wide * (all_heads * k + h), wide * (all_heads * k + h + 1))
                to = count * k + i
                wt_ref[to, pl.ds(pl.multiple_of(f * rows, rows), rows), :] = own_ref[:, part]
                wt_ref[to, pl.ds(pl.multiple_of((1 - f) * rows, rows), rows), :] = other_ref[:, part]
        sums_ref[...] = jnp.zeros_like(sums_ref) if first else sums0_ref[...]

    gain = vec_ref[0:1, :]
    n = normal(choose(step, (a_ref, b_ref), 0).astype(F32))
    merged = jnp.zeros(n.shape, F32)
    grad_first = jnp.zeros(n.shape, F32)
    for k, weights in enumerate((wm_ref, wm_far_ref)):
        for i, h in enumerate(heads):
            pack = packs[count * k + i]
            merged = merged + mm(pack[0, :, wide:], weights[HEAD * h : HEAD * (h + 1), :])
            gj = pack[0, :, :wide]
            row = 2 + all_heads * k + h
            sums_ref[row : row + 1, :wide] += colsum(gj.astype(F32))
            grad_first = grad_first + mm(gj, wt_ref[count * k + i], NT)
    u = grad_first * gain
    if not first:
        merged = merged + choose(step, (so0_ref, so1_ref), 0).astype(F32)
        u = u + choose(step, (so0_ref, so1_ref), 1).astype(F32)

    @pl.when(step < 2)
    def _():
        own_out[0], own_out[1] = merged.astype(BF16), u.astype(BF16)

    @pl.when(step >= 2)
    def _():
        near_out[0], near_out[1] = merged.astype(BF16), u.astype(BF16)

    sums_ref[0:1, :] += colsum(grad_first * n)
    sums_ref[1:2, :] += colsum(grad_first)


def collect(f, own_x, near_x, heads, packs, packs_far, vec, own, other, wm, wm_far, so_far=None):
    _, rows, width = own_x.shape
    pack = pl.BlockSpec((1, TILE, 4 * HEAD), lambda i, *_: (i, 0, 0))
    blocks = piece_specs(2, 2, width)
    so_far_specs = blocks
    if so_far is None:
        so_far = (jnp.zeros((8, 128), F32),) * 3
        so_far_specs = [whole((8, 128))] * 2
    return pl.pallas_call(
        functools.partial(collect_kernel, heads=heads),
        grid_spec=pltpu.PrefetchScalarGridSpec(
            num_scalar_prefetch=1,
            grid=(2 * rows // TILE,),
            in_specs=piece_specs(2, 1, width)
            + so_far_specs
            + [whole(v.shape) for v in (so_far[2], vec, own, other, wm, wm_far)]
            + [pack] * (2 * len(heads)),
            out_specs=blocks + [whole((8, width))],
            scratch_shapes=[pltpu.VMEM((2 * len(heads), width, 3 * HEAD), BF16)],
        ),
        out_shape=[
            jax.ShapeDtypeStruct((2, rows, width), BF16),
            jax.ShapeDtypeStruct((2, rows, width), BF16),
            jax.ShapeDtypeStruct((8, width), F32),
        ],
        compiler_params=params(),
        cost_estimate=beside(10 * rows * width),
        name="collect",
    )(f, own_x, near_x, *so_far, vec, own, other, wm, wm_far, *packs, *packs_far)


def slot_part(refs, slot, index):
    value = refs[0][index]
    for k in range(1, len(refs)):
        value = jnp.where(slot == k, refs[k][index], value)
    return value


def put_expand_kernel(c_ref, d_ref, *refs, shards):
    *ins, out = refs
    count, rows, columns = ins[0].shape
    cut = columns // shards
    k = (d_ref[0] - pl.program_id(0) + count) % count
    for b in range(CTX):
        slot = slot_of(c_ref[0] ^ b)
        value = slot_part(ins, slot, k).astype(F32)
        for g in range(shards):
            out[:, (g * CTX + b) * cut : (g * CTX + b + 1) * cut] = value[:, g * cut : (g + 1) * cut]


def put_expand(c, d, parts, shards):
    count, rows, columns = parts[0].shape
    return pl.pallas_call(
        functools.partial(put_expand_kernel, shards=shards),
        grid_spec=pltpu.PrefetchScalarGridSpec(
            num_scalar_prefetch=2,
            grid=(count // 2,),
            in_specs=[whole(parts[0].shape)] * CTX,
            out_specs=pl.BlockSpec((rows, CTX * columns), lambda a, *_: (a, 0)),
        ),
        out_shape=jax.ShapeDtypeStruct((count // 2 * rows, CTX * columns), F32),
        compiler_params=params(),
        cost_estimate=beside(50 * rows * columns),
        name="put_expand",
    )(c, d, *parts)


def put_reduce_kernel(c_ref, d_ref, *refs):
    *ins, out = refs
    count, rows, columns = ins[0].shape
    slot = slot_of(c_ref[0] ^ pl.program_id(0))
    for a in range(count // 2):
        k = (d_ref[0] - a - count // 2 + count) % count
        out[rows * a : rows * (a + 1), :] = slot_part(ins, slot, k).astype(F32)


def put_reduce(c, d, parts):
    count, rows, columns = parts[0].shape
    own = count // 2 * rows
    return pl.pallas_call(
        put_reduce_kernel,
        grid_spec=pltpu.PrefetchScalarGridSpec(
            num_scalar_prefetch=2,
            grid=(CTX,),
            in_specs=[whole(parts[0].shape)] * CTX,
            out_specs=pl.BlockSpec((own, columns), lambda b, *_: (b, 0)),
        ),
        out_shape=jax.ShapeDtypeStruct((CTX * own, columns), F32),
        compiler_params=params(),
        cost_estimate=beside(50 * rows * columns),
        name="put_reduce",
    )(c, d, *parts)


def put_heads_kernel(c_ref, d_ref, f_ref, *refs, top, with_merge):
    two, one = refs[:CTX], refs[CTX : 2 * CTX]
    outs = refs[2 * CTX : 2 * CTX + 1 + with_merge]
    s2, s1 = refs[2 * CTX + 1 + with_merge :]
    count, rows, wide = one[0].shape
    for b in range(CTX):
        slot = slot_of(c_ref[0] ^ b)
        for a in range(count):
            k = (d_ref[0] - a + count) % count
            s2[rows * a : rows * (a + 1), :] = slot_part(two, slot, k)
            s1[rows * a : rows * (a + 1), :] = slot_part(one, slot, k)
        at = 3 * wide * b
        outs[0][:, at : at + 2 * wide] = s2[:top, :].astype(F32)
        outs[0][:, at + 2 * wide : at + 3 * wide] = s1[:top, :].astype(F32)
        if with_merge:
            per = (count * rows - top) // HEAD

            @pl.when(b // (CTX // 2) == f_ref[0])
            def _(b=b):
                for h in range(3):
                    row = 3 * HEAD * (b % (CTX // 2)) + HEAD * h
                    for k in range(per):
                        src = slice(top + HEAD * k, top + HEAD * (k + 1))
                        part = s1[src, :] if h == 2 else s2[src, wide * h : wide * (h + 1)]
                        outs[1][row : row + HEAD, wide * k : wide * (k + 1)] = part.astype(F32)


def put_heads(c, d, f, two, one, top, width, with_merge):
    count, rows, wide = one[0].shape
    shapes = [jax.ShapeDtypeStruct((top, 3 * CTX * wide), F32)]
    if with_merge:
        shapes.append(jax.ShapeDtypeStruct((width // 2, width), F32))
    return pl.pallas_call(
        functools.partial(put_heads_kernel, top=top, with_merge=with_merge),
        grid_spec=pltpu.PrefetchScalarGridSpec(
            num_scalar_prefetch=3,
            grid=(1,),
            in_specs=[whole(v.shape) for v in (*two, *one)],
            out_specs=[whole(v.shape) for v in shapes],
            scratch_shapes=[
                pltpu.VMEM((count * rows, 2 * wide), BF16), pltpu.VMEM((count * rows, wide), BF16)
            ],
        ),
        out_shape=shapes,
        compiler_params=params(),
        cost_estimate=short(),
        name="put_heads",
    )(c, d, f, *two, *one)


def rotary(rows):
    lane = jnp.arange(2 * HEAD, dtype=jnp.int32)[None, :] % HEAD
    half = ROT // 2
    inverse = 10000.0 ** (-2.0 * (lane % half).astype(F32) / ROT)
    angles = jnp.arange(rows, dtype=jnp.int32).astype(F32)[:, None] * inverse
    cos = jnp.where(lane < ROT, jnp.cos(angles), 1.0)
    sine = jnp.sin(angles)
    low = jnp.where(lane < half, -sine, 0.0)
    high = jnp.where((lane >= half) & (lane < ROT), sine, 0.0)
    return cos, low, high


def local(
    tokens, cotangent, block_order, first_gain, first_shift, second_gain, second_shift,
    triple_weight, triple_bias, merge_weight, merge_bias, expand_weight, expand_bias,
    reduce_weight, reduce_bias,
):
    c, d, f = lax.axis_index("ctx"), lax.axis_index("dp"), lax.axis_index("fsdp")
    shards = lax.axis_size("fsdp")
    own_len, width = tokens.shape[1:]
    inner = expand_weight.shape[1]
    own_inner = inner // shards // CTX
    ctx_inner = inner // CTX
    own_heads = HEADS // CTX
    own_cols = own_heads * 3 * HEAD
    own_merge = own_heads * HEAD
    half = CTX // 2

    own_expand = jnp.concatenate(
        [
            lax.dynamic_slice_in_dim(expand_weight, g * CTX * own_inner + c * own_inner, own_inner, 1)
            for g in range(shards)
        ],
        axis=1,
    )
    own_reduce = lax.dynamic_slice_in_dim(reduce_weight, c * own_inner, own_inner, 0)
    own_bias = lax.dynamic_slice_in_dim(expand_bias, c * own_inner, own_inner, 0)
    own_triple = jnp.concatenate(
        [lax.dynamic_slice_in_dim(triple_weight, k * own_cols, own_cols, 1) for k in (c, c ^ 2)], axis=1
    )
    smalls = jnp.stack(
        [first_gain, first_shift, second_gain, second_shift, own_bias, merge_bias, reduce_bias]
    )
    if shards == 2:
        own_tb = lax.dynamic_slice_in_dim(triple_bias, (c % half) * own_cols, own_cols, 0)
        rows = jnp.concatenate(
            [
                jnp.pad(smalls, ((0, 1), (0, width - smalls.shape[1]))),
                jnp.pad(own_tb[None], ((0, 7), (0, width - own_cols))),
            ]
        )
        w_own = jnp.concatenate([own_expand, own_reduce, rows])
        w_other = swap(w_own, "fsdp", 1)
        last = width // 2 + ctx_inner // 2
        own_s, other_s = w_own[last:], w_other[last:]
        cut = smalls.shape[1]
        vec = jnp.where(
            f == 0,
            jnp.concatenate([own_s[:8, :cut], other_s[:8, :cut]], axis=1),
            jnp.concatenate([other_s[:8, :cut], own_s[:8, :cut]], axis=1),
        ).astype(F32)
        tb = jnp.where(f == c // half, own_s[8, :own_cols], other_s[8, :own_cols]).astype(F32)
        t_own = own_triple
        m_own = lax.dynamic_slice_in_dim(merge_weight, (c % half) * own_merge, own_merge, 0)
        side = f
    else:
        def full(v):
            return lax.all_gather(v, "fsdp", axis=0, tiled=True)

        we, wr, wt = full(own_expand), full(own_reduce), full(own_triple)
        w_own = jnp.concatenate([we[: width // 2], wr[: ctx_inner // 2]])
        w_other = jnp.concatenate([we[width // 2 :], wr[ctx_inner // 2 :]])
        t_own, t_other = wt[: width // 2], wt[width // 2 :]
        vec = lax.all_gather(smalls, "fsdp", axis=1, tiled=True).astype(F32)
        vec = jnp.pad(vec, ((0, 1), (0, 0)))
        tb = lax.dynamic_slice_in_dim(full(triple_bias), c * own_cols, own_cols, 0).astype(F32)
        m_own = full(merge_weight)
        side = jnp.int32(0)
    tb = tb.reshape(own_heads, 1, 3 * HEAD)
    flag = side.astype(jnp.int32).reshape(1)

    own = jnp.stack([tokens.reshape(own_len, width), cotangent.reshape(own_len, width)])
    far = swap(own, "ctx", 2)
    near = swap(own, "ctx", 1)
    pos = jnp.concatenate(
        [lax.dynamic_slice_in_dim(block_order, 2 * (c ^ r), 2) for r in range(CTX)]
    )
    blocks = jnp.arange(pos.shape[0], dtype=jnp.int32)
    slot = jnp.sum(jnp.where(pos[None, :] == blocks[:, None], blocks[None, :], 0), axis=1)
    slot = slot.astype(jnp.int32)
    tables = rotary(CTX * own_len)
    far, t_own, m_own, w_other, *tables = lax.optimization_barrier(
        (far, t_own, m_own, w_other, *tables)
    )
    both = swap(far, "ctx", 1)
    if shards == 2:
        t_other, m_other = swap(t_own, "fsdp", 1), swap(m_own, "fsdp", 1)
    else:
        m_own, m_other = (
            lax.dynamic_slice_in_dim(m_own, k * own_merge, own_merge, 0) for k in (c, c ^ 2)
        )

    lu_keep, lu_send, *g_feed, sums2 = feed(
        flag, own, far, near, both, vec, w_own, w_other, width, ctx_inner
    )
    way_f = Summed(split_feed(g_feed, shards, width), f, d)
    lu_send, pos, t_other, m_other = boundary([way_f], lu_send, pos, t_other, m_other)
    if shards == 2:
        wm = jnp.where(f == c // half, m_own, m_other)
        wm_far = jnp.where(f == c // half, m_other, m_own)
    else:
        wm, wm_far = m_own, m_other
    lu_in = swap(lu_send, "ctx", 1)
    last = pos.shape[0] // 2
    qk, vd, first, back = project(
        pos[:last], flag, (own, near), vec, tb, t_own, t_other, wm, tables
    )
    lu_far = add_low(lu_keep[1], lu_in[1])
    qk, lu_far = lax.optimization_barrier((qk, lu_far))
    lu_far = swap(lu_far, "ctx", 2)
    qk, vd, first, back = project(
        pos[last:], flag, (far, both), vec, tb, t_own, t_other, wm, tables, (qk, vd, first, back)
    )
    (qk,) = boundary([way_f], qk)
    packs, packs_far, gs = [], [], []

    def next_head(qk, h):
        pack, sent, *g = attend(slot, flag, qk, vd, tables, first, back, h)
        packs.append(pack)
        gs.append(g)
        return sent

    sent = next_head(qk, 0)
    qk, sent, lu_far = boundary([way_f], qk, sent, lu_far)
    packs_far.append(swap(sent, "ctx", 2))
    sent = next_head(qk, 1)
    g_two = [jnp.concatenate(g, axis=1) for g in zip(*gs)]
    way_two = Summed(split_rows(g_two, shards, width), f, d)
    qk, sent_two, packs_far[0] = boundary([way_two, way_f], qk, sent, packs_far[0])
    sent_one = next_head(qk, 2)
    way_one = Summed(split_rows(gs[-1], shards, width), f, d)
    ways = [way_one, way_two]
    c1, d1, f1 = (v.astype(jnp.int32).reshape(1) for v in (c, d, f))
    c1, sent_two, sent_one = boundary([way_one, way_f], c1, sent_two, sent_one, hold=[way_two])
    packs_far.append(swap(sent_two, "ctx", 2))
    feed_parts = way_f.finish()
    c1, feed_parts = boundary([way_two], c1, feed_parts)
    grad_expand = put_expand(c1, d1, feed_parts, shards)
    grad_reduce = put_reduce(c1, d1, feed_parts)
    flag1, grad_expand, grad_reduce, sent_one, packs_far[1] = boundary(
        [way_one], flag, grad_expand, grad_reduce, sent_one, packs_far[1], hold=[way_two]
    )
    packs_far.append(swap(sent_one, "ctx", 2))
    so_far = collect(
        flag1, own, near, (0, 1), packs[:2], packs_far[:2], vec, t_own, t_other, wm, wm_far
    )
    flag1, packs_far[2], so_far = boundary(ways, flag, packs_far[2], so_far)
    mu, mu_near, sums1 = collect(
        flag1, own, near, (2,), packs[2:], packs_far[2:], vec, t_own, t_other, wm, wm_far, so_far
    )

    tb_rows = sums1[2 : 2 + 2 * own_heads, : 3 * HEAD].reshape(2, own_cols)
    tb_rows = jnp.pad(tb_rows, ((0, 0), (0, width - own_cols)))
    eb_row = jnp.pad(sums2[2:3], ((0, 0), (0, width - ctx_inner)))
    mine = (jnp.arange(CTX) == c)[:, None]
    across = (jnp.arange(CTX) == (c ^ 2))[:, None]
    tb_block = jnp.where(mine, tb_rows[:1], jnp.where(across, tb_rows[1:], 0.0))
    vector = jnp.concatenate(
        [sums1[:2], sums2[:2], sums2[3:4], tb_block, jnp.where(mine, eb_row, 0.0)]
    )
    vector = jnp.pad(vector, ((0, 3), (0, 0)))

    c1, mu_near, vector = boundary(ways, c1, mu_near, vector)
    mu_in = swap(mu_near, "ctx", 1)
    if shards == 2:
        vector = vector + swap(vector, "fsdp", 1)
    else:
        vector = lax.psum(vector, "fsdp")
    mu_in, vector = lax.optimization_barrier((mu_in, vector))
    vector = vector + swap(vector, "dp", 1)
    lu = lu_keep[0].astype(F32) + lu_in[0].astype(F32) + lu_far.astype(F32)
    mixed, u = lu + mu.astype(F32) + mu_in.astype(F32)

    x_f = own[0].astype(F32)
    mixed = (x_f + mixed + (vec[5] + vec[6])[None, :]).astype(BF16)
    average = jnp.mean(x_f, axis=-1, keepdims=True)
    centred = x_f - average
    r = lax.rsqrt(jnp.mean(centred * centred, axis=-1, keepdims=True) + epsilon)
    n = centred * r
    input_grad = own[1].astype(F32) + r * (
        u - jnp.mean(u, axis=-1, keepdims=True) - n * jnp.mean(u * n, axis=-1, keepdims=True)
    )

    vector, mixed, input_grad = lax.optimization_barrier((vector, mixed, input_grad))
    vector = vector + swap(vector, "dp", 2)
    vector = vector + swap(vector, "ctx", 1)
    (vector,) = boundary(ways, vector)
    vector = vector + swap(vector, "ctx", 2)
    part = width // shards
    five = lax.dynamic_slice_in_dim(vector[:5], f * part, part, 1)
    d_g1, d_s1, d_g2, d_s2, d_cot = [five[i] for i in range(5)]
    d_tb = vector[5 : 5 + CTX, :own_cols].reshape(-1)
    d_tb = lax.dynamic_slice_in_dim(d_tb, f * (3 * part), 3 * part, 0)
    d_eb = lax.dynamic_slice_in_dim(vector[5 + CTX : 5 + 2 * CTX], f * own_inner, own_inner, 1)
    d_eb = d_eb.reshape(-1)

    two, one = way_two.finish(), way_one.finish()
    two, vector = lax.optimization_barrier((two, vector))
    placed = put_heads(c1, d1, f1, two, one, part, width, shards == 2)
    grad_triple = placed[0]
    if shards == 2:
        grad_merge = placed[1]
    else:
        count = lax.axis_size("dp")
        g_all = [
            jnp.concatenate([pick(g, (d - a) % count) for a in range(count)])
            for g in in_order([jnp.concatenate([a, b], axis=2) for a, b in zip(two, one)], c)
        ]
        wide = 3 * HEAD
        grad_merge = jnp.concatenate(
            [
                g[part:].reshape(width // wide, HEAD, own_heads, wide).transpose(2, 1, 0, 3)
                .reshape(own_merge, width) for g in g_all
            ]
        )
        grad_merge = lax.dynamic_slice_in_dim(grad_merge, f * part, part, 0).astype(F32)
    return (
        mixed[None],
        input_grad[None],
        d_g1,
        d_s1,
        d_g2,
        d_s2,
        grad_triple,
        d_tb,
        grad_merge,
        d_cot,
        grad_expand,
        d_eb,
        grad_reduce,
        d_cot,
    )


def split_feed(g, shards, width):
    if shards == 2:
        return tuple(g)
    g = jnp.stack(g)
    half = width // 2
    ge, gr = g[:, :half].reshape(width, -1), g[:, half:].reshape(-1, width)
    parts = [v.reshape(shards, v.shape[0] // shards, v.shape[1]) for v in (ge, gr)]
    return jnp.concatenate(parts, axis=1)


def split_rows(g, shards, width):
    if shards == 2:
        return tuple(g)
    g = jnp.stack(g)
    rows = g[:, : width // 2].reshape(shards, width // shards, g.shape[2])
    tail = jnp.broadcast_to(g[:1, width // 2 :], (shards,) + g[0, width // 2 :].shape)
    return jnp.concatenate([rows, tail], axis=1)


def solution(mesh):
    tokens = P(("dp", "fsdp"), "ctx", None)
    row, vector = P("fsdp", None), P("fsdp")
    weights = (row, vector, row, vector, row, vector, row, vector)
    in_specs = (tokens, tokens, P()) + (vector,) * 4 + weights
    out_specs = (tokens, tokens) + (vector,) * 4 + weights
    return jax.shard_map(local, mesh=mesh, in_specs=in_specs, out_specs=out_specs, check_vma=False)
```

```python
import functools
import math

import jax
import jax.numpy as jnp
from jax import lax
from jax.experimental import pallas as pl
from jax.experimental.pallas import tpu as pltpu
from jax.sharding import PartitionSpec as P

HEADS = 12
HEAD = 64
ROT = 16
TILE = 256
CTX = 4
epsilon = 1e-05
masked_value = -1e30
F32 = jnp.float32
BF16 = jnp.bfloat16
VMEM_LIMIT = 58 * 1024 * 1024

NN = (((1,), (0,)), ((), ()))
NT = (((1,), (1,)), ((), ()))
TN = (((0,), (0,)), ((), ()))


def mm(a, b, dims=NN):
    return lax.dot_general(a, b, dims, preferred_element_type=F32)


def swap(value, axis, bit):
    count = lax.axis_size(axis)
    return lax.ppermute(value, axis, [(i, i ^ bit) for i in range(count)])


def pick(stacked, index):
    return lax.dynamic_index_in_dim(stacked, index, 0, keepdims=False)


def add_low(a, b):
    return (a.astype(F32) + b.astype(F32)).astype(BF16)


def after(value, *others):
    return lax.optimization_barrier((value,) + others)[0]


def slot_of(relative):
    return (relative % 2) * 2 + relative // 2


def in_order(both, c):
    both = jnp.stack(both)
    return [pick(both, slot_of(c ^ b)) for b in range(CTX)]


class Summed:
    def __init__(self, value, f, d):
        self.value, self.f, self.d = value, f, d
        self.steps = ["fsdp", "dp_down", "dp_up", "far", "near"]
        self.moving = None

    def send(self):
        kind, value = self.steps[0], self.value
        count = lax.axis_size("dp")
        if kind == "fsdp":
            self.moving = [value[1]] if isinstance(value, tuple) else []
        elif kind == "dp_down":
            self.value = value.reshape(count, value.shape[0] // count, value.shape[1])
            self.moving = [pick(self.value, (self.d + k) % count) for k in range(1, count)]
        elif kind == "near":
            self.moving = [value[1]]
        else:
            self.moving = [value]
        return self.moving

    def receive(self):
        kind, moving = self.steps[0], self.moving
        count = lax.axis_size("dp")
        turns = [[(i, (i + k) % count) for i in range(count)] for k in range(1, count)]
        if kind == "fsdp":
            return [swap(v, "fsdp", 1) for v in moving]
        if kind == "dp_down":
            return [lax.ppermute(v, "dp", t) for v, t in zip(moving, turns)]
        if kind == "dp_up":
            return [lax.ppermute(moving[0], "dp", t) for t in turns]
        if kind == "far":
            return [swap(moving[0], "ctx", 2), swap(moving[0], "ctx", 1)]
        return [swap(moving[0], "ctx", 1)]

    def take(self, came):
        kind = self.steps.pop(0)
        if kind == "fsdp":
            if came:
                self.value = add_low(self.value[0], came[0])
            else:
                self.value = lax.psum_scatter(self.value, "fsdp", scatter_dimension=0, tiled=False)
        elif kind == "dp_down":
            total = pick(self.value, self.d).astype(F32)
            for v in came:
                total = total + v.astype(F32)
            self.value = total.astype(BF16)
        elif kind == "dp_up":
            self.value = jnp.stack([self.moving[0]] + came)
        elif kind == "far":
            self.value = [self.moving[0]] + came
        else:
            self.value = self.value + came
        self.moving = None

    def beside(self, other):
        self.value = jnp.concatenate([self.value, other.value], axis=1)
        return self

    def finish(self):
        while self.steps:
            if self.moving is None:
                self.send()
            self.take(self.receive())
        return self.value


def boundary(ways, *values, hold=()):
    moved = [way for way in (*ways, *hold) if way.moving is not None]
    came, values = lax.optimization_barrier(([way.receive() for way in moved], values))
    for way, v in zip(moved, came):
        way.take(v)
    for way in ways:
        way.moving = way.send() if way.steps else None
    for way in hold:
        way.value, values = lax.optimization_barrier((way.value, values))
    sent = [tuple(way.moving or ()) for way in ways]
    sent, values = lax.optimization_barrier((sent, values))
    for way, moving in zip(ways, sent):
        if way.moving is not None:
            way.moving = list(moving)
    return values


def normal(x):
    average = jnp.mean(x, axis=-1, keepdims=True)
    centred = x - average
    spread = jnp.mean(centred * centred, axis=-1, keepdims=True)
    return centred * lax.rsqrt(spread + epsilon)


def colsum(v):
    return jnp.sum(v, axis=0, keepdims=True)


def whole(shape):
    return pl.BlockSpec(shape, lambda *_: (0,) * len(shape))


def params(**more):
    return pltpu.CompilerParams(
        dimension_semantics=("arbitrary",), vmem_limit_bytes=VMEM_LIMIT, **more
    )


def cost(flops, moved, exps=0):
    return pl.CostEstimate(flops=flops, bytes_accessed=moved, transcendentals=exps)


def beside(moved):
    return cost(0, 100 * moved)


def short():
    return cost(0, 0)


def place(f, own, other, out):
    rows = own.shape[0]
    out[pl.ds(pl.multiple_of(f * rows, rows), rows), :] = own
    out[pl.ds(pl.multiple_of((1 - f) * rows, rows), rows), :] = other


def feed_kernel(
    f_ref, a_ref, b_ref, c_ref, d_ref, vec_ref, own_ref, other_ref,
    keep_ref, send_ref, g_keep_ref, g_send_ref, sums_ref, we_ref, wr_ref, ge_acc, gr_acc,
):
    step = pl.program_id(0)
    half = we_ref.shape[0] // 2

    @pl.when(step == 0)
    def _():
        f = f_ref[0]
        place(f, own_ref[:half], other_ref[:half], we_ref)
        place(f, own_ref[half : 2 * half], other_ref[half : 2 * half], wr_ref)
        ge_acc[...] = jnp.zeros_like(ge_acc)
        gr_acc[...] = jnp.zeros_like(gr_acc)
        sums_ref[...] = jnp.zeros_like(sums_ref)
        sums_ref[3:4, :] = colsum(a_ref[1].astype(F32))

    def piece(k):
        first = jnp.where(step == 0, a_ref[k], b_ref[k])
        return jnp.where(step < 2, first, jnp.where(step == 2, c_ref[k], d_ref[k]))

    gain, shift, bias = vec_ref[2:3, :], vec_ref[3:4, :], vec_ref[4:5, :]
    n = normal(piece(0).astype(F32))
    second = (n * gain + shift).astype(BF16)
    back = piece(1)
    hidden = mm(second, we_ref[...]) + bias
    cdf = 0.5 * (1.0 + lax.erf(hidden * (1.0 / math.sqrt(2.0))))
    active = (hidden * cdf).astype(BF16)
    low = mm(active, wr_ref[...]).astype(BF16)
    slope = cdf + hidden * (jnp.exp(-0.5 * hidden * hidden) * (1.0 / math.sqrt(2.0 * math.pi)))
    grad_hidden = (mm(back, wr_ref[...], NT) * slope).astype(BF16)
    gr_acc[...] += mm(active, back, TN)
    ge_acc[...] += mm(second, grad_hidden, TN)
    grad_second = mm(grad_hidden, we_ref[...], NT)
    u = (grad_second * gain).astype(BF16)
    sums_ref[0:1, :] += colsum(grad_second * n)
    sums_ref[1:2, :] += colsum(grad_second)
    sums_ref[2:3, :] += colsum(grad_hidden.astype(F32))

    @pl.when(step < 2)
    def _():
        keep_ref[0, 0], keep_ref[0, 1] = low, u

    @pl.when(step >= 2)
    def _():
        send_ref[0, 0], send_ref[0, 1] = low, u

    @pl.when(step == pl.num_programs(0) - 1)
    def _():
        for s, g_ref in ((f_ref[0], g_keep_ref), (1 - f_ref[0], g_send_ref)):
            rows = pl.ds(pl.multiple_of(s * half, half), half)
            g_ref[:half] = ge_acc[rows, :].astype(BF16)
            g_ref[half:] = gr_acc[rows, :].astype(BF16)


def feed(f, own_x, far, near, both, vec, own, other, width, inner):
    rows = own_x.shape[1]
    shape_e, shape_r = (width, inner), (inner, width)
    outs = [
        jax.ShapeDtypeStruct((2, 2, rows, width), BF16),
        jax.ShapeDtypeStruct((2, 2, rows, width), BF16),
        jax.ShapeDtypeStruct(((width + inner) // 2, width), BF16),
        jax.ShapeDtypeStruct(((width + inner) // 2, width), BF16),
        jax.ShapeDtypeStruct((8, width), F32),
    ]
    args = (own_x, far, near, both, vec, own, other)
    block = (1, 2, rows, width)
    return pl.pallas_call(
        feed_kernel,
        grid_spec=pltpu.PrefetchScalarGridSpec(
            num_scalar_prefetch=1,
            grid=(CTX,),
            in_specs=[whole(v.shape) for v in args],
            out_specs=[
                pl.BlockSpec(block, lambda i, *_: (jnp.minimum(i, 1), 0, 0, 0)),
                pl.BlockSpec(block, lambda i, *_: (jnp.maximum(i - 2, 0), 0, 0, 0)),
            ]
            + [whole(v.shape) for v in outs[2:]],
            scratch_shapes=[
                pltpu.VMEM(shape_e, BF16), pltpu.VMEM(shape_r, BF16),
                pltpu.VMEM(shape_e, F32), pltpu.VMEM(shape_r, F32),
            ],
        ),
        out_shape=outs,
        compiler_params=params(),
        cost_estimate=beside(16 * rows * width),
        name="feed",
    )(f, *args)


def turn(u, cos, sin_a, sin_b):
    return u * cos + pltpu.roll(u, 120, 1) * sin_a + pltpu.roll(u, 8, 1) * sin_b


def place_heads(f, own, other, out):
    rows = own.shape[0]
    wide = out.shape[2]
    for h in range(out.shape[0]):
        part = slice(wide * h, wide * (h + 1))
        out[h, pl.ds(pl.multiple_of(f * rows, rows), rows), :] = own[:, part]
        out[h, pl.ds(pl.multiple_of((1 - f) * rows, rows), rows), :] = other[:, part]


def choose(step, refs, index):
    value = refs[-1][index]
    for k in range(len(refs) - 2, -1, -1):
        value = jnp.where(step < 2 * k + 2, refs[k][index], value)
    return value


def piece_specs(count, lead, width, first=0):
    return [
        pl.BlockSpec(
            (lead, TILE, width), lambda i, *_, k=k: (first, jnp.clip(i - 2 * k, 0, 1), 0)
        )
        for k in range(count)
    ]


def project_kernel(pos_ref, f_ref, a_ref, b_ref, vec_ref, tb_ref, own_ref, other_ref, wm_ref,
    cos_ref, sa_ref, sb_ref, *refs):
    qk_ref, vd_ref, first_ref, back_ref, wt_ref = refs[-5:]
    step = pl.program_id(0)

    @pl.when(step == 0)
    def _():
        place_heads(f_ref[0], own_ref[...], other_ref[...], wt_ref)

    pieces = (a_ref, b_ref)
    x = choose(step, pieces, 0)
    back = choose(step, pieces, 1)
    first = (normal(x.astype(F32)) * vec_ref[0:1, :] + vec_ref[1:2, :]).astype(BF16)
    first_ref[...] = first
    back_ref[...] = back
    grad_out = mm(back, wm_ref[...], NT)
    heads = wt_ref.shape[0]
    lane = lax.broadcasted_iota(jnp.int32, (TILE, 2 * HEAD), 1)
    scale = jnp.where(lane < HEAD, 1.0 / math.sqrt(HEAD), 1.0)
    for h in range(heads):
        joined = mm(first, wt_ref[h]) + tb_ref[h]
        turned = turn(joined[:, : 2 * HEAD], cos_ref[...], sa_ref[...], sb_ref[...])
        qk_ref[h] = (turned * scale).astype(BF16)
        vd_ref[h, :, :HEAD] = joined[:, 2 * HEAD :].astype(BF16)
        vd_ref[h, :, HEAD:] = grad_out[:, HEAD * h : HEAD * (h + 1)].astype(BF16)


def project(pos, f, pieces, vec, tb, own, other, wm, tables, so_far=()):
    width = pieces[0].shape[2]
    rows = CTX * pieces[0].shape[1]
    heads = tb.shape[0]
    table = pl.BlockSpec((TILE, 2 * HEAD), lambda i, p, f: (p[i], 0))
    out = pl.BlockSpec((heads, TILE, 2 * HEAD), lambda i, p, f: (0, p[i], 0))
    row = pl.BlockSpec((TILE, width), lambda i, p, f: (p[i], 0))
    args = (pos, f, *pieces, vec, tb, own, other, wm, *tables)
    return pl.pallas_call(
        project_kernel,
        grid_spec=pltpu.PrefetchScalarGridSpec(
            num_scalar_prefetch=2,
            grid=(rows // TILE // 2,),
            in_specs=piece_specs(2, 2, width)
            + [whole(v.shape) for v in (vec, tb, own, other, wm)]
            + [table] * 3
            + [pl.BlockSpec(memory_space=pl.ANY)] * len(so_far),
            out_specs=[out, out, row, row],
            scratch_shapes=[pltpu.VMEM((heads, width, 3 * HEAD), BF16)],
        ),
        out_shape=[jax.ShapeDtypeStruct((heads, rows, 2 * HEAD), BF16)] * 2
        + [jax.ShapeDtypeStruct((rows, width), BF16)] * 2,
        input_output_aliases={len(args) + k: k for k in range(len(so_far))},
        compiler_params=params(),
        cost_estimate=beside(10 * rows * width),
        name="project",
    )(*args, *so_far)


def attend_kernel(
    slot_ref, f_ref, qk_ref, vd_ref, cos_ref, sa_ref, sb_ref, first_ref, back_ref, keep_ref, send_ref, g_keep_ref, g_send_ref,
    qt, vt, ks, vs, ds_, s_ref, gq, gk, gv, att_ref, gj_ref, grad_t,
):
    rows = qk_ref.shape[1]
    blocks = rows // TILE

    for b in range(blocks):
        r = slice(TILE * b, TILE * (b + 1))
        qt[:, r] = qk_ref[0, r, :].T
        vt[:, r] = vd_ref[0, r, :].T
        ks[r, :] = qk_ref[0, r, HEAD:]
        vs[r, :] = vd_ref[0, r, :HEAD]
        ds_[r, :] = vd_ref[0, r, HEAD:]
    key_id = lax.broadcasted_iota(jnp.int32, (TILE, TILE), 0)
    query_id = lax.broadcasted_iota(jnp.int32, (TILE, TILE), 1)
    keep = key_id <= query_id
    def put_scores(i, j, peak):
        kr = slice(TILE * j, TILE * (j + 1))
        s = mm(ks[kr, :], qt[:HEAD, TILE * i : TILE * (i + 1)])
        if j == i:
            s = jnp.where(keep, s, masked_value)
        s_ref[i % 2, kr, :] = s
        top = jnp.max(s, axis=0, keepdims=True)
        return top if peak is None else jnp.maximum(peak, top)

    next_peak = put_scores(0, 0, None)
    for i in range(blocks):
        qr = slice(TILE * i, TILE * (i + 1))
        peak, next_peak = next_peak, None
        total = jnp.zeros((1, TILE), F32)
        out = jnp.zeros((HEAD, TILE), F32)
        for j in range(i + 1):
            kr = slice(TILE * j, TILE * (j + 1))
            e = jnp.exp(s_ref[i % 2, kr, :] - peak)
            if i + 1 < blocks:
                next_peak = put_scores(i + 1, j, next_peak)
            s_ref[i % 2, kr, :] = e
            total = total + jnp.sum(e, axis=0, keepdims=True)
            out = out + mm(vt[:HEAD, kr], e.astype(BF16))
        if i + 1 < blocks:
            next_peak = put_scores(i + 1, i + 1, next_peak)
        inv = 1.0 / total
        out = out * inv
        att_ref[:, qr] = out.astype(BF16)
        gj_ref[qr, 3 * HEAD :] = out.T.astype(BF16)
        d_t = vt[HEAD:, qr]
        delta = jnp.sum(d_t.astype(F32) * out, axis=0, keepdims=True)
        q = qk_ref[0, qr, :HEAD]
        d = ds_[qr, :]
        grad_q = jnp.zeros((HEAD, TILE), F32)
        for j in range(i + 1):
            kr = slice(TILE * j, TILE * (j + 1))
            p = s_ref[i % 2, kr, :] * inv
            g = (p * (mm(vs[kr, :], d_t) - delta)).astype(BF16)
            grad_v = mm(p.astype(BF16), d)
            grad_k = mm(g, q)
            grad_q = grad_q + mm(qt[HEAD:, kr], g)
            if j == i:
                gv[kr, :] = grad_v
                gk[kr, :] = grad_k
            else:
                gv[kr, :] += grad_v
                gk[kr, :] += grad_k
        gq[:, qr] = grad_q * (1.0 / math.sqrt(HEAD))
    for b in range(blocks):
        r = slice(TILE * b, TILE * (b + 1))
        both = jnp.concatenate([gq[:, r].T, gk[r, :]], axis=1)
        gj_ref[r, : 2 * HEAD] = turn(both, cos_ref[r, :], -sa_ref[r, :], -sb_ref[r, :]).astype(BF16)
        gj_ref[r, 2 * HEAD : 3 * HEAD] = gv[r, :].astype(BF16)
    grad_t[...] = mm(first_ref[...], gj_ref[:, : 3 * HEAD], TN).astype(BF16)
    grad_m = mm(att_ref[...], back_ref[...]).astype(BF16)
    wide = 3 * HEAD
    half = grad_t.shape[0] // 2
    for s, g_ref in ((f_ref[0], g_keep_ref), (1 - f_ref[0], g_send_ref)):
        g_ref[:half, :] = grad_t[pl.ds(pl.multiple_of(s * half, half), half), :]
        for k in range(grad_m.shape[1] // wide):
            g_ref[half + HEAD * k : half + HEAD * (k + 1), :] = grad_m[:, wide * k : wide * (k + 1)]
    for b in range(blocks):
        slot = slot_ref[b]
        r = slice(TILE * b, TILE * (b + 1))

        @pl.when(slot < blocks // 2)
        def _(r=r, slot=slot):
            keep_ref[slot] = gj_ref[r, :]

        @pl.when(slot >= blocks // 2)
        def _(r=r, slot=slot):
            send_ref[slot - blocks // 2] = gj_ref[r, :]


def attend(slot, f, qk, vd, tables, first, back, h):
    rows = qk.shape[1]
    width = first.shape[1]
    packed = pl.BlockSpec((1, rows, 2 * HEAD), lambda *_: (h, 0, 0))
    g_rows = width // 2 + width // (3 * HEAD) * HEAD
    outs = [
        jax.ShapeDtypeStruct((rows // TILE // 2, TILE, 4 * HEAD), BF16),
        jax.ShapeDtypeStruct((rows // TILE // 2, TILE, 4 * HEAD), BF16),
        jax.ShapeDtypeStruct((g_rows, 3 * HEAD), BF16),
        jax.ShapeDtypeStruct((g_rows, 3 * HEAD), BF16),
    ]
    return pl.pallas_call(
        attend_kernel,
        grid_spec=pltpu.PrefetchScalarGridSpec(
            num_scalar_prefetch=2,
            grid=(1,),
            in_specs=[packed, packed]
            + [whole((rows, 2 * HEAD))] * 3
            + [whole(first.shape), whole(back.shape)],
            out_specs=[whole(v.shape) for v in outs],
            scratch_shapes=[
                pltpu.VMEM((2 * HEAD, rows), BF16),
                pltpu.VMEM((2 * HEAD, rows), BF16),
                pltpu.VMEM((rows, HEAD), BF16),
                pltpu.VMEM((rows, HEAD), BF16),
                pltpu.VMEM((rows, HEAD), BF16),
                pltpu.VMEM((2, rows, TILE), F32),
                pltpu.VMEM((HEAD, rows), F32),
                pltpu.VMEM((rows, HEAD), F32),
                pltpu.VMEM((rows, HEAD), F32),
                pltpu.VMEM((HEAD, rows), BF16),
                pltpu.VMEM((rows, 4 * HEAD), BF16),
                pltpu.VMEM((width, 3 * HEAD), BF16),
            ],
        ),
        out_shape=outs,
        compiler_params=params(),
        cost_estimate=beside(20 * rows * width),
        name="attend",
    )(slot, f, qk, vd, *tables, first, back)


def collect_kernel(f_ref, a_ref, b_ref, *refs, heads):
    (so0_ref, so1_ref, sums0_ref, vec_ref, own_ref, other_ref, wm_ref, wm_far_ref) = refs[:8]
    refs = refs[8:]
    packs, refs = refs[: 2 * len(heads)], refs[2 * len(heads) :]
    own_out, near_out, sums_ref, wt_ref = refs
    step = pl.program_id(0)
    first = heads[0] == 0
    wide = 3 * HEAD
    count = len(heads)
    all_heads = own_ref.shape[1] // wide // 2

    @pl.when(step == 0)
    def _():
        f, rows = f_ref[0], own_ref.shape[0]
        for k in range(2):
            for i, h in enumerate(heads):
                part = slice(wide * (all_heads * k + h), wide * (all_heads * k + h + 1))
                to = count * k + i
                wt_ref[to, pl.ds(pl.multiple_of(f * rows, rows), rows), :] = own_ref[:, part]
                wt_ref[to, pl.ds(pl.multiple_of((1 - f) * rows, rows), rows), :] = other_ref[:, part]
        sums_ref[...] = jnp.zeros_like(sums_ref) if first else sums0_ref[...]

    gain = vec_ref[0:1, :]
    n = normal(choose(step, (a_ref, b_ref), 0).astype(F32))
    merged = jnp.zeros(n.shape, F32)
    grad_first = jnp.zeros(n.shape, F32)
    for k, weights in enumerate((wm_ref, wm_far_ref)):
        for i, h in enumerate(heads):
            pack = packs[count * k + i]
            merged = merged + mm(pack[0, :, wide:], weights[HEAD * h : HEAD * (h + 1), :])
            gj = pack[0, :, :wide]
            row = 2 + all_heads * k + h
            sums_ref[row : row + 1, :wide] += colsum(gj.astype(F32))
            grad_first = grad_first + mm(gj, wt_ref[count * k + i], NT)
    u = grad_first * gain
    if not first:
        merged = merged + choose(step, (so0_ref, so1_ref), 0).astype(F32)
        u = u + choose(step, (so0_ref, so1_ref), 1).astype(F32)

    @pl.when(step < 2)
    def _():
        own_out[0], own_out[1] = merged.astype(BF16), u.astype(BF16)

    @pl.when(step >= 2)
    def _():
        near_out[0], near_out[1] = merged.astype(BF16), u.astype(BF16)

    sums_ref[0:1, :] += colsum(grad_first * n)
    sums_ref[1:2, :] += colsum(grad_first)


def collect(f, own_x, near_x, heads, packs, packs_far, vec, own, other, wm, wm_far, so_far=None):
    _, rows, width = own_x.shape
    pack = pl.BlockSpec((1, TILE, 4 * HEAD), lambda i, *_: (i, 0, 0))
    blocks = piece_specs(2, 2, width)
    so_far_specs = blocks
    if so_far is None:
        so_far = (jnp.zeros((8, 128), F32),) * 3
        so_far_specs = [whole((8, 128))] * 2
    return pl.pallas_call(
        functools.partial(collect_kernel, heads=heads),
        grid_spec=pltpu.PrefetchScalarGridSpec(
            num_scalar_prefetch=1,
            grid=(2 * rows // TILE,),
            in_specs=piece_specs(2, 1, width)
            + so_far_specs
            + [whole(v.shape) for v in (so_far[2], vec, own, other, wm, wm_far)]
            + [pack] * (2 * len(heads)),
            out_specs=blocks + [whole((8, width))],
            scratch_shapes=[pltpu.VMEM((2 * len(heads), width, 3 * HEAD), BF16)],
        ),
        out_shape=[
            jax.ShapeDtypeStruct((2, rows, width), BF16),
            jax.ShapeDtypeStruct((2, rows, width), BF16),
            jax.ShapeDtypeStruct((8, width), F32),
        ],
        compiler_params=params(),
        cost_estimate=beside(10 * rows * width),
        name="collect",
    )(f, own_x, near_x, *so_far, vec, own, other, wm, wm_far, *packs, *packs_far)


def slot_part(refs, slot, index):
    value = refs[0][index]
    for k in range(1, len(refs)):
        value = jnp.where(slot == k, refs[k][index], value)
    return value


def put_expand_kernel(c_ref, d_ref, *refs, shards):
    *ins, out = refs
    count, rows, columns = ins[0].shape
    cut = columns // shards
    k = (d_ref[0] - pl.program_id(0) + count) % count
    for b in range(CTX):
        slot = slot_of(c_ref[0] ^ b)
        value = slot_part(ins, slot, k).astype(F32)
        for g in range(shards):
            out[:, (g * CTX + b) * cut : (g * CTX + b + 1) * cut] = value[:, g * cut : (g + 1) * cut]


def put_expand(c, d, parts, shards):
    count, rows, columns = parts[0].shape
    return pl.pallas_call(
        functools.partial(put_expand_kernel, shards=shards),
        grid_spec=pltpu.PrefetchScalarGridSpec(
            num_scalar_prefetch=2,
            grid=(count // 2,),
            in_specs=[whole(parts[0].shape)] * CTX,
            out_specs=pl.BlockSpec((rows, CTX * columns), lambda a, *_: (a, 0)),
        ),
        out_shape=jax.ShapeDtypeStruct((count // 2 * rows, CTX * columns), F32),
        compiler_params=params(),
        cost_estimate=beside(50 * rows * columns),
        name="put_expand",
    )(c, d, *parts)


def put_reduce_kernel(c_ref, d_ref, *refs):
    *ins, out = refs
    count, rows, columns = ins[0].shape
    slot = slot_of(c_ref[0] ^ pl.program_id(0))
    for a in range(count // 2):
        k = (d_ref[0] - a - count // 2 + count) % count
        out[rows * a : rows * (a + 1), :] = slot_part(ins, slot, k).astype(F32)


def put_reduce(c, d, parts):
    count, rows, columns = parts[0].shape
    own = count // 2 * rows
    return pl.pallas_call(
        put_reduce_kernel,
        grid_spec=pltpu.PrefetchScalarGridSpec(
            num_scalar_prefetch=2,
            grid=(CTX,),
            in_specs=[whole(parts[0].shape)] * CTX,
            out_specs=pl.BlockSpec((own, columns), lambda b, *_: (b, 0)),
        ),
        out_shape=jax.ShapeDtypeStruct((CTX * own, columns), F32),
        compiler_params=params(),
        cost_estimate=beside(50 * rows * columns),
        name="put_reduce",
    )(c, d, *parts)


def put_heads_kernel(c_ref, d_ref, f_ref, *refs, top, with_merge):
    parts, outs, scratch = refs[:CTX], refs[CTX : CTX + 1 + with_merge], refs[-1]
    count, rows, columns = parts[0].shape
    heads = columns // (3 * HEAD)
    wide = 3 * HEAD
    for b in range(CTX):
        slot = slot_of(c_ref[0] ^ b)
        for a in range(count):
            k = (d_ref[0] - a + count) % count
            scratch[rows * a : rows * (a + 1), :] = slot_part(parts, slot, k)
        outs[0][:, columns * b : columns * (b + 1)] = scratch[:top, :].astype(F32)
        if with_merge:
            per = (count * rows - top) // HEAD

            @pl.when(b // (CTX // 2) == f_ref[0])
            def _(b=b):
                for h in range(heads):
                    row = heads * HEAD * (b % (CTX // 2)) + HEAD * h
                    for k in range(per):
                        src = slice(top + HEAD * k, top + HEAD * (k + 1))
                        part = scratch[src, wide * h : wide * (h + 1)]
                        outs[1][row : row + HEAD, wide * k : wide * (k + 1)] = part.astype(F32)


def put_heads(c, d, f, parts, top, width, with_merge):
    count, rows, columns = parts[0].shape
    shapes = [jax.ShapeDtypeStruct((top, CTX * columns), F32)]
    if with_merge:
        shapes.append(jax.ShapeDtypeStruct((width // 2, width), F32))
    return pl.pallas_call(
        functools.partial(put_heads_kernel, top=top, with_merge=with_merge),
        grid_spec=pltpu.PrefetchScalarGridSpec(
            num_scalar_prefetch=3,
            grid=(1,),
            in_specs=[whole(v.shape) for v in parts],
            out_specs=[whole(v.shape) for v in shapes],
            scratch_shapes=[pltpu.VMEM((count * rows, columns), BF16)],
        ),
        out_shape=shapes,
        compiler_params=params(),
        cost_estimate=short(),
        name="put_heads",
    )(c, d, f, *parts)


def rotary(rows):
    lane = jnp.arange(2 * HEAD, dtype=jnp.int32)[None, :] % HEAD
    half = ROT // 2
    inverse = 10000.0 ** (-2.0 * (lane % half).astype(F32) / ROT)
    angles = jnp.arange(rows, dtype=jnp.int32).astype(F32)[:, None] * inverse
    cos = jnp.where(lane < ROT, jnp.cos(angles), 1.0)
    sine = jnp.sin(angles)
    low = jnp.where(lane < half, -sine, 0.0)
    high = jnp.where((lane >= half) & (lane < ROT), sine, 0.0)
    return cos, low, high


def local(
    tokens, cotangent, block_order, first_gain, first_shift, second_gain, second_shift,
    triple_weight, triple_bias, merge_weight, merge_bias, expand_weight, expand_bias,
    reduce_weight, reduce_bias,
):
    c, d, f = lax.axis_index("ctx"), lax.axis_index("dp"), lax.axis_index("fsdp")
    shards = lax.axis_size("fsdp")
    own_len, width = tokens.shape[1:]
    inner = expand_weight.shape[1]
    own_inner = inner // shards // CTX
    ctx_inner = inner // CTX
    own_heads = HEADS // CTX
    own_cols = own_heads * 3 * HEAD
    own_merge = own_heads * HEAD
    half = CTX // 2

    own_expand = jnp.concatenate(
        [
            lax.dynamic_slice_in_dim(expand_weight, g * CTX * own_inner + c * own_inner, own_inner, 1)
            for g in range(shards)
        ],
        axis=1,
    )
    own_reduce = lax.dynamic_slice_in_dim(reduce_weight, c * own_inner, own_inner, 0)
    own_bias = lax.dynamic_slice_in_dim(expand_bias, c * own_inner, own_inner, 0)
    own_triple = jnp.concatenate(
        [lax.dynamic_slice_in_dim(triple_weight, k * own_cols, own_cols, 1) for k in (c, c ^ 2)], axis=1
    )
    smalls = jnp.stack(
        [first_gain, first_shift, second_gain, second_shift, own_bias, merge_bias, reduce_bias]
    )
    if shards == 2:
        own_tb = lax.dynamic_slice_in_dim(triple_bias, (c % half) * own_cols, own_cols, 0)
        rows = jnp.concatenate(
            [
                jnp.pad(smalls, ((0, 1), (0, width - smalls.shape[1]))),
                jnp.pad(own_tb[None], ((0, 7), (0, width - own_cols))),
            ]
        )
        w_own = jnp.concatenate([own_expand, own_reduce, rows])
        w_other = swap(w_own, "fsdp", 1)
        last = width // 2 + ctx_inner // 2
        own_s, other_s = w_own[last:], w_other[last:]
        cut = smalls.shape[1]
        vec = jnp.where(
            f == 0,
            jnp.concatenate([own_s[:8, :cut], other_s[:8, :cut]], axis=1),
            jnp.concatenate([other_s[:8, :cut], own_s[:8, :cut]], axis=1),
        ).astype(F32)
        tb = jnp.where(f == c // half, own_s[8, :own_cols], other_s[8, :own_cols]).astype(F32)
        t_own = own_triple
        m_own = lax.dynamic_slice_in_dim(merge_weight, (c % half) * own_merge, own_merge, 0)
        side = f
    else:
        def full(v):
            return lax.all_gather(v, "fsdp", axis=0, tiled=True)

        we, wr, wt = full(own_expand), full(own_reduce), full(own_triple)
        w_own = jnp.concatenate([we[: width // 2], wr[: ctx_inner // 2]])
        w_other = jnp.concatenate([we[width // 2 :], wr[ctx_inner // 2 :]])
        t_own, t_other = wt[: width // 2], wt[width // 2 :]
        vec = lax.all_gather(smalls, "fsdp", axis=1, tiled=True).astype(F32)
        vec = jnp.pad(vec, ((0, 1), (0, 0)))
        tb = lax.dynamic_slice_in_dim(full(triple_bias), c * own_cols, own_cols, 0).astype(F32)
        m_own = full(merge_weight)
        side = jnp.int32(0)
    tb = tb.reshape(own_heads, 1, 3 * HEAD)
    flag = side.astype(jnp.int32).reshape(1)

    own = jnp.stack([tokens.reshape(own_len, width), cotangent.reshape(own_len, width)])
    far = swap(own, "ctx", 2)
    near = swap(own, "ctx", 1)
    pos = jnp.concatenate(
        [lax.dynamic_slice_in_dim(block_order, 2 * (c ^ r), 2) for r in range(CTX)]
    )
    blocks = jnp.arange(pos.shape[0], dtype=jnp.int32)
    slot = jnp.sum(jnp.where(pos[None, :] == blocks[:, None], blocks[None, :], 0), axis=1)
    slot = slot.astype(jnp.int32)
    tables = rotary(CTX * own_len)
    far, t_own, m_own, w_other, *tables = lax.optimization_barrier(
        (far, t_own, m_own, w_other, *tables)
    )
    both = swap(far, "ctx", 1)
    if shards == 2:
        t_other, m_other = swap(t_own, "fsdp", 1), swap(m_own, "fsdp", 1)
    else:
        m_own, m_other = (
            lax.dynamic_slice_in_dim(m_own, k * own_merge, own_merge, 0) for k in (c, c ^ 2)
        )

    lu_keep, lu_send, *g_feed, sums2 = feed(
        flag, own, far, near, both, vec, w_own, w_other, width, ctx_inner
    )
    way_f = Summed(split_feed(g_feed, shards, width), f, d)
    lu_send, pos, t_other, m_other = boundary([way_f], lu_send, pos, t_other, m_other)
    if shards == 2:
        wm = jnp.where(f == c // half, m_own, m_other)
        wm_far = jnp.where(f == c // half, m_other, m_own)
    else:
        wm, wm_far = m_own, m_other
    lu_in = swap(lu_send, "ctx", 1)
    last = pos.shape[0] // 2
    qk, vd, first, back = project(
        pos[:last], flag, (own, near), vec, tb, t_own, t_other, wm, tables
    )
    lu_far = add_low(lu_keep[1], lu_in[1])
    qk, lu_far = lax.optimization_barrier((qk, lu_far))
    lu_far = swap(lu_far, "ctx", 2)
    qk, vd, first, back = project(
        pos[last:], flag, (far, both), vec, tb, t_own, t_other, wm, tables, (qk, vd, first, back)
    )
    (qk,) = boundary([way_f], qk)
    packs, packs_far, gs = [], [], []

    def next_head(qk, h):
        pack, sent, *g = attend(slot, flag, qk, vd, tables, first, back, h)
        packs.append(pack)
        gs.append(g)
        return sent

    sent = next_head(qk, 0)
    qk, sent, lu_far = boundary([way_f], qk, sent, lu_far)
    packs_far.append(swap(sent, "ctx", 2))
    sent = next_head(qk, 1)
    g_two = [jnp.concatenate(g, axis=1) for g in zip(*gs)]
    way_two = Summed(split_rows(g_two, shards, width), f, d)
    qk, sent_two, packs_far[0] = boundary([way_two, way_f], qk, sent, packs_far[0])
    sent_one = next_head(qk, 2)
    way_one = Summed(split_rows(gs[-1], shards, width), f, d)
    ways = [way_one, way_two]
    c1, d1, f1 = (v.astype(jnp.int32).reshape(1) for v in (c, d, f))
    c1, sent_two, sent_one = boundary([way_one, way_f], c1, sent_two, sent_one, hold=[way_two])
    packs_far.append(swap(sent_two, "ctx", 2))
    feed_parts = way_f.finish()
    c1, feed_parts = boundary([way_two], c1, feed_parts)
    grad_expand = put_expand(c1, d1, feed_parts, shards)
    grad_reduce = put_reduce(c1, d1, feed_parts)
    flag1, grad_expand, grad_reduce, sent_one, packs_far[1] = boundary(
        [way_one], flag, grad_expand, grad_reduce, sent_one, packs_far[1], hold=[way_two]
    )
    packs_far.append(swap(sent_one, "ctx", 2))
    so_far = collect(
        flag1, own, near, (0, 1), packs[:2], packs_far[:2], vec, t_own, t_other, wm, wm_far
    )
    flag1, packs_far[2], so_far = boundary([], flag, packs_far[2], so_far, hold=[way_one])
    way_t = way_two.beside(way_one)
    ways = [way_t]
    flag1, so_far = boundary(ways, flag1, so_far)
    mu, mu_near, sums1 = collect(
        flag1, own, near, (2,), packs[2:], packs_far[2:], vec, t_own, t_other, wm, wm_far, so_far
    )

    tb_rows = sums1[2 : 2 + 2 * own_heads, : 3 * HEAD].reshape(2, own_cols)
    tb_rows = jnp.pad(tb_rows, ((0, 0), (0, width - own_cols)))
    eb_row = jnp.pad(sums2[2:3], ((0, 0), (0, width - ctx_inner)))
    mine = (jnp.arange(CTX) == c)[:, None]
    across = (jnp.arange(CTX) == (c ^ 2))[:, None]
    tb_block = jnp.where(mine, tb_rows[:1], jnp.where(across, tb_rows[1:], 0.0))
    vector = jnp.concatenate(
        [sums1[:2], sums2[:2], sums2[3:4], tb_block, jnp.where(mine, eb_row, 0.0)]
    )
    vector = jnp.pad(vector, ((0, 3), (0, 0)))

    c1, mu_near, vector = boundary(ways, c1, mu_near, vector)
    mu_in = swap(mu_near, "ctx", 1)
    if shards == 2:
        vector = vector + swap(vector, "fsdp", 1)
    else:
        vector = lax.psum(vector, "fsdp")
    mu_in, vector = lax.optimization_barrier((mu_in, vector))
    vector = vector + swap(vector, "dp", 1)
    lu = lu_keep[0].astype(F32) + lu_in[0].astype(F32) + lu_far.astype(F32)
    mixed, u = lu + mu.astype(F32) + mu_in.astype(F32)

    x_f = own[0].astype(F32)
    mixed = (x_f + mixed + (vec[5] + vec[6])[None, :]).astype(BF16)
    average = jnp.mean(x_f, axis=-1, keepdims=True)
    centred = x_f - average
    r = lax.rsqrt(jnp.mean(centred * centred, axis=-1, keepdims=True) + epsilon)
    n = centred * r
    input_grad = own[1].astype(F32) + r * (
        u - jnp.mean(u, axis=-1, keepdims=True) - n * jnp.mean(u * n, axis=-1, keepdims=True)
    )

    vector, mixed, input_grad = lax.optimization_barrier((vector, mixed, input_grad))
    vector = vector + swap(vector, "dp", 2)
    vector = vector + swap(vector, "ctx", 1)
    (vector,) = boundary(ways, vector)
    vector = vector + swap(vector, "ctx", 2)
    part = width // shards
    five = lax.dynamic_slice_in_dim(vector[:5], f * part, part, 1)
    d_g1, d_s1, d_g2, d_s2, d_cot = [five[i] for i in range(5)]
    d_tb = vector[5 : 5 + CTX, :own_cols].reshape(-1)
    d_tb = lax.dynamic_slice_in_dim(d_tb, f * (3 * part), 3 * part, 0)
    d_eb = lax.dynamic_slice_in_dim(vector[5 + CTX : 5 + 2 * CTX], f * own_inner, own_inner, 1)
    d_eb = d_eb.reshape(-1)

    parts = way_t.finish()
    parts, vector = lax.optimization_barrier((parts, vector))
    placed = put_heads(c1, d1, f1, parts, part, width, shards == 2)
    grad_triple = placed[0]
    if shards == 2:
        grad_merge = placed[1]
    else:
        count = lax.axis_size("dp")
        g_all = [
            jnp.concatenate([pick(g, (d - a) % count) for a in range(count)])
            for g in in_order(parts, c)
        ]
        wide = 3 * HEAD
        grad_merge = jnp.concatenate(
            [
                g[part:].reshape(width // wide, HEAD, own_heads, wide).transpose(2, 1, 0, 3)
                .reshape(own_merge, width) for g in g_all
            ]
        )
        grad_merge = lax.dynamic_slice_in_dim(grad_merge, f * part, part, 0).astype(F32)
    return (
        mixed[None],
        input_grad[None],
        d_g1,
        d_s1,
        d_g2,
        d_s2,
        grad_triple,
        d_tb,
        grad_merge,
        d_cot,
        grad_expand,
        d_eb,
        grad_reduce,
        d_cot,
    )


def split_feed(g, shards, width):
    if shards == 2:
        return tuple(g)
    g = jnp.stack(g)
    half = width // 2
    ge, gr = g[:, :half].reshape(width, -1), g[:, half:].reshape(-1, width)
    parts = [v.reshape(shards, v.shape[0] // shards, v.shape[1]) for v in (ge, gr)]
    return jnp.concatenate(parts, axis=1)


def split_rows(g, shards, width):
    if shards == 2:
        return tuple(g)
    g = jnp.stack(g)
    rows = g[:, : width // 2].reshape(shards, width // shards, g.shape[2])
    tail = jnp.broadcast_to(g[:1, width // 2 :], (shards,) + g[0, width // 2 :].shape)
    return jnp.concatenate([rows, tail], axis=1)


def solution(mesh):
    tokens = P(("dp", "fsdp"), "ctx", None)
    row, vector = P("fsdp", None), P("fsdp")
    weights = (row, vector, row, vector, row, vector, row, vector)
    in_specs = (tokens, tokens, P()) + (vector,) * 4 + weights
    out_specs = (tokens, tokens) + (vector,) * 4 + weights
    return jax.shard_map(local, mesh=mesh, in_specs=in_specs, out_specs=out_specs, check_vma=False)
```

```python
import functools
import math

import jax
import jax.numpy as jnp
from jax import lax
from jax.experimental import pallas as pl
from jax.experimental.pallas import tpu as pltpu
from jax.sharding import PartitionSpec as P

HEADS = 12
HEAD = 64
ROT = 16
TILE = 256
CTX = 4
epsilon = 1e-05
masked_value = -1e30
F32 = jnp.float32
BF16 = jnp.bfloat16
VMEM_LIMIT = 58 * 1024 * 1024

NN = (((1,), (0,)), ((), ()))
NT = (((1,), (1,)), ((), ()))
TN = (((0,), (0,)), ((), ()))


def mm(a, b, dims=NN):
    return lax.dot_general(a, b, dims, preferred_element_type=F32)


def swap(value, axis, bit):
    count = lax.axis_size(axis)
    return lax.ppermute(value, axis, [(i, i ^ bit) for i in range(count)])


def pick(stacked, index):
    return lax.dynamic_index_in_dim(stacked, index, 0, keepdims=False)


def add_low(a, b):
    return (a.astype(F32) + b.astype(F32)).astype(BF16)


def after(value, *others):
    return lax.optimization_barrier((value,) + others)[0]


def slot_of(relative):
    return (relative % 2) * 2 + relative // 2


def in_order(both, c):
    both = jnp.stack(both)
    return [pick(both, slot_of(c ^ b)) for b in range(CTX)]


class Summed:
    def __init__(self, value, f, d):
        self.value, self.f, self.d = value, f, d
        self.steps = ["fsdp", "dp_down", "dp_up", "far", "near"]
        self.moving = None

    def send(self):
        kind, value = self.steps[0], self.value
        count = lax.axis_size("dp")
        if kind == "fsdp":
            self.moving = [value[1]] if isinstance(value, tuple) else []
        elif kind == "dp_down":
            self.value = value.reshape(count, value.shape[0] // count, value.shape[1])
            self.moving = [pick(self.value, (self.d + k) % count) for k in range(1, count)]
        elif kind == "near":
            self.moving = [value[1]]
        else:
            self.moving = [value]
        return self.moving

    def receive(self):
        kind, moving = self.steps[0], self.moving
        count = lax.axis_size("dp")
        turns = [[(i, (i + k) % count) for i in range(count)] for k in range(1, count)]
        if kind == "fsdp":
            return [swap(v, "fsdp", 1) for v in moving]
        if kind == "dp_down":
            return [lax.ppermute(v, "dp", t) for v, t in zip(moving, turns)]
        if kind == "dp_up":
            return [lax.ppermute(moving[0], "dp", t) for t in turns]
        if kind == "far":
            return [swap(moving[0], "ctx", 2), swap(moving[0], "ctx", 1)]
        return [swap(moving[0], "ctx", 1)]

    def take(self, came):
        kind = self.steps.pop(0)
        if kind == "fsdp":
            if came:
                self.value = add_low(self.value[0], came[0])
            else:
                self.value = lax.psum_scatter(self.value, "fsdp", scatter_dimension=0, tiled=False)
        elif kind == "dp_down":
            total = pick(self.value, self.d).astype(F32)
            for v in came:
                total = total + v.astype(F32)
            self.value = total.astype(BF16)
        elif kind == "dp_up":
            self.value = jnp.stack([self.moving[0]] + came)
        elif kind == "far":
            self.value = [self.moving[0]] + came
        else:
            self.value = self.value + came
        self.moving = None

    def beside(self, other):
        self.value = jnp.concatenate([self.value, other.value], axis=1)
        return self

    def finish(self):
        while self.steps:
            if self.moving is None:
                self.send()
            self.take(self.receive())
        return self.value


def boundary(ways, *values, hold=()):
    moved = [way for way in (*ways, *hold) if way.moving is not None]
    came, values = lax.optimization_barrier(([way.receive() for way in moved], values))
    for way, v in zip(moved, came):
        way.take(v)
    for way in ways:
        way.moving = way.send() if way.steps else None
    for way in hold:
        way.value, values = lax.optimization_barrier((way.value, values))
    sent = [tuple(way.moving or ()) for way in ways]
    sent, values = lax.optimization_barrier((sent, values))
    for way, moving in zip(ways, sent):
        if way.moving is not None:
            way.moving = list(moving)
    return values


def normal(x):
    average = jnp.mean(x, axis=-1, keepdims=True)
    centred = x - average
    spread = jnp.mean(centred * centred, axis=-1, keepdims=True)
    return centred * lax.rsqrt(spread + epsilon)


def colsum(v):
    return jnp.sum(v, axis=0, keepdims=True)


def whole(shape):
    return pl.BlockSpec(shape, lambda *_: (0,) * len(shape))


def params(**more):
    return pltpu.CompilerParams(
        dimension_semantics=("arbitrary",), vmem_limit_bytes=VMEM_LIMIT, **more
    )


def cost(flops, moved, exps=0):
    return pl.CostEstimate(flops=flops, bytes_accessed=moved, transcendentals=exps)


def beside(moved):
    return cost(0, 100 * moved)


def short():
    return cost(0, 0)


def place(f, own, other, out):
    rows = own.shape[0]
    out[pl.ds(pl.multiple_of(f * rows, rows), rows), :] = own
    out[pl.ds(pl.multiple_of((1 - f) * rows, rows), rows), :] = other


def feed_kernel(
    f_ref, a_ref, b_ref, c_ref, d_ref, vec_ref, own_ref, other_ref,
    keep_ref, send_ref, g_keep_ref, g_send_ref, sums_ref, we_ref, wr_ref, ge_acc, gr_acc,
):
    step = pl.program_id(0)
    half = we_ref.shape[0] // 2

    @pl.when(step == 0)
    def _():
        f = f_ref[0]
        place(f, own_ref[:half], other_ref[:half], we_ref)
        place(f, own_ref[half : 2 * half], other_ref[half : 2 * half], wr_ref)
        ge_acc[...] = jnp.zeros_like(ge_acc)
        gr_acc[...] = jnp.zeros_like(gr_acc)
        sums_ref[...] = jnp.zeros_like(sums_ref)
        sums_ref[3:4, :] = colsum(a_ref[1].astype(F32))

    def piece(k):
        first = jnp.where(step == 0, a_ref[k], b_ref[k])
        return jnp.where(step < 2, first, jnp.where(step == 2, c_ref[k], d_ref[k]))

    gain, shift, bias = vec_ref[2:3, :], vec_ref[3:4, :], vec_ref[4:5, :]
    n = normal(piece(0).astype(F32))
    second = (n * gain + shift).astype(BF16)
    back = piece(1)
    hidden = mm(second, we_ref[...]) + bias
    grad_active = mm(back, wr_ref[...], NT)
    cdf = 0.5 * (1.0 + lax.erf(hidden * (1.0 / math.sqrt(2.0))))
    active = (hidden * cdf).astype(BF16)
    low = mm(active, wr_ref[...]).astype(BF16)
    slope = cdf + hidden * (jnp.exp(-0.5 * hidden * hidden) * (1.0 / math.sqrt(2.0 * math.pi)))
    grad_hidden = (grad_active * slope).astype(BF16)
    gr_acc[...] += mm(active, back, TN)
    ge_acc[...] += mm(second, grad_hidden, TN)
    grad_second = mm(grad_hidden, we_ref[...], NT)
    u = (grad_second * gain).astype(BF16)
    sums_ref[0:1, :] += colsum(grad_second * n)
    sums_ref[1:2, :] += colsum(grad_second)
    sums_ref[2:3, :] += colsum(grad_hidden.astype(F32))

    @pl.when(step < 2)
    def _():
        keep_ref[0, 0], keep_ref[0, 1] = low, u

    @pl.when(step >= 2)
    def _():
        send_ref[0, 0], send_ref[0, 1] = low, u

    @pl.when(step == pl.num_programs(0) - 1)
    def _():
        for s, g_ref in ((f_ref[0], g_keep_ref), (1 - f_ref[0], g_send_ref)):
            rows = pl.ds(pl.multiple_of(s * half, half), half)
            g_ref[:half] = ge_acc[rows, :].astype(BF16)
            g_ref[half:] = gr_acc[rows, :].astype(BF16)


def feed(f, own_x, far, near, both, vec, own, other, width, inner):
    rows = own_x.shape[1]
    shape_e, shape_r = (width, inner), (inner, width)
    outs = [
        jax.ShapeDtypeStruct((2, 2, rows, width), BF16),
        jax.ShapeDtypeStruct((2, 2, rows, width), BF16),
        jax.ShapeDtypeStruct(((width + inner) // 2, width), BF16),
        jax.ShapeDtypeStruct(((width + inner) // 2, width), BF16),
        jax.ShapeDtypeStruct((8, width), F32),
    ]
    args = (own_x, far, near, both, vec, own, other)
    block = (1, 2, rows, width)
    return pl.pallas_call(
        feed_kernel,
        grid_spec=pltpu.PrefetchScalarGridSpec(
            num_scalar_prefetch=1,
            grid=(CTX,),
            in_specs=[whole(v.shape) for v in args],
            out_specs=[
                pl.BlockSpec(block, lambda i, *_: (jnp.minimum(i, 1), 0, 0, 0)),
                pl.BlockSpec(block, lambda i, *_: (jnp.maximum(i - 2, 0), 0, 0, 0)),
            ]
            + [whole(v.shape) for v in outs[2:]],
            scratch_shapes=[
                pltpu.VMEM(shape_e, BF16), pltpu.VMEM(shape_r, BF16),
                pltpu.VMEM(shape_e, F32), pltpu.VMEM(shape_r, F32),
            ],
        ),
        out_shape=outs,
        compiler_params=params(),
        cost_estimate=beside(16 * rows * width),
        name="feed",
    )(f, *args)


def turn(u, cos, sin_a, sin_b):
    return u * cos + pltpu.roll(u, 120, 1) * sin_a + pltpu.roll(u, 8, 1) * sin_b


def place_heads(f, own, other, out):
    rows = own.shape[0]
    wide = out.shape[2]
    for h in range(out.shape[0]):
        part = slice(wide * h, wide * (h + 1))
        out[h, pl.ds(pl.multiple_of(f * rows, rows), rows), :] = own[:, part]
        out[h, pl.ds(pl.multiple_of((1 - f) * rows, rows), rows), :] = other[:, part]


def choose(step, refs, index):
    value = refs[-1][index]
    for k in range(len(refs) - 2, -1, -1):
        value = jnp.where(step < 2 * k + 2, refs[k][index], value)
    return value


def piece_specs(count, lead, width, first=0):
    return [
        pl.BlockSpec(
            (lead, TILE, width), lambda i, *_, k=k: (first, jnp.clip(i - 2 * k, 0, 1), 0)
        )
        for k in range(count)
    ]


def project_kernel(pos_ref, f_ref, a_ref, b_ref, vec_ref, tb_ref, own_ref, other_ref, wm_ref,
    cos_ref, sa_ref, sb_ref, *refs):
    qk_ref, vd_ref, first_ref, back_ref, wt_ref = refs[-5:]
    step = pl.program_id(0)

    @pl.when(step == 0)
    def _():
        place_heads(f_ref[0], own_ref[...], other_ref[...], wt_ref)

    pieces = (a_ref, b_ref)
    x = choose(step, pieces, 0)
    back = choose(step, pieces, 1)
    first = (normal(x.astype(F32)) * vec_ref[0:1, :] + vec_ref[1:2, :]).astype(BF16)
    first_ref[...] = first
    back_ref[...] = back
    grad_out = mm(back, wm_ref[...], NT)
    heads = wt_ref.shape[0]
    lane = lax.broadcasted_iota(jnp.int32, (TILE, 2 * HEAD), 1)
    scale = jnp.where(lane < HEAD, 1.0 / math.sqrt(HEAD), 1.0)
    for h in range(heads):
        joined = mm(first, wt_ref[h]) + tb_ref[h]
        turned = turn(joined[:, : 2 * HEAD], cos_ref[...], sa_ref[...], sb_ref[...])
        qk_ref[h] = (turned * scale).astype(BF16)
        vd_ref[h, :, :HEAD] = joined[:, 2 * HEAD :].astype(BF16)
        vd_ref[h, :, HEAD:] = grad_out[:, HEAD * h : HEAD * (h + 1)].astype(BF16)


def project(pos, f, pieces, vec, tb, own, other, wm, tables, so_far=()):
    width = pieces[0].shape[2]
    rows = CTX * pieces[0].shape[1]
    heads = tb.shape[0]
    table = pl.BlockSpec((TILE, 2 * HEAD), lambda i, p, f: (p[i], 0))
    out = pl.BlockSpec((heads, TILE, 2 * HEAD), lambda i, p, f: (0, p[i], 0))
    row = pl.BlockSpec((TILE, width), lambda i, p, f: (p[i], 0))
    args = (pos, f, *pieces, vec, tb, own, other, wm, *tables)
    return pl.pallas_call(
        project_kernel,
        grid_spec=pltpu.PrefetchScalarGridSpec(
            num_scalar_prefetch=2,
            grid=(rows // TILE // 2,),
            in_specs=piece_specs(2, 2, width)
            + [whole(v.shape) for v in (vec, tb, own, other, wm)]
            + [table] * 3
            + [pl.BlockSpec(memory_space=pl.ANY)] * len(so_far),
            out_specs=[out, out, row, row],
            scratch_shapes=[pltpu.VMEM((heads, width, 3 * HEAD), BF16)],
        ),
        out_shape=[jax.ShapeDtypeStruct((heads, rows, 2 * HEAD), BF16)] * 2
        + [jax.ShapeDtypeStruct((rows, width), BF16)] * 2,
        input_output_aliases={len(args) + k: k for k in range(len(so_far))},
        compiler_params=params(),
        cost_estimate=beside(10 * rows * width),
        name="project",
    )(*args, *so_far)


def attend_kernel(
    slot_ref, f_ref, qk_ref, vd_ref, cos_ref, sa_ref, sb_ref, first_ref, back_ref, keep_ref, send_ref, g_keep_ref, g_send_ref,
    qt, vt, ks, vs, ds_, s_ref, gq, gk, gv, att_ref, gj_ref, grad_t,
):
    rows = qk_ref.shape[1]
    blocks = rows // TILE

    for b in range(blocks):
        r = slice(TILE * b, TILE * (b + 1))
        qt[:, r] = qk_ref[0, r, :].T
        vt[:, r] = vd_ref[0, r, :].T
        ks[r, :] = qk_ref[0, r, HEAD:]
        vs[r, :] = vd_ref[0, r, :HEAD]
        ds_[r, :] = vd_ref[0, r, HEAD:]
    key_id = lax.broadcasted_iota(jnp.int32, (TILE, TILE), 0)
    query_id = lax.broadcasted_iota(jnp.int32, (TILE, TILE), 1)
    keep = key_id <= query_id
    def put_scores(i, j, peak):
        kr = slice(TILE * j, TILE * (j + 1))
        s = mm(ks[kr, :], qt[:HEAD, TILE * i : TILE * (i + 1)])
        if j == i:
            s = jnp.where(keep, s, masked_value)
        s_ref[i % 2, kr, :] = s
        top = jnp.max(s, axis=0, keepdims=True)
        return top if peak is None else jnp.maximum(peak, top)

    next_peak = put_scores(0, 0, None)
    for i in range(blocks):
        qr = slice(TILE * i, TILE * (i + 1))
        peak, next_peak = next_peak, None
        total = jnp.zeros((1, TILE), F32)
        out = jnp.zeros((HEAD, TILE), F32)
        for j in range(i + 1):
            kr = slice(TILE * j, TILE * (j + 1))
            e = jnp.exp(s_ref[i % 2, kr, :] - peak)
            if i + 1 < blocks:
                next_peak = put_scores(i + 1, j, next_peak)
            s_ref[i % 2, kr, :] = e
            total = total + jnp.sum(e, axis=0, keepdims=True)
            out = out + mm(vt[:HEAD, kr], e.astype(BF16))
        if i + 1 < blocks:
            next_peak = put_scores(i + 1, i + 1, next_peak)
        inv = 1.0 / total
        out = out * inv
        att_ref[:, qr] = out.astype(BF16)
        gj_ref[qr, 3 * HEAD :] = out.T.astype(BF16)
        d_t = vt[HEAD:, qr]
        delta = jnp.sum(d_t.astype(F32) * out, axis=0, keepdims=True)
        q = qk_ref[0, qr, :HEAD]
        d = ds_[qr, :]
        grad_q = jnp.zeros((HEAD, TILE), F32)
        for j in range(i + 1):
            kr = slice(TILE * j, TILE * (j + 1))
            p = s_ref[i % 2, kr, :] * inv
            g = (p * (mm(vs[kr, :], d_t) - delta)).astype(BF16)
            grad_v = mm(p.astype(BF16), d)
            grad_k = mm(g, q)
            grad_q = grad_q + mm(qt[HEAD:, kr], g)
            if j == i:
                gv[kr, :] = grad_v
                gk[kr, :] = grad_k
            else:
                gv[kr, :] += grad_v
                gk[kr, :] += grad_k
        gq[:, qr] = grad_q * (1.0 / math.sqrt(HEAD))
    for b in range(blocks):
        r = slice(TILE * b, TILE * (b + 1))
        both = jnp.concatenate([gq[:, r].T, gk[r, :]], axis=1)
        gj_ref[r, : 2 * HEAD] = turn(both, cos_ref[r, :], -sa_ref[r, :], -sb_ref[r, :]).astype(BF16)
        gj_ref[r, 2 * HEAD : 3 * HEAD] = gv[r, :].astype(BF16)
    grad_t[...] = mm(first_ref[...], gj_ref[:, : 3 * HEAD], TN).astype(BF16)
    grad_m = mm(att_ref[...], back_ref[...]).astype(BF16)
    wide = 3 * HEAD
    half = grad_t.shape[0] // 2
    for s, g_ref in ((f_ref[0], g_keep_ref), (1 - f_ref[0], g_send_ref)):
        g_ref[:half, :] = grad_t[pl.ds(pl.multiple_of(s * half, half), half), :]
        for k in range(grad_m.shape[1] // wide):
            g_ref[half + HEAD * k : half + HEAD * (k + 1), :] = grad_m[:, wide * k : wide * (k + 1)]
    for b in range(blocks):
        slot = slot_ref[b]
        r = slice(TILE * b, TILE * (b + 1))

        @pl.when(slot < blocks // 2)
        def _(r=r, slot=slot):
            keep_ref[slot] = gj_ref[r, :]

        @pl.when(slot >= blocks // 2)
        def _(r=r, slot=slot):
            send_ref[slot - blocks // 2] = gj_ref[r, :]


def attend(slot, f, qk, vd, tables, first, back, h):
    rows = qk.shape[1]
    width = first.shape[1]
    packed = pl.BlockSpec((1, rows, 2 * HEAD), lambda *_: (h, 0, 0))
    g_rows = width // 2 + width // (3 * HEAD) * HEAD
    outs = [
        jax.ShapeDtypeStruct((rows // TILE // 2, TILE, 4 * HEAD), BF16),
        jax.ShapeDtypeStruct((rows // TILE // 2, TILE, 4 * HEAD), BF16),
        jax.ShapeDtypeStruct((g_rows, 3 * HEAD), BF16),
        jax.ShapeDtypeStruct((g_rows, 3 * HEAD), BF16),
    ]
    return pl.pallas_call(
        attend_kernel,
        grid_spec=pltpu.PrefetchScalarGridSpec(
            num_scalar_prefetch=2,
            grid=(1,),
            in_specs=[packed, packed]
            + [whole((rows, 2 * HEAD))] * 3
            + [whole(first.shape), whole(back.shape)],
            out_specs=[whole(v.shape) for v in outs],
            scratch_shapes=[
                pltpu.VMEM((2 * HEAD, rows), BF16),
                pltpu.VMEM((2 * HEAD, rows), BF16),
                pltpu.VMEM((rows, HEAD), BF16),
                pltpu.VMEM((rows, HEAD), BF16),
                pltpu.VMEM((rows, HEAD), BF16),
                pltpu.VMEM((2, rows, TILE), F32),
                pltpu.VMEM((HEAD, rows), F32),
                pltpu.VMEM((rows, HEAD), F32),
                pltpu.VMEM((rows, HEAD), F32),
                pltpu.VMEM((HEAD, rows), BF16),
                pltpu.VMEM((rows, 4 * HEAD), BF16),
                pltpu.VMEM((width, 3 * HEAD), BF16),
            ],
        ),
        out_shape=outs,
        compiler_params=params(),
        cost_estimate=beside(20 * rows * width),
        name="attend",
    )(slot, f, qk, vd, *tables, first, back)


def collect_kernel(f_ref, a_ref, b_ref, *refs, heads):
    (so0_ref, so1_ref, sums0_ref, vec_ref, own_ref, other_ref, wm_ref, wm_far_ref) = refs[:8]
    refs = refs[8:]
    packs, refs = refs[: 2 * len(heads)], refs[2 * len(heads) :]
    own_out, near_out, sums_ref, wt_ref = refs
    step = pl.program_id(0)
    first = heads[0] == 0
    wide = 3 * HEAD
    count = len(heads)
    all_heads = own_ref.shape[1] // wide // 2

    @pl.when(step == 0)
    def _():
        f, rows = f_ref[0], own_ref.shape[0]
        for k in range(2):
            for i, h in enumerate(heads):
                part = slice(wide * (all_heads * k + h), wide * (all_heads * k + h + 1))
                to = count * k + i
                wt_ref[to, pl.ds(pl.multiple_of(f * rows, rows), rows), :] = own_ref[:, part]
                wt_ref[to, pl.ds(pl.multiple_of((1 - f) * rows, rows), rows), :] = other_ref[:, part]
        sums_ref[...] = jnp.zeros_like(sums_ref) if first else sums0_ref[...]

    gain = vec_ref[0:1, :]
    n = normal(choose(step, (a_ref, b_ref), 0).astype(F32))
    merged = jnp.zeros(n.shape, F32)
    grad_first = jnp.zeros(n.shape, F32)
    for k, weights in enumerate((wm_ref, wm_far_ref)):
        for i, h in enumerate(heads):
            pack = packs[count * k + i]
            merged = merged + mm(pack[0, :, wide:], weights[HEAD * h : HEAD * (h + 1), :])
            gj = pack[0, :, :wide]
            row = 2 + all_heads * k + h
            sums_ref[row : row + 1, :wide] += colsum(gj.astype(F32))
            grad_first = grad_first + mm(gj, wt_ref[count * k + i], NT)
    u = grad_first * gain
    if not first:
        merged = merged + choose(step, (so0_ref, so1_ref), 0).astype(F32)
        u = u + choose(step, (so0_ref, so1_ref), 1).astype(F32)

    @pl.when(step < 2)
    def _():
        own_out[0], own_out[1] = merged.astype(BF16), u.astype(BF16)

    @pl.when(step >= 2)
    def _():
        near_out[0], near_out[1] = merged.astype(BF16), u.astype(BF16)

    sums_ref[0:1, :] += colsum(grad_first * n)
    sums_ref[1:2, :] += colsum(grad_first)


def collect(f, own_x, near_x, heads, packs, packs_far, vec, own, other, wm, wm_far, so_far=None):
    _, rows, width = own_x.shape
    pack = pl.BlockSpec((1, TILE, 4 * HEAD), lambda i, *_: (i, 0, 0))
    blocks = piece_specs(2, 2, width)
    so_far_specs = blocks
    if so_far is None:
        so_far = (jnp.zeros((8, 128), F32),) * 3
        so_far_specs = [whole((8, 128))] * 2
    return pl.pallas_call(
        functools.partial(collect_kernel, heads=heads),
        grid_spec=pltpu.PrefetchScalarGridSpec(
            num_scalar_prefetch=1,
            grid=(2 * rows // TILE,),
            in_specs=piece_specs(2, 1, width)
            + so_far_specs
            + [whole(v.shape) for v in (so_far[2], vec, own, other, wm, wm_far)]
            + [pack] * (2 * len(heads)),
            out_specs=blocks + [whole((8, width))],
            scratch_shapes=[pltpu.VMEM((2 * len(heads), width, 3 * HEAD), BF16)],
        ),
        out_shape=[
            jax.ShapeDtypeStruct((2, rows, width), BF16),
            jax.ShapeDtypeStruct((2, rows, width), BF16),
            jax.ShapeDtypeStruct((8, width), F32),
        ],
        compiler_params=params(),
        cost_estimate=beside(10 * rows * width),
        name="collect",
    )(f, own_x, near_x, *so_far, vec, own, other, wm, wm_far, *packs, *packs_far)


def slot_part(refs, slot, index):
    value = refs[0][index]
    for k in range(1, len(refs)):
        value = jnp.where(slot == k, refs[k][index], value)
    return value


def put_expand_kernel(c_ref, d_ref, *refs, shards):
    *ins, out = refs
    count, rows, columns = ins[0].shape
    cut = columns // shards
    k = (d_ref[0] - pl.program_id(0) + count) % count
    for b in range(CTX):
        slot = slot_of(c_ref[0] ^ b)
        value = slot_part(ins, slot, k).astype(F32)
        for g in range(shards):
            out[:, (g * CTX + b) * cut : (g * CTX + b + 1) * cut] = value[:, g * cut : (g + 1) * cut]


def put_expand(c, d, parts, shards):
    count, rows, columns = parts[0].shape
    return pl.pallas_call(
        functools.partial(put_expand_kernel, shards=shards),
        grid_spec=pltpu.PrefetchScalarGridSpec(
            num_scalar_prefetch=2,
            grid=(count // 2,),
            in_specs=[whole(parts[0].shape)] * CTX,
            out_specs=pl.BlockSpec((rows, CTX * columns), lambda a, *_: (a, 0)),
        ),
        out_shape=jax.ShapeDtypeStruct((count // 2 * rows, CTX * columns), F32),
        compiler_params=params(),
        cost_estimate=beside(50 * rows * columns),
        name="put_expand",
    )(c, d, *parts)


def put_reduce_kernel(c_ref, d_ref, *refs):
    *ins, out = refs
    count, rows, columns = ins[0].shape
    slot = slot_of(c_ref[0] ^ pl.program_id(0))
    for a in range(count // 2):
        k = (d_ref[0] - a - count // 2 + count) % count
        out[rows * a : rows * (a + 1), :] = slot_part(ins, slot, k).astype(F32)


def put_reduce(c, d, parts):
    count, rows, columns = parts[0].shape
    own = count // 2 * rows
    return pl.pallas_call(
        put_reduce_kernel,
        grid_spec=pltpu.PrefetchScalarGridSpec(
            num_scalar_prefetch=2,
            grid=(CTX,),
            in_specs=[whole(parts[0].shape)] * CTX,
            out_specs=pl.BlockSpec((own, columns), lambda b, *_: (b, 0)),
        ),
        out_shape=jax.ShapeDtypeStruct((CTX * own, columns), F32),
        compiler_params=params(),
        cost_estimate=beside(50 * rows * columns),
        name="put_reduce",
    )(c, d, *parts)


def put_heads_kernel(c_ref, d_ref, f_ref, *refs, top, with_merge):
    parts, outs, scratch = refs[:CTX], refs[CTX : CTX + 1 + with_merge], refs[-1]
    count, rows, columns = parts[0].shape
    heads = columns // (3 * HEAD)
    wide = 3 * HEAD
    for b in range(CTX):
        slot = slot_of(c_ref[0] ^ b)
        for a in range(count):
            k = (d_ref[0] - a + count) % count
            scratch[rows * a : rows * (a + 1), :] = slot_part(parts, slot, k)
        outs[0][:, columns * b : columns * (b + 1)] = scratch[:top, :].astype(F32)
        if with_merge:
            per = (count * rows - top) // HEAD

            @pl.when(b // (CTX // 2) == f_ref[0])
            def _(b=b):
                for h in range(heads):
                    row = heads * HEAD * (b % (CTX // 2)) + HEAD * h
                    for k in range(per):
                        src = slice(top + HEAD * k, top + HEAD * (k + 1))
                        part = scratch[src, wide * h : wide * (h + 1)]
                        outs[1][row : row + HEAD, wide * k : wide * (k + 1)] = part.astype(F32)


def put_heads(c, d, f, parts, top, width, with_merge):
    count, rows, columns = parts[0].shape
    shapes = [jax.ShapeDtypeStruct((top, CTX * columns), F32)]
    if with_merge:
        shapes.append(jax.ShapeDtypeStruct((width // 2, width), F32))
    return pl.pallas_call(
        functools.partial(put_heads_kernel, top=top, with_merge=with_merge),
        grid_spec=pltpu.PrefetchScalarGridSpec(
            num_scalar_prefetch=3,
            grid=(1,),
            in_specs=[whole(v.shape) for v in parts],
            out_specs=[whole(v.shape) for v in shapes],
            scratch_shapes=[pltpu.VMEM((count * rows, columns), BF16)],
        ),
        out_shape=shapes,
        compiler_params=params(),
        cost_estimate=short(),
        name="put_heads",
    )(c, d, f, *parts)


def rotary(rows):
    lane = jnp.arange(2 * HEAD, dtype=jnp.int32)[None, :] % HEAD
    half = ROT // 2
    inverse = 10000.0 ** (-2.0 * (lane % half).astype(F32) / ROT)
    angles = jnp.arange(rows, dtype=jnp.int32).astype(F32)[:, None] * inverse
    cos = jnp.where(lane < ROT, jnp.cos(angles), 1.0)
    sine = jnp.sin(angles)
    low = jnp.where(lane < half, -sine, 0.0)
    high = jnp.where((lane >= half) & (lane < ROT), sine, 0.0)
    return cos, low, high


def local(
    tokens, cotangent, block_order, first_gain, first_shift, second_gain, second_shift,
    triple_weight, triple_bias, merge_weight, merge_bias, expand_weight, expand_bias,
    reduce_weight, reduce_bias,
):
    c, d, f = lax.axis_index("ctx"), lax.axis_index("dp"), lax.axis_index("fsdp")
    shards = lax.axis_size("fsdp")
    own_len, width = tokens.shape[1:]
    inner = expand_weight.shape[1]
    own_inner = inner // shards // CTX
    ctx_inner = inner // CTX
    own_heads = HEADS // CTX
    own_cols = own_heads * 3 * HEAD
    own_merge = own_heads * HEAD
    half = CTX // 2

    own_expand = jnp.concatenate(
        [
            lax.dynamic_slice_in_dim(expand_weight, g * CTX * own_inner + c * own_inner, own_inner, 1)
            for g in range(shards)
        ],
        axis=1,
    )
    own_reduce = lax.dynamic_slice_in_dim(reduce_weight, c * own_inner, own_inner, 0)
    own_bias = lax.dynamic_slice_in_dim(expand_bias, c * own_inner, own_inner, 0)
    own_triple = jnp.concatenate(
        [lax.dynamic_slice_in_dim(triple_weight, k * own_cols, own_cols, 1) for k in (c, c ^ 2)], axis=1
    )
    smalls = jnp.stack(
        [first_gain, first_shift, second_gain, second_shift, own_bias, merge_bias, reduce_bias]
    )
    if shards == 2:
        own_tb = lax.dynamic_slice_in_dim(triple_bias, (c % half) * own_cols, own_cols, 0)
        rows = jnp.concatenate(
            [
                jnp.pad(smalls, ((0, 1), (0, width - smalls.shape[1]))),
                jnp.pad(own_tb[None], ((0, 7), (0, width - own_cols))),
            ]
        )
        w_own = jnp.concatenate([own_expand, own_reduce, rows])
        w_other = swap(w_own, "fsdp", 1)
        last = width // 2 + ctx_inner // 2
        own_s, other_s = w_own[last:], w_other[last:]
        cut = smalls.shape[1]
        vec = jnp.where(
            f == 0,
            jnp.concatenate([own_s[:8, :cut], other_s[:8, :cut]], axis=1),
            jnp.concatenate([other_s[:8, :cut], own_s[:8, :cut]], axis=1),
        ).astype(F32)
        tb = jnp.where(f == c // half, own_s[8, :own_cols], other_s[8, :own_cols]).astype(F32)
        t_own = own_triple
        m_own = lax.dynamic_slice_in_dim(merge_weight, (c % half) * own_merge, own_merge, 0)
        side = f
    else:
        def full(v):
            return lax.all_gather(v, "fsdp", axis=0, tiled=True)

        we, wr, wt = full(own_expand), full(own_reduce), full(own_triple)
        w_own = jnp.concatenate([we[: width // 2], wr[: ctx_inner // 2]])
        w_other = jnp.concatenate([we[width // 2 :], wr[ctx_inner // 2 :]])
        t_own, t_other = wt[: width // 2], wt[width // 2 :]
        vec = lax.all_gather(smalls, "fsdp", axis=1, tiled=True).astype(F32)
        vec = jnp.pad(vec, ((0, 1), (0, 0)))
        tb = lax.dynamic_slice_in_dim(full(triple_bias), c * own_cols, own_cols, 0).astype(F32)
        m_own = full(merge_weight)
        side = jnp.int32(0)
    tb = tb.reshape(own_heads, 1, 3 * HEAD)
    flag = side.astype(jnp.int32).reshape(1)

    own = jnp.stack([tokens.reshape(own_len, width), cotangent.reshape(own_len, width)])
    far = swap(own, "ctx", 2)
    near = swap(own, "ctx", 1)
    pos = jnp.concatenate(
        [lax.dynamic_slice_in_dim(block_order, 2 * (c ^ r), 2) for r in range(CTX)]
    )
    blocks = jnp.arange(pos.shape[0], dtype=jnp.int32)
    slot = jnp.sum(jnp.where(pos[None, :] == blocks[:, None], blocks[None, :], 0), axis=1)
    slot = slot.astype(jnp.int32)
    tables = rotary(CTX * own_len)
    far, t_own, m_own, w_other, *tables = lax.optimization_barrier(
        (far, t_own, m_own, w_other, *tables)
    )
    both = swap(far, "ctx", 1)
    if shards == 2:
        t_other, m_other = swap(t_own, "fsdp", 1), swap(m_own, "fsdp", 1)
    else:
        m_own, m_other = (
            lax.dynamic_slice_in_dim(m_own, k * own_merge, own_merge, 0) for k in (c, c ^ 2)
        )

    lu_keep, lu_send, *g_feed, sums2 = feed(
        flag, own, far, near, both, vec, w_own, w_other, width, ctx_inner
    )
    way_f = Summed(split_feed(g_feed, shards, width), f, d)
    lu_send, pos, t_other, m_other = boundary([way_f], lu_send, pos, t_other, m_other)
    if shards == 2:
        wm = jnp.where(f == c // half, m_own, m_other)
        wm_far = jnp.where(f == c // half, m_other, m_own)
    else:
        wm, wm_far = m_own, m_other
    lu_in = swap(lu_send, "ctx", 1)
    last = pos.shape[0] // 2
    qk, vd, first, back = project(
        pos[:last], flag, (own, near), vec, tb, t_own, t_other, wm, tables
    )
    lu_far = add_low(lu_keep[1], lu_in[1])
    qk, lu_far = lax.optimization_barrier((qk, lu_far))
    lu_far = swap(lu_far, "ctx", 2)
    qk, vd, first, back = project(
        pos[last:], flag, (far, both), vec, tb, t_own, t_other, wm, tables, (qk, vd, first, back)
    )
    (qk,) = boundary([way_f], qk)
    packs, packs_far, gs = [], [], []

    def next_head(qk, h):
        pack, sent, *g = attend(slot, flag, qk, vd, tables, first, back, h)
        packs.append(pack)
        gs.append(g)
        return sent

    sent = next_head(qk, 0)
    qk, sent, lu_far = boundary([way_f], qk, sent, lu_far)
    packs_far.append(swap(sent, "ctx", 2))
    sent = next_head(qk, 1)
    g_two = [jnp.concatenate(g, axis=1) for g in zip(*gs)]
    way_two = Summed(split_rows(g_two, shards, width), f, d)
    qk, sent_two, packs_far[0] = boundary([way_two, way_f], qk, sent, packs_far[0])
    sent_one = next_head(qk, 2)
    way_one = Summed(split_rows(gs[-1], shards, width), f, d)
    ways = [way_one, way_two]
    c1, d1, f1 = (v.astype(jnp.int32).reshape(1) for v in (c, d, f))
    c1, sent_two, sent_one = boundary([way_one, way_f], c1, sent_two, sent_one, hold=[way_two])
    packs_far.append(swap(sent_two, "ctx", 2))
    feed_parts = way_f.finish()
    c1, feed_parts = boundary([way_two], c1, feed_parts)
    grad_expand = put_expand(c1, d1, feed_parts, shards)
    grad_reduce = put_reduce(c1, d1, feed_parts)
    flag1, grad_expand, grad_reduce, sent_one, packs_far[1] = boundary(
        [way_one], flag, grad_expand, grad_reduce, sent_one, packs_far[1], hold=[way_two]
    )
    packs_far.append(swap(sent_one, "ctx", 2))
    so_far = collect(
        flag1, own, near, (0, 1), packs[:2], packs_far[:2], vec, t_own, t_other, wm, wm_far
    )
    flag1, packs_far[2], so_far = boundary([], flag, packs_far[2], so_far, hold=[way_one])
    way_t = way_two.beside(way_one)
    ways = [way_t]
    flag1, so_far = boundary(ways, flag1, so_far)
    mu, mu_near, sums1 = collect(
        flag1, own, near, (2,), packs[2:], packs_far[2:], vec, t_own, t_other, wm, wm_far, so_far
    )

    tb_rows = sums1[2 : 2 + 2 * own_heads, : 3 * HEAD].reshape(2, own_cols)
    tb_rows = jnp.pad(tb_rows, ((0, 0), (0, width - own_cols)))
    eb_row = jnp.pad(sums2[2:3], ((0, 0), (0, width - ctx_inner)))
    mine = (jnp.arange(CTX) == c)[:, None]
    across = (jnp.arange(CTX) == (c ^ 2))[:, None]
    tb_block = jnp.where(mine, tb_rows[:1], jnp.where(across, tb_rows[1:], 0.0))
    vector = jnp.concatenate(
        [sums1[:2], sums2[:2], sums2[3:4], tb_block, jnp.where(mine, eb_row, 0.0)]
    )
    vector = jnp.pad(vector, ((0, 3), (0, 0)))

    c1, mu_near, vector = boundary(ways, c1, mu_near, vector)
    mu_in = swap(mu_near, "ctx", 1)
    if shards == 2:
        vector = vector + swap(vector, "fsdp", 1)
    else:
        vector = lax.psum(vector, "fsdp")
    mu_in, vector = lax.optimization_barrier((mu_in, vector))
    vector = vector + swap(vector, "dp", 1)
    lu = lu_keep[0].astype(F32) + lu_in[0].astype(F32) + lu_far.astype(F32)
    mixed, u = lu + mu.astype(F32) + mu_in.astype(F32)

    x_f = own[0].astype(F32)
    mixed = (x_f + mixed + (vec[5] + vec[6])[None, :]).astype(BF16)
    average = jnp.mean(x_f, axis=-1, keepdims=True)
    centred = x_f - average
    r = lax.rsqrt(jnp.mean(centred * centred, axis=-1, keepdims=True) + epsilon)
    n = centred * r
    input_grad = own[1].astype(F32) + r * (
        u - jnp.mean(u, axis=-1, keepdims=True) - n * jnp.mean(u * n, axis=-1, keepdims=True)
    )

    vector, mixed, input_grad = lax.optimization_barrier((vector, mixed, input_grad))
    vector = vector + swap(vector, "dp", 2)
    vector = vector + swap(vector, "ctx", 1)
    (vector,) = boundary(ways, vector)
    vector = vector + swap(vector, "ctx", 2)
    part = width // shards
    five = lax.dynamic_slice_in_dim(vector[:5], f * part, part, 1)
    d_g1, d_s1, d_g2, d_s2, d_cot = [five[i] for i in range(5)]
    d_tb = vector[5 : 5 + CTX, :own_cols].reshape(-1)
    d_tb = lax.dynamic_slice_in_dim(d_tb, f * (3 * part), 3 * part, 0)
    d_eb = lax.dynamic_slice_in_dim(vector[5 + CTX : 5 + 2 * CTX], f * own_inner, own_inner, 1)
    d_eb = d_eb.reshape(-1)

    parts = way_t.finish()
    parts, vector = lax.optimization_barrier((parts, vector))
    placed = put_heads(c1, d1, f1, parts, part, width, shards == 2)
    grad_triple = placed[0]
    if shards == 2:
        grad_merge = placed[1]
    else:
        count = lax.axis_size("dp")
        g_all = [
            jnp.concatenate([pick(g, (d - a) % count) for a in range(count)])
            for g in in_order(parts, c)
        ]
        wide = 3 * HEAD
        grad_merge = jnp.concatenate(
            [
                g[part:].reshape(width // wide, HEAD, own_heads, wide).transpose(2, 1, 0, 3)
                .reshape(own_merge, width) for g in g_all
            ]
        )
        grad_merge = lax.dynamic_slice_in_dim(grad_merge, f * part, part, 0).astype(F32)
    return (
        mixed[None],
        input_grad[None],
        d_g1,
        d_s1,
        d_g2,
        d_s2,
        grad_triple,
        d_tb,
        grad_merge,
        d_cot,
        grad_expand,
        d_eb,
        grad_reduce,
        d_cot,
    )


def split_feed(g, shards, width):
    if shards == 2:
        return tuple(g)
    g = jnp.stack(g)
    half = width // 2
    ge, gr = g[:, :half].reshape(width, -1), g[:, half:].reshape(-1, width)
    parts = [v.reshape(shards, v.shape[0] // shards, v.shape[1]) for v in (ge, gr)]
    return jnp.concatenate(parts, axis=1)


def split_rows(g, shards, width):
    if shards == 2:
        return tuple(g)
    g = jnp.stack(g)
    rows = g[:, : width // 2].reshape(shards, width // shards, g.shape[2])
    tail = jnp.broadcast_to(g[:1, width // 2 :], (shards,) + g[0, width // 2 :].shape)
    return jnp.concatenate([rows, tail], axis=1)


def solution(mesh):
    tokens = P(("dp", "fsdp"), "ctx", None)
    row, vector = P("fsdp", None), P("fsdp")
    weights = (row, vector, row, vector, row, vector, row, vector)
    in_specs = (tokens, tokens, P()) + (vector,) * 4 + weights
    out_specs = (tokens, tokens) + (vector,) * 4 + weights
    return jax.shard_map(local, mesh=mesh, in_specs=in_specs, out_specs=out_specs, check_vma=False)
```
